32 devices in a mesh: dp: 8 (over z, y), rep: 4 (over x, core).
Axes of the slice: x: 2, y: 2, z: 4, core: 2. Of those that a mesh axis runs over, the one named last changes fastest.
Arguments:
- tokens: bfloat16 [8, 704, 1024], P('dp', 'rep'), may hold values from -6 to 6
- offsets: int32 [8, 8], P('dp'), may hold values from 0 to 703, as said below
- w_proj: bfloat16 [1024, 3072], replicated, may hold values from -0.1875 to 0.1875
- forget_weight: float32 [1024], replicated, may hold values from -1 to 1
- reset_weight: float32 [1024], replicated, may hold values from -1 to 1
- forget_bias: float32 [1024], replicated, may hold values from 0 to 10
- reset_bias: float32 [1024], replicated, may hold values from -1 to 1
- layer_norm_gain: float32 [1024], replicated, may hold values from 0.5 to 1.5
- layer_norm_bias: float32 [1024], replicated, may hold values from -6 to 6
- cotangent: bfloat16 [8, 704, 1024], P('dp', 'rep'), may hold values from -6 to 6
Outputs:
- output: bfloat16 [8, 704, 1024], P('dp', 'rep')
- input_grad: bfloat16 [8, 704, 1024], P('dp', 'rep')
- proj_grad: float32 [1024, 3072], replicated
- forget_weight_grad: float32 [1024], replicated
- reset_weight_grad: float32 [1024], replicated
- forget_bias_grad: float32 [1024], replicated
- reset_bias_grad: float32 [1024], replicated
- gain_grad: float32 [1024], replicated
- bias_grad: float32 [1024], replicated
The draws below stay inside these ranges and needn't reach their ends.
Inputs may be any that keep to these rules, and one draw needn't show every extreme that they name: offsets[r] lists start positions of row r's documents in ascending order; the first is 0; a position may repeat.
All inputs are finite; a program needn't handle non-finite values.
Results may differ from the reference program's by a relative error of at most 0.0059.
Values sent between devices are 32-bit elements; how exact they have to be, the bound alone decides.
No kernel may reach another device: no remote copies, remote signals or barrier semaphores. Data moves between devices by JAX's collectives and lax.ppermute only.
A program may use at most 128 MiB of HBM per device.

```python
import math
import jax
import jax.numpy as jnp
from jax import lax

D = 1024
TOK_DEV = 176
DOCS = 8
ROW_LEN = 704
ROWS = 8


def draw_offsets(key, part):
    key = jax.random.fold_in(key, 7)
    key_first, key_last, key_spare = jax.random.split(key, 3)
    first = jax.random.randint(key_first, (ROWS, 1), 1, TOK_DEV)
    last = ROW_LEN - jax.random.randint(key_last, (ROWS, 1), 1, TOK_DEV)
    spare = jax.random.randint(key_spare, (ROWS, DOCS - 3), 0, first + ROW_LEN - last)
    others = jnp.where(spare < first, spare, spare - first + last)
    starts = jnp.concatenate([jnp.zeros((ROWS, 1), jnp.int32), first, last, others], axis=1)
    return jnp.sort(starts, axis=1).astype(jnp.int32)


def draw_forget_bias(key, part):
    key = jax.random.fold_in(key, 11)
    key_rate, key_pick, key_fast = jax.random.split(key, 3)
    middle_rate = math.log(TOK_DEV) + 0.6
    slower_bias = middle_rate + jax.random.uniform(key_rate, (D,), jnp.float32, -1.0, 2.0)
    faster_share = 0.25
    faster_bias = jax.random.uniform(key_fast, (D,), jnp.float32, 0.0, 2.0)
    picked = jax.random.uniform(key_pick, (D,), jnp.float32) < faster_share
    return jnp.where(picked, faster_bias, slower_bias).astype(jnp.float32)


def draw_forget_weight(key, part):
    key = jax.random.fold_in(key, 13)
    key_sign, key_size = jax.random.split(key)
    signs = jnp.where(jax.random.uniform(key_sign, (D,), jnp.float32) < 0.5, -1.0, 1.0)
    magnitude = jax.random.uniform(key_size, (D,), jnp.float32, 0.5, 1.0)
    return (signs * magnitude).astype(jnp.float32)


def block_scale(stream_key, extent, pieces, smallest, high):
    def one(axis_at, shards_of):
        heights = jax.random.uniform(jax.random.fold_in(jax.random.fold_in(stream_key, 6), axis_at), (shards_of,), jnp.float32, smallest / len(pieces), high / len(pieces))
        return jnp.repeat(jnp.exp(heights), extent[axis_at] // shards_of).reshape((-1,) + (1,) * (len(extent) - axis_at - 1))

    loudness = one(*pieces[0])
    for cut in pieces[1:]:
        loudness = loudness * one(*cut)
    return loudness


def centred(own_key, shape, deviation, bound, cuts=(), kind=jnp.bfloat16):
    loudness = block_scale(own_key, shape, cuts, -0.22, 0.18) if cuts else 1.0
    array = jax.random.normal(own_key, shape, jnp.float32) * deviation * loudness
    return jnp.minimum(jnp.maximum(array, -bound), bound).astype(kind)


def setup_inputs(seed: int = 0) -> dict:
    streams_of = jax.random.split(jax.random.key(seed), 11)
    return {
        "tokens": centred(streams_of[0], (ROWS, ROW_LEN, D), 1.0, 6.0, ((0, 8), (1, 4))),
        "offsets": draw_offsets(jax.random.fold_in(streams_of[10], 71), 0),
        "w_proj": centred(streams_of[2], (D, 3 * D), D ** -0.5, 0.1875),
        "forget_weight": draw_forget_weight(jax.random.fold_in(streams_of[10], 71), 0),
        "reset_weight": jnp.clip(jax.random.uniform(streams_of[4], (D,), jnp.float32, -1.0, 1.0), -1.0, 1.0),
        "forget_bias": draw_forget_bias(jax.random.fold_in(streams_of[10], 71), 0),
        "reset_bias": jnp.clip(jax.random.uniform(streams_of[6], (D,), jnp.float32, -1.0, 1.0), -1.0, 1.0),
        "layer_norm_gain": jnp.clip(1.0 + 0.1 * jax.random.normal(streams_of[7], (D,), jnp.float32), 0.5, 1.5),
        "layer_norm_bias": centred(streams_of[8], (D,), 1.5, 6.0, (), jnp.float32),
        "cotangent": centred(streams_of[9], (ROWS, ROW_LEN, D), 1.0, 6.0, ((0, 8), (1, 4))),
    }


EPS = 1e-05

@jax.custom_vjp
def low(v):
    return lax.optimization_barrier(v.astype(jnp.bfloat16)).astype(jnp.float32)

@jax.custom_vjp
def low_back(v):
    return v

def low_keep(v):
    return (low(v), None)

def low_pass(kept, grad):
    return (grad,)

def back_keep(v):
    return (v, None)

def back_low(kept, grad):
    return (low(grad),)
low.defvjp(low_keep, low_pass)
low_back.defvjp(back_keep, back_low)

def layer(inputs, weight, forget_weight, reset_weight, forget_bias, reset_bias, layer_norm_gain, layer_norm_bias, keep):
    mean_removed = inputs - lax.optimization_barrier(jnp.mean(inputs, axis=-1, keepdims=True))
    variance = lax.optimization_barrier(jnp.mean(mean_removed * mean_removed, axis=-1, keepdims=True))
    normed = mean_removed * lax.rsqrt(variance + EPS) * layer_norm_gain + layer_norm_bias
    normalized_reduced = low(normed)
    proj = low_back(jnp.einsum('td,de->te', normalized_reduced, weight, precision=lax.Precision.HIGHEST))
    cand = proj[:, :D]
    forget_in = proj[:, D:2 * D]
    reset_in = proj[:, 2 * D:]

    def step(state, inp):
        cand_t, fin_t, rin_t, input_t, keep_t = inp
        prev = state * keep_t
        forget = jax.nn.sigmoid(fin_t + forget_weight * prev + forget_bias)
        reset = jax.nn.sigmoid(rin_t + reset_weight * prev + reset_bias)
        state_new = forget * prev + (1.0 - forget) * cand_t
        return (state_new, reset * state_new + (1.0 - reset) * input_t)
    start = jnp.zeros((D,), jnp.float32)
    final_state, outs = lax.scan(jax.checkpoint(step), start, (cand, forget_in, reset_in, inputs, keep))
    return outs

def reference(tokens, offsets, w_proj, forget_weight, reset_weight, forget_bias, reset_bias, layer_norm_gain, layer_norm_bias, cotangent):
    params = (w_proj.astype(jnp.float32), forget_weight, reset_weight, forget_bias, reset_bias, layer_norm_gain, layer_norm_bias)
    positions = jnp.arange(ROW_LEN).astype(jnp.int32)

    def one_row(totals, row):
        row_tokens, row_offsets, row_cot = row
        hits = jnp.any(positions[:, None] == row_offsets[None, :].astype(jnp.int32), axis=1)
        keep = jnp.where(hits, 0.0, 1.0).astype(jnp.float32)

        def forward(inputs, *weights):
            return layer(inputs, *weights, keep)
        outs, pull = jax.vjp(forward, row_tokens.astype(jnp.float32), *params)
        grads = pull(row_cot.astype(jnp.float32))
        totals = tuple((total + grad for total, grad in zip(totals, grads[1:])))
        return (totals, (outs.astype(jnp.bfloat16), grads[0].astype(jnp.bfloat16)))
    zeros = tuple((jnp.zeros_like(param) for param in params))
    totals, (outputs, input_grads) = lax.scan(one_row, zeros, (tokens, offsets, cotangent))
    return (outputs, input_grads, totals[0], totals[1], totals[2], totals[3], totals[4], totals[5], totals[6])
```

```python
import functools

import jax
import jax.numpy as jnp
from jax import lax
from jax.experimental import pallas as pl
from jax.experimental.pallas import tpu as pltpu
from jax.sharding import Mesh
from jax.sharding import PartitionSpec as P

EPS = 1e-05
SWAP = [(0, 1), (1, 0)]
VMEM_BYTES = 56 * 2**20
F32 = jnp.float32
BF16 = jnp.bfloat16


def swap(block, axis):
    return lax.ppermute(block, axis, SWAP)


def xor_permute(block, axis, distance):
    size = lax.axis_size(axis)
    return lax.ppermute(block, axis, [(i, i ^ distance) for i in range(size)])


def whole(ref_shape):
    return pl.BlockSpec(ref_shape, lambda i, s: (0,) * len(ref_shape))


def any_spec():
    return pl.BlockSpec(memory_space=pl.ANY)


def vmem():
    return pl.BlockSpec(memory_space=pltpu.VMEM)


def smem():
    return pl.BlockSpec(memory_space=pltpu.SMEM)


def shaped(shape, dtype=F32):
    return jax.ShapeDtypeStruct(shape, dtype)


def params(mib):
    return pltpu.CompilerParams(vmem_limit_bytes=mib * 2**20)


def widen_kernel(tokens_ref, tokens_out):
    tokens_out[...] = tokens_ref[...].astype(F32)


def widen(tokens):
    return pl.pallas_call(
        widen_kernel,
        out_shape=shaped(tokens.shape),
        in_specs=[vmem()],
        out_specs=vmem(),
        name="widen",
    )(tokens)


def widen_cot_kernel(sel, cot_ref, cot_out):
    cols = cot_ref.shape[1] // 4
    for k in range(2):
        at = pl.multiple_of((2 * k + sel[0]) * cols, cols)
        cot_out[:, k * cols : (k + 1) * cols] = cot_ref[:, pl.ds(at, cols)].astype(F32)


def widen_cot(sel, cot):
    return pl.pallas_call(
        widen_cot_kernel,
        out_shape=shaped((cot.shape[0], cot.shape[1] // 2)),
        in_specs=[smem(), vmem()],
        out_specs=vmem(),
        name="widen_cot",
    )(sel, cot)


def pack_cot_kernel(sel, cot_ref, sibling_ref, cot_out):
    block, cols = cot_ref.shape[0], cot_ref.shape[1] // 4
    mine = pl.multiple_of(sel[0] * cols, cols)
    cot_out[0:block, :] = cot_ref[:, pl.ds(mine, cols)].astype(F32)
    sibling = pl.multiple_of(sel[1] * cols, cols)
    cot_out[block:, :] = sibling_ref[:, pl.ds(sibling, cols)]


def pack_cot(sel, cot, sibling):
    return pl.pallas_call(
        pack_cot_kernel,
        out_shape=shaped((2 * cot.shape[0], cot.shape[1] // 4)),
        in_specs=[smem(), vmem(), vmem()],
        out_specs=vmem(),
        name="pack_cot",
    )(sel, cot, sibling)


def standardized(x):
    mean = jnp.mean(x, axis=-1, keepdims=True)
    centred = x - mean
    rdev = lax.rsqrt(jnp.mean(centred * centred, axis=-1, keepdims=True) + EPS)
    return centred * rdev, rdev


def norm_and_project(toks, norm_ref, weights, gates_ref, normed, cand, zf, zr, base):
    gain, bias = norm_ref[0:1, :], norm_ref[1:2, :]
    fb, rb = gates_ref[2:3, :], gates_ref[3:4, :]
    block = toks[0].shape[0]
    step = 16
    for at, tok in enumerate(toks):

        def body(i, carry, tok=tok, at=at):
            here = pl.ds(pl.multiple_of(i * step, step), step)
            there = pl.ds(pl.multiple_of(at * block + i * step, step), step)
            xhat, _ = standardized(tok[here, :])
            normed[there, :] = (xhat * gain + bias).astype(BF16)
            return carry

        lax.fori_loop(0, block // step, body, 0, unroll=True)
    rows = normed[...]
    here = slice(base, base + 2 * block)
    cand[here, :] = jnp.dot(rows, weights[0][...], preferred_element_type=F32)
    zf[here, :] = 0.5 * (jnp.dot(rows, weights[1][...], preferred_element_type=F32) + fb)
    zr[here, :] = 0.5 * (jnp.dot(rows, weights[2][...], preferred_element_type=F32) + rb)


def near_kernel(sel, tok0, tok1, w0, w1, w2, gates_ref, norm_ref, normed, cand, zf, zr):
    norm_and_project((tok0, tok1), norm_ref, (w0, w1, w2), gates_ref, normed, cand, zf, zr, 0)


def weight_specs(width, cols):
    return [
        pl.BlockSpec((width, cols), lambda i, s, k=k: (0, s[0] + k * (width // cols)))
        for k in range(3)
    ]


def run_near(sel, toks, w_proj, gates, norm):
    block, width = toks[0].shape
    cols = width // 4
    return pl.pallas_call(
        near_kernel,
        out_shape=(shaped((2 * block, width), BF16),) + (shaped((2 * block, cols)),) * 3,
        grid_spec=pltpu.PrefetchScalarGridSpec(
            num_scalar_prefetch=1,
            grid=(1,),
            in_specs=[whole((block, width))] * 2
            + weight_specs(width, cols)
            + [pl.BlockSpec((8, cols), lambda i, s: (0, s[0])), whole((8, width))],
            out_specs=(whole((2 * block, width)),) + (whole((2 * block, cols)),) * 3,
        ),
        compiler_params=params(24),
        name="near_blocks",
    )(sel, *toks, w_proj, w_proj, w_proj, gates, norm)


def forward_kernel(
    sel,
    tok0,
    tok1,
    cand_near,
    zf_near,
    zr_near,
    keep_ref,
    w0,
    w1,
    w2,
    gates_ref,
    norm_ref,
    normed,
    cand,
    zf,
    zr,
    state,
    half_prev,
    fwk,
    kh,
):
    length, cols = cand.shape
    block = length // 4
    near = slice(0, 2 * block)
    cand[near, :], zf[near, :], zr[near, :] = cand_near[...], zf_near[...], zr_near[...]
    half_fw = 0.5 * gates_ref[0:1, :]
    step = 16

    def keep_body(i, carry):
        here = pl.ds(pl.multiple_of(i * step, step), step)
        keep = jnp.broadcast_to(keep_ref[here, :], (step, cols))
        kh[here, :] = 0.5 * keep
        fwk[here, :] = keep * half_fw
        return carry

    lax.fori_loop(0, length // step, keep_body, 0, unroll=4)
    norm_and_project(
        (tok0, tok1), norm_ref, (w0, w1, w2), gates_ref, normed, cand, zf, zr, 2 * block
    )
    c = jnp.zeros((1, cols), F32)
    for k in range(4):
        base = sel[1 + k] * block

        def body(i, c, base=base):
            row = pl.ds(base + i, 1)
            th = jnp.tanh(zf[row, :] + fwk[row, :] * c)
            hp = kh[row, :] * c
            hc = 0.5 * cand[row, :]
            c = (hp + hc) + (hp - hc) * th
            state[row, :] = c
            half_prev[row, :] = hp
            return c

        c = lax.fori_loop(0, block, body, c, unroll=16)


def run_forward(sel, toks, near, keep, w_proj, gates, norm):
    block, width = toks[0].shape
    cols = width // 4
    length = 4 * block
    return pl.pallas_call(
        forward_kernel,
        out_shape=(shaped((2 * block, width), BF16),) + (shaped((length, cols)),) * 5,
        grid_spec=pltpu.PrefetchScalarGridSpec(
            num_scalar_prefetch=1,
            grid=(1,),
            in_specs=[whole((block, width))] * 2
            + [whole((2 * block, cols))] * 3
            + [whole((length, 1))]
            + weight_specs(width, cols)
            + [pl.BlockSpec((8, cols), lambda i, s: (0, s[0])), whole((8, width))],
            out_specs=(whole((2 * block, width)),) + (whole((length, cols)),) * 5,
            scratch_shapes=[pltpu.VMEM((length, cols), F32)] * 2,
        ),
        compiler_params=params(30),
        name="forward_scan",
    )(sel, *toks, *near, keep, w_proj, w_proj, w_proj, gates, norm)


def backward_kernel(
    sel,
    x0,
    x1,
    x2,
    x3,
    g0,
    g1,
    g23,
    cand_ref,
    zf_ref,
    zr_ref,
    state,
    half_prev,
    keep_ref,
    gates_ref,
    near_ref,
    far_ref,
    dproj_ref,
    out_ref,
    dxh_ref,
    small_ref,
    *rest,
    pieces,
):
    outs = rest[:pieces]
    coef, add_b, add_e, gz, omf = rest[pieces:]
    length, cols = cand_ref.shape
    block = length // 4
    width = near_ref.shape[1]
    part = outs[0].shape[0]
    fw, rw = gates_ref[0:1, :], gates_ref[1:2, :]
    half_fw, half_rw = 0.5 * fw, 0.5 * rw
    step = 16
    zero = jnp.zeros((step, cols), F32)
    sums = (zero, zero)
    sources = ((x0, g0, 0), (x1, g1, 0), (x2, g23, 0), (x3, g23, block))
    for b, (x_ref, g_ref, g_at) in enumerate(sources):

        def gate_body(i, carry, b=b, x_ref=x_ref, g_ref=g_ref, g_at=g_at):
            at = pl.multiple_of(i * step, step)
            here = pl.ds(pl.multiple_of(b * block + at, step), step)
            x = x_ref[pl.ds(at, step), :]
            g = g_ref[pl.ds(pl.multiple_of(g_at + at, step), step), :].astype(F32)
            keep = keep_ref[here, :]
            prev = 2.0 * half_prev[here, :]
            c, cd = state[here, :], cand_ref[here, :]
            forget = 0.5 + 0.5 * jnp.tanh(zf_ref[here, :] + half_fw * prev)
            reset = 0.5 + 0.5 * jnp.tanh(zr_ref[here, :] + half_rw * prev)
            not_forget, not_reset = 1.0 - forget, 1.0 - reset
            out_ref[here, :] = reset * c + not_reset * x
            dxh_ref[here, :] = g * not_reset
            dzr = g * (c - x) * reset * not_reset
            slope = (prev - cd) * forget * not_forget
            coef[here, :] = keep * (forget + slope * fw)
            add_b[here, :] = keep * (dzr * rw)
            add_e[here, :] = g * reset
            gz[here, :] = slope
            omf[here, :] = not_forget
            dproj_ref[here, 2 * cols : 3 * cols] = dzr.astype(BF16)
            return (carry[0] + dzr * prev, carry[1] + dzr)

        sums = lax.fori_loop(0, block // step, gate_body, sums, unroll=True)
    rw_sum, rb_sum = sums

    s = jnp.zeros((1, cols), F32)
    for k in range(3, -1, -1):
        last = sel[1 + k] * block + block - 1

        def backward_body(i, s, last=last):
            row = pl.ds(last - i, 1)
            total = s + add_e[row, :]
            add_e[row, :] = total
            return coef[row, :] * total + add_b[row, :]

        s = lax.fori_loop(0, block, backward_body, s, unroll=16)

    def grad_body(i, carry):
        here = pl.ds(pl.multiple_of(i * step, step), step)
        total = add_e[here, :]
        prev = 2.0 * half_prev[here, :]
        dzf = total * gz[here, :]
        dproj_ref[here, 0:cols] = (total * omf[here, :]).astype(BF16)
        dproj_ref[here, cols : 2 * cols] = dzf.astype(BF16)
        return (carry[0] + dzf * prev, carry[1] + dzf)

    fw_sum, fb_sum = lax.fori_loop(0, length // step, grad_body, (zero, zero), unroll=4)
    small_ref[...] = jnp.concatenate(
        [jnp.sum(v, axis=0, keepdims=True) for v in (fw_sum, rw_sum, fb_sum, rb_sum)]
        + [jnp.zeros((4, cols), F32)],
        axis=0,
    )
    outer_products(sel, 5, near_ref, far_ref, dproj_ref, outs)


def outer_products(sel, first, near_ref, far_ref, dproj_ref, outs):
    part = outs[0].shape[0]
    half = near_ref.shape[0]
    for i, out in enumerate(outs):
        at = pl.ds(pl.multiple_of(sel[first + i] * part, part), part)
        dims = (((0,), (0,)), ((), ()))
        out[...] = lax.dot_general(
            near_ref[:, at], dproj_ref[0:half, :], dims, preferred_element_type=F32
        ) + lax.dot_general(
            far_ref[:, at], dproj_ref[half:, :], dims, preferred_element_type=F32
        )


def run_backward(sel, toks, cots, scanned, keep, gates, normed, pieces):
    cot_own, cot_sibling, cot_far = cots
    block, width = toks[0].shape
    cols = width // 4
    length = 4 * block
    strip = pl.BlockSpec((block, cols), lambda i, s: (0, s[0]))
    return pl.pallas_call(
        functools.partial(backward_kernel, pieces=pieces),
        out_shape=(
            shaped((length, 3 * cols), BF16),
            shaped((length, cols)),
            shaped((length, cols)),
            shaped((8, cols)),
        )
        + (shaped((width // 8, 3 * cols)),) * pieces,
        grid_spec=pltpu.PrefetchScalarGridSpec(
            num_scalar_prefetch=1,
            grid=(1,),
            in_specs=[strip] * 4
            + [strip, pl.BlockSpec((block, cols), lambda i, s: (0, s[5 + pieces]))]
            + [whole((2 * block, cols))]
            + [whole((length, cols))] * 5
            + [whole((length, 1)), pl.BlockSpec((8, cols), lambda i, s: (0, s[0]))]
            + [whole((2 * block, width))] * 2,
            out_specs=(
                whole((length, 3 * cols)),
                whole((length, cols)),
                whole((length, cols)),
                whole((8, cols)),
            )
            + (whole((width // 8, 3 * cols)),) * pieces,
            scratch_shapes=[pltpu.VMEM((length, cols), F32)] * 5,
        ),
        compiler_params=params(30),
        name="backward_scan",
    )(sel, *toks, cot_own, cot_sibling, cot_far, *scanned, keep, gates, *normed)


def products_kernel(sel, near_ref, far_ref, dproj_ref, *outs):
    outer_products(sel, 0, near_ref, far_ref, dproj_ref, outs)


def run_products(sel, normed, dproj, pieces):
    width = normed[0].shape[1]
    return pl.pallas_call(
        products_kernel,
        out_shape=(shaped((width // 8, dproj.shape[1])),) * pieces,
        in_specs=[smem()] + [vmem()] * 3,
        out_specs=(vmem(),) * pieces,
        compiler_params=params(24),
        name="own_products",
    )(sel, *normed, dproj)


def input_kernel(
    sel,
    tok0,
    tok1,
    tok2,
    tok3,
    dproj_ref,
    dxh_ref,
    out_ref,
    gate_small_ref,
    w0,
    w1,
    w2,
    norm_ref,
    mine_ref,
    send_ref,
    dnormed,
):
    cols = dxh_ref.shape[1]
    block, width = tok0.shape
    gain, bias = norm_ref[0:1, :], norm_ref[1:2, :]
    mine = pl.multiple_of(sel[0] * cols, cols)
    step = 8
    sums = (jnp.zeros((step, width), F32), jnp.zeros((step, width), F32))
    for b, tok in enumerate((tok0, tok1, tok2, tok3)):
        rows = slice(b * block, (b + 1) * block)
        total = None
        for k, w in enumerate((w0, w1, w2)):
            term = lax.dot_general(
                dproj_ref[rows, k * cols : (k + 1) * cols],
                w[...],
                (((1,), (1,)), ((), ())),
                preferred_element_type=F32,
            )
            total = term if total is None else total + term
        dnormed[...] = total
        where = send_ref if b % 2 else mine_ref
        base = (b // 2) * block

        def body(i, carry, tok=tok, base=base, where=where):
            here = pl.ds(pl.multiple_of(i * step, step), step)
            there = pl.ds(pl.multiple_of(base + i * step, step), step)
            xhat, rdev = standardized(tok[here, :])
            dn = dnormed[here, :]
            dxhat = dn * gain
            mean1 = jnp.mean(dxhat, axis=-1, keepdims=True)
            mean2 = jnp.mean(dxhat * xhat, axis=-1, keepdims=True)
            where[there, 0:width] = rdev * (dxhat - mean1 - xhat * mean2)
            return (carry[0] + dn * xhat, carry[1] + dn)

        sums = lax.fori_loop(0, block // step, body, sums, unroll=11)
        to = pl.ds(base, block)
        where[to, pl.ds(mine, cols)] += dxh_ref[rows, :]
        where[to, width : width + cols] = out_ref[rows, :]
    tail = slice(2 * block, 2 * block + 8)
    for ref in (mine_ref, send_ref):
        ref[tail, :] = jnp.zeros((8, width + cols), F32)
    where = mine_ref
    where[2 * block : 2 * block + 4, pl.ds(mine, cols)] = gate_small_ref[0:4, :]
    for i, v in enumerate(sums):
        where[2 * block + 4 + i : 2 * block + 5 + i, 0:width] = jnp.sum(v, axis=0, keepdims=True)
    send_ref[tail, :] = mine_ref[tail, :]


def run_input(sel, toks, dproj, dxh, out, gate_small, w_proj, norm):
    block, width = toks[0].shape
    length, cols = dxh.shape
    shape = (2 * block + 8, width + cols)
    return pl.pallas_call(
        input_kernel,
        out_shape=(shaped(shape), shaped(shape)),
        grid_spec=pltpu.PrefetchScalarGridSpec(
            num_scalar_prefetch=1,
            grid=(1,),
            in_specs=[whole((block, width))] * 4
            + [whole((length, 3 * cols)), whole((length, cols)), whole((length, cols))]
            + [whole((8, cols))]
            + weight_specs(width, cols)
            + [whole((8, width))],
            out_specs=(whole(shape), whole(shape)),
            scratch_shapes=[pltpu.VMEM((block, width), F32)],
        ),
        compiler_params=params(30),
        name="input_side",
    )(sel, *toks, dproj, dxh, out, gate_small, w_proj, w_proj, w_proj, norm)


def combine_kernel(sel, mine_ref, got_ref, keep_ref, send_ref):
    rows = mine_ref.shape[0]
    block = (rows - 8) // 2
    width = mine_ref.shape[1] * 4 // 5
    cols = width // 4
    low = pl.multiple_of(width + sel[0] * cols, cols)
    high = pl.multiple_of(width + (1 - sel[0]) * cols, cols)
    for ref, first, count in ((keep_ref, 0, block), (send_ref, block, block + 8)):
        here = slice(first, first + count)
        ref[:, 0:width] = mine_ref[here, 0:width] + got_ref[here, 0:width]
        ref[:, pl.ds(low, cols)] = mine_ref[here, width:]
        ref[:, pl.ds(high, cols)] = got_ref[here, width:]


def combine(sel, mine, got):
    rows, both = mine.shape
    block, width = (rows - 8) // 2, both * 4 // 5
    return pl.pallas_call(
        combine_kernel,
        out_shape=(shaped((block, width * 3 // 2)), shaped((block + 8, width * 3 // 2))),
        in_specs=[smem(), vmem(), vmem()],
        out_specs=(vmem(), vmem()),
        compiler_params=params(16),
        name="combine",
    )(sel, mine, got)


def join_kernel(sel, mine_ref, sent_ref, got_ref, out_ref, grad_ref, small_ref):
    block, width = out_ref.shape
    half = width // 2
    at = pl.multiple_of(sel[0] * half, half)
    other = pl.multiple_of((1 - sel[0]) * half, half)
    out_ref[:, pl.ds(at, half)] = mine_ref[:, width:].astype(BF16)
    out_ref[:, pl.ds(other, half)] = got_ref[0:block, width:].astype(BF16)
    grad_ref[...] = (mine_ref[:, 0:width] + got_ref[0:block, 0:width]).astype(BF16)
    small_ref[...] = sent_ref[block:, 0:width] + got_ref[block:, 0:width]


def join(sel, mine, sent, got):
    block, width = mine.shape[0], mine.shape[1] * 2 // 3
    return pl.pallas_call(
        join_kernel,
        out_shape=(shaped((block, width), BF16), shaped((block, width), BF16), shaped((8, width))),
        in_specs=[smem(), vmem(), vmem(), vmem()],
        out_specs=(vmem(),) * 3,
        compiler_params=params(16),
        name="join",
    )(sel, mine, sent, got)


def place_kernel(sel, *refs, count, first):
    pieces, target, sem = refs[:count], refs[-2], refs[-1]
    rows, cols = pieces[0].shape[0], pieces[0].shape[1] // 3
    width = target.shape[1] // 3
    copies = []
    for i, piece in enumerate(pieces):
        row = pl.multiple_of(sel[2 * (first + i)] * rows, rows)
        col = sel[2 * (first + i) + 1] * cols
        for k in range(3):
            to = pl.multiple_of(col + k * width, cols)
            copies.append(
                pltpu.make_async_copy(
                    piece.at[:, pl.ds(k * cols, cols)],
                    target.at[pl.ds(row, rows), pl.ds(to, cols)],
                    sem.at[3 * i + k],
                )
            )
    for c in copies:
        c.start()
    for c in copies:
        c.wait()


def place(sel, pieces, first, target, shape):
    count = len(pieces)
    extra = [] if target is None else [target]
    return pl.pallas_call(
        functools.partial(place_kernel, count=count, first=first),
        out_shape=shaped(shape),
        in_specs=[smem()] + [vmem()] * count + [any_spec()] * len(extra),
        out_specs=any_spec(),
        scratch_shapes=[pltpu.SemaphoreType.DMA((3 * count,))],
        input_output_aliases={1 + count: 0} if extra else {},
        compiler_params=params(16),
        name="place",
    )(sel, *pieces, *extra)


def on_device(
    tokens,
    offsets,
    w_proj,
    forget_weight,
    reset_weight,
    forget_bias,
    reset_bias,
    layer_norm_gain,
    layer_norm_bias,
    cotangent,
):
    _, block, width = tokens.shape
    z, y, x, c = (lax.axis_index(a) for a in ("z", "y", "x", "c"))
    tuned = lax.axis_size("z") == 4
    mine = 2 * x + c
    int32 = lambda values: jnp.stack([jnp.asarray(v, jnp.int32) for v in values])

    cot = cotangent[0]
    own = widen(tokens[0])
    tok_x = swap(own, "x")
    tok_c = swap(own, "c")
    cot_sibling = swap(widen_cot(int32([1 - c]), cot), "c")
    cot_far = swap(pack_cot(int32([2 * (1 - x) + c, 1 - x]), cot, cot_sibling), "x")
    tok_xc = swap(tok_x, "c")

    at = jnp.stack([2 * x + c, 2 * x + 1 - c, 2 * (1 - x) + c, 2 * (1 - x) + 1 - c])
    positions = (at[:, None] * block + jnp.arange(block)[None, :]).reshape(-1)
    hits = jnp.any(positions[:, None] == offsets[0][None, :], axis=1)
    keep = jnp.where(hits, 0.0, 1.0).astype(F32)[:, None]
    pad = jnp.zeros((4, width), F32)
    gates = jnp.concatenate([jnp.stack([forget_weight, reset_weight, forget_bias, reset_bias]), pad])
    norm = jnp.concatenate([jnp.stack([layer_norm_gain, layer_norm_bias]), pad, pad[:2]])

    stored = [2 * ((k // 2) ^ x) + ((k % 2) ^ c) for k in range(4)]
    order = (2, 3, 1, 0)
    send_rows = [2 * (z ^ d) + 1 - y for d in order] if tuned else list(range(4))
    keep_rows = [2 * (z ^ d) + y for d in order] if tuned else list(range(4, 8))
    sel = int32([mine, *stored, *send_rows, x])
    near = run_near(sel, (own, tok_c), w_proj, gates, norm)
    far = run_forward(sel, (tok_x, tok_xc), near[1:], keep, w_proj, gates, norm)
    normed = (near[0], far[0])
    toks = (own, tok_c, tok_x, tok_xc)
    dproj, out, dxh, gate_small, *sends = run_backward(
        sel, toks, (cot, cot_sibling, cot_far), far[1:], keep, gates, normed, 4
    )
    keeps = run_products(int32(keep_rows), normed, dproj, 4)

    grad_mine, grad_send = run_input(sel, toks, dproj, dxh, out, gate_small, w_proj, norm)
    kept, sent = combine(int32([c]), grad_mine, swap(grad_send, "c"))
    output, input_grad, small = join(int32([x]), kept, sent, swap(sent, "x"))

    if tuned:
        q2, q3, q1, q0 = (keep + swap(send, "y") for keep, send in zip(keeps, sends))
        h3 = q3 + xor_permute(q2, "z", 1)
        total = q0 + xor_permute(q1, "z", 1) + xor_permute(h3, "z", 3)
        small = small + swap(small, "y")
        small = small + xor_permute(small, "z", 1)
        small = small + xor_permute(small, "z", 2)
        z1, z3 = xor_permute(total, "z", 1), xor_permute(total, "z", 3)
        column = ((0, total), (1, z1), (3, z3), (2, xor_permute(z3, "z", 1)))
        held = []
        for d, piece in column:
            px, py = swap(piece, "x"), swap(piece, "y")
            corner = swap(px, "y") if d in (0, 3) else swap(py, "x")
            row, row_y = 2 * (z ^ d) + y, 2 * (z ^ d) + 1 - y
            held.append(((piece, row, x), (px, row, 1 - x), (py, row_y, x), (corner, row_y, 1 - x)))
    else:
        small = lax.psum(small, ("z", "y"))
        pieces = lax.psum(jnp.stack(sends + list(keeps)), ("z", "y"))
        across = swap(pieces, "x")
        held = [
            tuple((part[r], r, at) for r in range(8)) for part, at in ((pieces, x), (across, 1 - x))
        ]
    where, first = [], 0
    for group in held:
        for _, row, x_at in group:
            where += [row, 2 * x_at + c, row, 2 * x_at + 1 - c]
    where = int32(where)
    proj_grad = None
    for group in held:
        arrays = []
        for piece, _, _ in group:
            arrays += [piece, swap(piece, "c")]
        proj_grad = place(where, arrays, first, proj_grad, (width, 3 * width))
        first += len(arrays)
    return (output[None], input_grad[None], proj_grad, *(small[i] for i in range(6)))


def solution(mesh):
    dp, rep = mesh.shape["dp"], mesh.shape["rep"]
    fine = Mesh(mesh.devices.reshape(dp // 2, 2, rep // 2, 2), ("z", "y", "x", "c"))
    row, seq = ("z", "y"), ("x", "c")
    in_specs = (P(row, seq, None), P(row, None)) + (P(),) * 7 + (P(row, seq, None),)
    out_specs = (P(row, seq, None), P(row, seq, None)) + (P(),) * 7
    return jax.shard_map(
        on_device, mesh=fine, in_specs=in_specs, out_specs=out_specs, check_vma=False
    )
```

```python
import functools

import jax
import jax.numpy as jnp
from jax import lax
from jax.experimental import pallas as pl
from jax.experimental.pallas import tpu as pltpu
from jax.sharding import Mesh
from jax.sharding import PartitionSpec as P

EPS = 1e-05
SWAP = [(0, 1), (1, 0)]
VMEM_BYTES = 56 * 2**20
F32 = jnp.float32
BF16 = jnp.bfloat16


def swap(block, axis):
    return lax.ppermute(block, axis, SWAP)


def xor_permute(block, axis, distance):
    size = lax.axis_size(axis)
    return lax.ppermute(block, axis, [(i, i ^ distance) for i in range(size)])


def any_spec():
    return pl.BlockSpec(memory_space=pl.ANY)


def hbm():
    return pl.BlockSpec(memory_space=pltpu.HBM)


def vmem():
    return pl.BlockSpec(memory_space=pltpu.VMEM)


def smem():
    return pl.BlockSpec(memory_space=pltpu.SMEM)


def shaped(shape, dtype=F32):
    return jax.ShapeDtypeStruct(shape, dtype)


def params(mib):
    return pltpu.CompilerParams(vmem_limit_bytes=mib * 2**20)


def cost(us):
    return pl.CostEstimate(
        flops=int(us * 1.1e9), bytes_accessed=int(us * 3.6e6), transcendentals=0
    )


def own_columns(sel, cols):
    return pl.ds(pl.multiple_of((2 * sel[0] + sel[1]) * cols, cols), cols)


def stored_at(sel, k):
    return 2 * ((k // 2) ^ sel[0]) + ((k % 2) ^ sel[1])


def row_part(sel, row):
    return row if isinstance(row, int) else 2 * (sel[3] ^ row[0]) + (sel[2] ^ row[1])


def tick_kernel(*refs):
    refs[-1][...] = jnp.zeros(refs[-1].shape, F32)


def tick(*values):
    return pl.pallas_call(
        tick_kernel,
        out_shape=shaped((8, 128)),
        in_specs=[any_spec()] * len(values),
        out_specs=vmem(),
        compiler_params=params(1),
        cost_estimate=cost(20),
        name="tick",
    )(*values)


def hold_kernel(*refs):
    del refs


def hold(values, *waits):
    count = len(values)
    return pl.pallas_call(
        hold_kernel,
        out_shape=tuple(shaped(v.shape, v.dtype) for v in values),
        in_specs=[any_spec()] * (count + len(waits)),
        out_specs=(any_spec(),) * count,
        input_output_aliases={i: i for i in range(count)},
        compiler_params=params(1),
        cost_estimate=cost(0.05),
        name="hold",
    )(*values, *waits)


def add_kernel(a_ref, b_ref, *refs):
    refs[-1][...] = a_ref[...] + b_ref[...]


def add(a, b, *waits):
    return pl.pallas_call(
        add_kernel,
        out_shape=shaped(a.shape),
        in_specs=[vmem()] * 2 + [any_spec()] * len(waits),
        out_specs=vmem(),
        compiler_params=params(4),
        cost_estimate=cost(0.05),
        name="add",
    )(a, b, *waits)


def take_weights_kernel(sel, w_ref, mine_ref, sem):
    width, cols = mine_ref.shape[0], mine_ref.shape[1] // 3
    copies = []
    for k in range(3):
        at = pl.multiple_of((2 * sel[0] + sel[1]) * cols + k * width, cols)
        copies.append(
            pltpu.make_async_copy(
                w_ref.at[:, pl.ds(at, cols)], mine_ref.at[:, k * cols : (k + 1) * cols], sem.at[k]
            )
        )
    for c in copies:
        c.start()
    for c in copies:
        c.wait()


def take_weights(sel, w_proj):
    width = w_proj.shape[0]
    return pl.pallas_call(
        take_weights_kernel,
        out_shape=shaped((width, 3 * width // 4), BF16),
        in_specs=[smem(), hbm()],
        out_specs=vmem(),
        scratch_shapes=[pltpu.SemaphoreType.DMA((3,))],
        compiler_params=params(4),
        cost_estimate=cost(3),
        name="take_weights",
    )(sel, w_proj)


def widen_cot_kernel(sel, cot_ref, cot_out):
    cols = cot_ref.shape[1] // 4
    for k in range(2):
        at = pl.multiple_of((2 * k + 1 - sel[1]) * cols, cols)
        cot_out[:, k * cols : (k + 1) * cols] = cot_ref[:, pl.ds(at, cols)].astype(F32)


def widen_cot(sel, cot):
    return pl.pallas_call(
        widen_cot_kernel,
        out_shape=shaped((cot.shape[0], cot.shape[1] // 2)),
        in_specs=[smem(), vmem()],
        out_specs=vmem(),
        compiler_params=params(4),
        cost_estimate=cost(2),
        name="widen_cot",
    )(sel, cot)


def pack_cot_kernel(sel, cot_ref, sibling_ref, cot_out):
    block, cols = cot_ref.shape[0], cot_ref.shape[1] // 4
    mine = pl.multiple_of((2 * (1 - sel[0]) + sel[1]) * cols, cols)
    cot_out[0:block, :] = cot_ref[:, pl.ds(mine, cols)].astype(F32)
    sibling = pl.multiple_of((1 - sel[0]) * cols, cols)
    cot_out[block:, :] = sibling_ref[:, pl.ds(sibling, cols)]


def pack_cot(sel, cot, sibling):
    return pl.pallas_call(
        pack_cot_kernel,
        out_shape=shaped((2 * cot.shape[0], cot.shape[1] // 4)),
        in_specs=[smem(), vmem(), vmem()],
        out_specs=vmem(),
        compiler_params=params(4),
        cost_estimate=cost(2),
        name="pack_cot",
    )(sel, cot, sibling)


def standardized(x):
    mean = jnp.mean(x, axis=-1, keepdims=True)
    centred = x - mean
    rdev = lax.rsqrt(jnp.mean(centred * centred, axis=-1, keepdims=True) + EPS)
    return centred * rdev, rdev


def norm_and_project(sel, toks, norm, w_ref, gates, normed, cand, zf, zr, base):
    cols = cand.shape[1]
    mine = own_columns(sel, cols)
    gain, bias = norm[0][...], norm[1][...]
    fb, rb = gates[2][:, mine], gates[3][:, mine]
    block = toks[0].shape[0]
    step = 16
    for at, tok in enumerate(toks):

        def body(i, carry, tok=tok, at=at):
            here = pl.ds(pl.multiple_of(i * step, step), step)
            there = pl.ds(pl.multiple_of(at * block + i * step, step), step)
            xhat, _ = standardized(tok[here, :])
            normed[there, :] = (xhat * gain + bias).astype(BF16)
            return carry

        lax.fori_loop(0, block // step, body, 0, unroll=True)
    rows = normed[...]
    here = slice(base, base + 2 * block)
    part = lambda k: jnp.dot(
        rows, w_ref[:, k * cols : (k + 1) * cols], preferred_element_type=F32
    )
    cand[here, :] = part(0)
    zf[here, :] = 0.5 * (part(1) + fb)
    zr[here, :] = 0.5 * (part(2) + rb)


def near_kernel(sel, offsets, tok0, tok1, w_ref, *refs):
    gates, norm, (normed, cand, zf, zr, half_keep) = refs[:4], refs[4:6], refs[6:]
    length, cols = half_keep.shape
    block = length // 4
    step = 16
    for b in range(4):
        base = stored_at(sel, b) * block

        def body(i, carry, b=b, base=base):
            at = pl.multiple_of(i * step, step)
            token = base + at + lax.broadcasted_iota(jnp.int32, (step, cols), 0)
            starts = token == offsets[0, 0]
            for k in range(1, offsets.shape[1]):
                starts = starts | (token == offsets[0, k])
            here = pl.ds(pl.multiple_of(b * block + at, step), step)
            half_keep[here, :] = jnp.where(starts, 0.0, 0.5)
            return carry

        lax.fori_loop(0, block // step, body, 0)
    norm_and_project(sel, (tok0, tok1), norm, w_ref, gates, normed, cand, zf, zr, 0)


def run_near(sel, offsets, toks, w_mine, vectors):
    block, width = toks[0].shape
    cols = width // 4
    return pl.pallas_call(
        near_kernel,
        out_shape=(shaped((2 * block, width), BF16),)
        + (shaped((2 * block, cols)),) * 3
        + (shaped((4 * block, cols)),),
        in_specs=[smem()] * 2 + [vmem()] * 9,
        out_specs=(vmem(),) * 5,
        compiler_params=params(16),
        cost_estimate=cost(10),
        name="near_blocks",
    )(sel, offsets, *toks, w_mine, *vectors)


def forward_kernel(sel, tok0, tok1, cand_near, zf_near, zr_near, half_keep, w_ref, *refs):
    gates, norm, (normed, cand, zf, zr, state, half_prev) = refs[:4], refs[4:6], refs[6:]
    length, cols = cand.shape
    block = length // 4
    near = slice(0, 2 * block)
    cand[near, :], zf[near, :], zr[near, :] = cand_near[...], zf_near[...], zr_near[...]
    fw = gates[0][:, own_columns(sel, cols)]
    norm_and_project(sel, (tok0, tok1), norm, w_ref, gates, normed, cand, zf, zr, 2 * block)
    c = jnp.zeros((1, cols), F32)
    for k in range(4):
        base = stored_at(sel, k) * block

        def body(i, c, base=base):
            row = pl.ds(base + i, 1)
            half = half_keep[row, :]
            th = jnp.tanh(zf[row, :] + (half * fw) * c)
            hp = half * c
            hc = 0.5 * cand[row, :]
            c = (hp + hc) + (hp - hc) * th
            state[row, :] = c
            half_prev[row, :] = hp
            return c

        c = lax.fori_loop(0, block, body, c, unroll=16)


def run_forward(sel, toks, near, w_mine, vectors):
    block, width = toks[0].shape
    cols = width // 4
    length = 4 * block
    return pl.pallas_call(
        forward_kernel,
        out_shape=(shaped((2 * block, width), BF16),) + (shaped((length, cols)),) * 5,
        in_specs=[smem()] + [vmem()] * 13,
        out_specs=(vmem(),) * 6,
        compiler_params=params(20),
        cost_estimate=cost(20),
        name="forward_scan",
    )(sel, *toks, *near, w_mine, *vectors)


def backward_kernel(
    sel,
    x0,
    x1,
    x2,
    x3,
    g0,
    g1,
    g23,
    cand_ref,
    zf_ref,
    zr_ref,
    state,
    half_prev,
    half_keep,
    fw_ref,
    rw_ref,
    near_ref,
    far_ref,
    dproj_ref,
    out_ref,
    dxh_ref,
    small_ref,
    *refs,
    rows,
):
    products, (coef, add_b, add_e, gz, omf) = refs[: len(rows)], refs[len(rows) :]
    length, cols = cand_ref.shape
    block = length // 4
    mine = own_columns(sel, cols)
    half = pl.ds(pl.multiple_of(sel[0] * cols, cols), cols)
    fw, rw = fw_ref[:, mine], rw_ref[:, mine]
    half_fw, half_rw = 0.5 * fw, 0.5 * rw
    step = 16
    zero = jnp.zeros((step, cols), F32)
    sums = (zero, zero)
    everything = slice(0, cols)
    sources = (
        (x0, g0, 0, mine),
        (x1, g1, 0, half),
        (x2, g23, 0, everything),
        (x3, g23, block, everything),
    )
    for b, (x_ref, g_ref, g_at, g_cols) in enumerate(sources):

        def gate_body(i, carry, b=b, x_ref=x_ref, g_ref=g_ref, g_at=g_at, g_cols=g_cols):
            at = pl.multiple_of(i * step, step)
            here = pl.ds(pl.multiple_of(b * block + at, step), step)
            x = x_ref[pl.ds(at, step), mine]
            g = g_ref[pl.ds(pl.multiple_of(g_at + at, step), step), g_cols].astype(F32)
            keep = 2.0 * half_keep[here, :]
            prev = 2.0 * half_prev[here, :]
            c, cd = state[here, :], cand_ref[here, :]
            forget = 0.5 + 0.5 * jnp.tanh(zf_ref[here, :] + half_fw * prev)
            reset = 0.5 + 0.5 * jnp.tanh(zr_ref[here, :] + half_rw * prev)
            not_forget, not_reset = 1.0 - forget, 1.0 - reset
            out_ref[here, :] = reset * c + not_reset * x
            dxh_ref[here, :] = g * not_reset
            dzr = g * (c - x) * reset * not_reset
            slope = (prev - cd) * forget * not_forget
            coef[here, :] = keep * (forget + slope * fw)
            add_b[here, :] = keep * (dzr * rw)
            add_e[here, :] = g * reset
            gz[here, :] = slope
            omf[here, :] = not_forget
            dproj_ref[here, 2 * cols : 3 * cols] = dzr.astype(BF16)
            return (carry[0] + dzr * prev, carry[1] + dzr)

        sums = lax.fori_loop(0, block // step, gate_body, sums, unroll=True)
    rw_sum, rb_sum = sums

    s = jnp.zeros((1, cols), F32)
    for k in range(3, -1, -1):
        last = stored_at(sel, k) * block + block - 1

        def backward_body(i, s, last=last):
            row = pl.ds(last - i, 1)
            total = s + add_e[row, :]
            add_e[row, :] = total
            return coef[row, :] * total + add_b[row, :]

        s = lax.fori_loop(0, block, backward_body, s, unroll=16)

    def grad_body(i, carry):
        here = pl.ds(pl.multiple_of(i * step, step), step)
        total = add_e[here, :]
        prev = 2.0 * half_prev[here, :]
        dzf = total * gz[here, :]
        dproj_ref[here, 0:cols] = (total * omf[here, :]).astype(BF16)
        dproj_ref[here, cols : 2 * cols] = dzf.astype(BF16)
        return (carry[0] + dzf * prev, carry[1] + dzf)

    fw_sum, fb_sum = lax.fori_loop(0, length // step, grad_body, (zero, zero), unroll=4)
    small_ref[...] = jnp.concatenate(
        [jnp.sum(v, axis=0, keepdims=True) for v in (fw_sum, rw_sum, fb_sum, rb_sum)]
        + [jnp.zeros((4, cols), F32)],
        axis=0,
    )
    outer_products(sel, rows, near_ref, far_ref, dproj_ref, products)


def outer_products(sel, rows, near_ref, far_ref, dproj_ref, outs):
    half, width = near_ref.shape
    part = width // 8
    dims = (((0,), (0,)), ((), ()))
    for out, places in zip(outs, rows):
        for k, place_of in enumerate(places):
            at = pl.ds(pl.multiple_of(row_part(sel, place_of) * part, part), part)
            out[k * part : (k + 1) * part, :] = lax.dot_general(
                near_ref[:, at], dproj_ref[0:half, :], dims, preferred_element_type=F32
            ) + lax.dot_general(
                far_ref[:, at], dproj_ref[half:, :], dims, preferred_element_type=F32
            )


def product_shapes(width, rows):
    return tuple(shaped((len(places) * width // 8, 3 * width // 4)) for places in rows)


def run_backward(sel, toks, cots, scanned, half_keep, gates, normed, rows):
    block, width = toks[0].shape
    cols = width // 4
    length = 4 * block
    return pl.pallas_call(
        functools.partial(backward_kernel, rows=rows),
        out_shape=(
            shaped((length, 3 * cols), BF16),
            shaped((length, cols)),
            shaped((length, cols)),
            shaped((8, cols)),
        )
        + product_shapes(width, rows),
        in_specs=[smem()] + [vmem()] * 17,
        out_specs=(vmem(),) * (4 + len(rows)),
        scratch_shapes=[pltpu.VMEM((length, cols), F32)] * 5,
        compiler_params=params(24),
        cost_estimate=cost(20),
        name="backward_scan",
    )(sel, *toks, *cots, *scanned, half_keep, *gates[:2], *normed)


def products_kernel(sel, near_ref, far_ref, dproj_ref, *outs, rows):
    outer_products(sel, rows, near_ref, far_ref, dproj_ref, outs)


def run_products(sel, normed, dproj, rows):
    return pl.pallas_call(
        functools.partial(products_kernel, rows=rows),
        out_shape=product_shapes(normed[0].shape[1], rows),
        in_specs=[smem()] + [vmem()] * 3,
        out_specs=(vmem(),) * len(rows),
        compiler_params=params(12),
        cost_estimate=cost(0.05),
        name="products",
    )(sel, *normed, dproj)


def input_kernel(
    sel,
    tok0,
    tok1,
    tok2,
    tok3,
    dproj_ref,
    dxh_ref,
    out_ref,
    gate_small_ref,
    w_ref,
    gain_ref,
    *refs,
):
    mine_ref, send_ref, dnormed = refs[-3:]
    cols = dxh_ref.shape[1]
    block, width = tok0.shape
    gain = gain_ref[...]
    mine = own_columns(sel, cols)
    step = 8
    sums = (jnp.zeros((step, width), F32), jnp.zeros((step, width), F32))
    for b, tok in enumerate((tok0, tok1, tok2, tok3)):
        rows = slice(b * block, (b + 1) * block)
        dnormed[...] = lax.dot_general(
            dproj_ref[rows, :], w_ref[...], (((1,), (1,)), ((), ())), preferred_element_type=F32
        )
        where = send_ref if b % 2 else mine_ref
        base = (b // 2) * block

        def body(i, carry, tok=tok, base=base, where=where):
            here = pl.ds(pl.multiple_of(i * step, step), step)
            there = pl.ds(pl.multiple_of(base + i * step, step), step)
            xhat, rdev = standardized(tok[here, :])
            dn = dnormed[here, :]
            dxhat = dn * gain
            mean1 = jnp.mean(dxhat, axis=-1, keepdims=True)
            mean2 = jnp.mean(dxhat * xhat, axis=-1, keepdims=True)
            where[there, 0:width] = rdev * (dxhat - mean1 - xhat * mean2)
            return (carry[0] + dn * xhat, carry[1] + dn)

        sums = lax.fori_loop(0, block // step, body, sums, unroll=11)
        to = pl.ds(base, block)
        where[to, mine] += dxh_ref[rows, :]
        where[to, width : width + cols] = out_ref[rows, :]
    tail = slice(2 * block, 2 * block + 8)
    mine_ref[tail, :] = jnp.zeros((8, width + cols), F32)
    mine_ref[2 * block : 2 * block + 4, mine] = gate_small_ref[0:4, :]
    for i, v in enumerate(sums):
        row = 2 * block + 4 + i
        mine_ref[row : row + 1, 0:width] = jnp.sum(v, axis=0, keepdims=True)
    send_ref[tail, :] = mine_ref[tail, :]


def run_input(sel, toks, dproj, dxh, out, gate_small, w_mine, gain, *waits):
    block, width = toks[0].shape
    shape = (2 * block + 8, width + width // 4)
    return pl.pallas_call(
        input_kernel,
        out_shape=(shaped(shape), shaped(shape)),
        in_specs=[smem()] + [vmem()] * 10 + [any_spec()] * len(waits),
        out_specs=(vmem(),) * 2,
        scratch_shapes=[pltpu.VMEM((block, width), F32)],
        compiler_params=params(20),
        cost_estimate=cost(0.05),
        name="input_side",
    )(sel, *toks, dproj, dxh, out, gate_small, w_mine, gain, *waits)


def combine_kernel(sel, mine_ref, got_ref, *refs):
    keep_ref, send_ref, small_ref = refs[-3:]
    block, width = keep_ref.shape[0], small_ref.shape[1]
    cols = width // 4
    low = pl.ds(pl.multiple_of(width + sel[1] * cols, cols), cols)
    high = pl.ds(pl.multiple_of(width + (1 - sel[1]) * cols, cols), cols)
    for ref, first in ((keep_ref, 0), (send_ref, block)):
        here = slice(first, first + block)
        ref[:, 0:width] = mine_ref[here, 0:width] + got_ref[here, 0:width]
        ref[:, low] = mine_ref[here, width:]
        ref[:, high] = got_ref[here, width:]
    small_ref[...] = mine_ref[2 * block :, 0:width] + got_ref[2 * block :, 0:width]


def combine(sel, mine, got, *waits):
    block, width = (mine.shape[0] - 8) // 2, mine.shape[1] * 4 // 5
    return pl.pallas_call(
        combine_kernel,
        out_shape=(shaped((block, width * 3 // 2)),) * 2 + (shaped((8, width)),),
        in_specs=[smem(), vmem(), vmem()] + [any_spec()] * len(waits),
        out_specs=(vmem(),) * 3,
        compiler_params=params(16),
        cost_estimate=cost(0.05),
        name="combine",
    )(sel, mine, got, *waits)


def join_kernel(sel, mine_ref, got_ref, out_ref, grad_ref):
    width = out_ref.shape[1]
    half = width // 2
    at = pl.multiple_of(sel[0] * half, half)
    other = pl.multiple_of((1 - sel[0]) * half, half)
    out_ref[:, pl.ds(at, half)] = mine_ref[:, width:].astype(BF16)
    out_ref[:, pl.ds(other, half)] = got_ref[:, width:].astype(BF16)
    grad_ref[...] = (mine_ref[:, 0:width] + got_ref[:, 0:width]).astype(BF16)


def join(sel, mine, got):
    block, width = mine.shape[0], mine.shape[1] * 2 // 3
    return pl.pallas_call(
        join_kernel,
        out_shape=(shaped((block, width), BF16),) * 2,
        in_specs=[smem()] + [vmem()] * 2,
        out_specs=(vmem(),) * 2,
        compiler_params=params(16),
        cost_estimate=cost(0.05),
        name="join",
    )(sel, mine, got)


def fold_small(small):
    rows, cols = 6, small.shape[1] // 4
    tails = [small[i : i + 1, 3 * cols :] for i in range(rows)]
    last = [jnp.concatenate(tails[:3], axis=1), jnp.concatenate(tails[3:], axis=1)]
    return jnp.concatenate([small[0:rows, : 3 * cols]] + last, axis=0)


def finish_kernel(keep_ref, got_ref, a1_ref, a3_ref, small_mine, small_got, total_ref):
    part = keep_ref.shape[0]
    total_ref[0:part, :] = keep_ref[...] + got_ref[...] + a1_ref[...] + a3_ref[...]
    total_ref[part:, :] = fold_small(small_mine[...] + small_got[...])


def finish(keep, got, a1, a3, small_mine, small_got):
    part, cols3 = keep.shape
    return pl.pallas_call(
        finish_kernel,
        out_shape=shaped((part + 8, cols3)),
        in_specs=[vmem()] * 6,
        out_specs=vmem(),
        compiler_params=params(8),
        cost_estimate=cost(0.05),
        name="finish",
    )(keep, got, a1, a3, small_mine, small_got)


def first_kernel(a_ref, first_ref):
    first_ref[...] = a_ref[0 : first_ref.shape[0], :]


def first_half(a):
    return pl.pallas_call(
        first_kernel,
        out_shape=shaped((a.shape[0] // 2, a.shape[1])),
        in_specs=[vmem()],
        out_specs=vmem(),
        compiler_params=params(6),
        cost_estimate=cost(0.05),
        name="first_half",
    )(a)


def pair_kernel(a_ref, b_ref, pair_ref):
    rows = a_ref.shape[0]
    pair_ref[0:rows, :] = a_ref[...]
    pair_ref[rows:, :] = b_ref[...]


def pair(a, b):
    rows, cols3 = a.shape
    return pl.pallas_call(
        pair_kernel,
        out_shape=shaped((2 * rows, cols3)),
        in_specs=[vmem()] * 2,
        out_specs=vmem(),
        compiler_params=params(6),
        cost_estimate=cost(0.05),
        name="pair",
    )(a, b)


def small_kernel(*refs, where):
    pieces, outs = refs[:-6], refs[-6:]
    sums = [pieces[i][at : at + 8, :] for i, at in where]
    while len(sums) > 1:
        sums = [a + b for a, b in zip(sums[::2], sums[1::2])]
    total = sums[0]
    cols = total.shape[1] // 3
    for i, out in enumerate(outs):
        out[:, 0 : 3 * cols] = total[i : i + 1, :]
        out[:, 3 * cols :] = total[6 + i // 3 : 7 + i // 3, (i % 3) * cols : (i % 3 + 1) * cols]


def small_sums(pieces, where):
    width = pieces[0].shape[1] // 3 * 4
    return pl.pallas_call(
        functools.partial(small_kernel, where=where),
        out_shape=(shaped((1, width)),) * 6,
        in_specs=[vmem()] * len(pieces),
        out_specs=(vmem(),) * 6,
        compiler_params=params(8),
        cost_estimate=cost(0.05),
        name="small_sums",
    )(*pieces)


def place_kernel(sel, *refs, where, give):
    target, sem = refs[-2 - bool(give)], refs[-1]
    cols = refs[0].shape[1] // 3
    width = target.shape[1] // 3
    part = width // 8
    copies = []

    def copy(src, dst):
        copies.append(pltpu.make_async_copy(src, dst, sem.at[len(copies)]))
        copies[-1].start()

    for at, (array, first, row, x_off, c_off) in enumerate(where):
        piece = refs[array].at[pl.ds(first, part)]
        to_row = pl.multiple_of(row_part(sel, row) * part, part)
        col = (2 * (sel[0] ^ x_off) + (sel[1] ^ c_off)) * cols
        for k in range(3):
            to = pl.multiple_of(col + k * width, cols)
            copy(piece.at[:, pl.ds(k * cols, cols)], target.at[pl.ds(to_row, part), pl.ds(to, cols)])
        if at < give:
            copy(piece, refs[-2].at[pl.ds(at * part, part)])
    for c in copies:
        c.wait()


def place(sel, arrays, where, target, width, give, *waits):
    count = len(arrays)
    extra = [] if target is None else [target]
    cols3 = 3 * width // 4
    return pl.pallas_call(
        functools.partial(place_kernel, where=where, give=give),
        out_shape=(shaped((width, 3 * width)),)
        + ((shaped((give * width // 8, cols3)),) if give else ()),
        in_specs=[smem()]
        + [vmem()] * count
        + [hbm()] * len(extra)
        + [any_spec()] * len(waits),
        out_specs=(hbm(), vmem()) if give else (hbm(),),
        scratch_shapes=[pltpu.SemaphoreType.DMA((3 * len(where) + give,))],
        input_output_aliases={1 + count: 0} if extra else {},
        compiler_params=params(8),
        cost_estimate=cost(0.05),
        name="place",
    )(sel, *arrays, *extra, *waits)


def given(array, where, part):
    return [(array, i * part, row, x_off, 1) for i, (_, _, row, x_off, _) in enumerate(where)]


def on_device(
    tokens,
    offsets,
    w_proj,
    forget_weight,
    reset_weight,
    forget_bias,
    reset_bias,
    layer_norm_gain,
    layer_norm_bias,
    cotangent,
):
    _, block, width = tokens.shape
    z, y, x, c = (lax.axis_index(a) for a in ("z", "y", "x", "c"))
    tuned = lax.axis_size("z") == 4
    sel = jnp.stack([x, c, y, z]).astype(jnp.int32)
    part = width // 8

    cot = cotangent[0]
    own = lax.optimization_barrier(tokens[0].astype(F32))
    tok_x = swap(own, "x")
    tok_c = swap(own, "c")
    cot_sibling = swap(widen_cot(sel, cot), "c")
    cot_packed = pack_cot(sel, cot, cot_sibling)
    cot_far = swap(cot_packed, "x")

    gates = [
        v.reshape(1, width) for v in (forget_weight, reset_weight, forget_bias, reset_bias)
    ]
    gain = layer_norm_gain.reshape(1, width)
    vectors = (*gates, gain, layer_norm_bias.reshape(1, width))
    w_mine = take_weights(sel, w_proj)
    near = run_near(sel, offsets, (own, tok_c), w_mine, vectors)
    (tok_x,) = hold((tok_x,), near[4], cot_packed)
    tok_xc = swap(tok_x, "c")
    far = run_forward(sel, (tok_x, tok_xc), near[1:], w_mine, vectors)
    normed = (near[0], far[0])
    toks = (own, tok_c, tok_x, tok_xc)
    if tuned:
        rows = [[[(d, 1)] for d in (2, 3, 1, 0)], [[(d, 0)] for d in (2, 3, 1, 0)]]
    else:
        rows = [[[0], [1], [2], [3]], [[4], [5], [6], [7]]]
    dproj, out, dxh, gate_small, s2 = run_backward(
        sel, toks, (cot, cot_sibling, cot_far), far[1:], near[4], gates, normed, rows[0][:1]
    )
    s3, s1, s0 = run_products(sel, normed, dproj, rows[0][1:])
    k2, k3, k1, k0 = run_products(sel, normed, dproj, rows[1])
    input_side = lambda *waits: run_input(
        sel, toks, dproj, dxh, out, gate_small, w_mine, gain, *waits
    )

    if tuned:
        r2, r3, r1, r0 = (swap(piece, "y") for piece in (s2, s3, s1, s0))
        q2 = add(k2, r2, s0)
        a2 = xor_permute(q2, "z", 1)
        grad_mine, grad_send = input_side(q2)
        h3 = add(add(k3, r3), a2)
        a3 = xor_permute(h3, "z", 3)
        kept, sent, small = combine(
            sel, grad_mine, swap(grad_send, "c"), h3, tick(grad_send)
        )
        small_got = swap(small, "x")
        (sent,) = hold((sent,), small_got)
        got = swap(sent, "x")
        a1 = xor_permute(add(k1, r1, sent), "z", 1)
        total = finish(k0, r0, a1, a3, small, small_got)
        output, input_grad = join(sel, kept, got)

        z3, px0, py0 = xor_permute(total, "z", 3), swap(total, "x"), swap(total, "y")
        z1 = xor_permute(total, "z", 1)
        (px0,) = hold((px0,), input_grad)
        corner0 = swap(px0, "y")
        z3, z1, corner0, py0 = hold((z3, z1, corner0, py0))
        z13 = pair(z1, z3)
        z2, px13, py13 = xor_permute(z3, "z", 1), swap(z13, "x"), swap(z13, "y")
        corner3 = xor_permute(corner0, "z", 3)
        own = [(0, 0, (0, 0), 0, 0), (1, 0, (0, 0), 1, 0), (2, 0, (0, 1), 0, 0), (3, 0, (0, 1), 1, 0)]
        proj_grad, give = place(sel, (total, px0, py0, corner0), own, None, width, 4)
        z2, px13, py13, corner3 = hold((z2, px13, py13, corner3), give)
        px2, py2 = swap(z2, "x"), swap(z2, "y")
        corner12 = xor_permute(pair(corner0, corner3), "z", 1)
        other = given(3, own, part)
        own = [
            (array, (part + 8) * i, (d, y_off), x_off, 0)
            for array, y_off, x_off in ((0, 0, 0), (1, 0, 1), (2, 1, 0))
            for i, d in ((0, 1), (1, 3))
        ]
        proj_grad, give = place(
            sel,
            (z13, px13, py13, swap(give, "c")),
            own + other,
            proj_grad,
            width,
            6,
            tick(give),
        )
        other = given(2, own, part)
        own = [(0, 0, (2, 0), 0, 0), (1, 0, (3, 1), 1, 0)]
        proj_grad, give = place(
            sel, (z2, corner3, swap(give, "c")), own + other, proj_grad, width, 2, tick(give)
        )
        px2, py2, corner12 = hold((px2, py2, corner12), give)
        other = given(0, own, part)
        arrays, places = [swap(give, "c")], []
        last = (
            (px2, (((2, 0), 1),)),
            (py2, (((2, 1), 0),)),
            (corner12, (((1, 1), 1), ((2, 1), 1))),
        )
        for piece, parts in last:
            for held, c_off in ((piece, 0), (swap(piece, "c"), 1)):
                for i, (row, x_off) in enumerate(parts):
                    places.append((len(arrays), (part + 8) * i, row, x_off, c_off))
                arrays.append(held)
        (proj_grad,) = place(sel, arrays, other + places, proj_grad, width, 0, tick(give))
        tail = part + 8 + part
        where = [(0, part), (1, part), (2, part), (3, part), (4, part), (5, part), (2, tail), (3, tail)]
        small = small_sums((total, py0, z13, py13, z2, py2), where)
    else:
        grad_mine, grad_send = input_side()
        kept, sent, small = combine(sel, grad_mine, swap(grad_send, "c"))
        got = swap(sent, "x")
        small = lax.psum(small + swap(small, "x"), ("z", "y"))
        pieces = jnp.stack([s2, s3, s1, s0, k2, k3, k1, k0])
        pieces = lax.psum(pieces, ("z", "y"))
        proj_grad = None
        for x_off, held in ((0, pieces), (1, swap(pieces, "x"))):
            own = [(r, 0, r, x_off, 0) for r in range(8)]
            proj_grad, give = place(sel, list(held), own, proj_grad, width, 8)
            other = given(0, own, part)
            (proj_grad,) = place(sel, [swap(give, "c")], other, proj_grad, width, 0)
        output, input_grad = join(sel, kept, got)
    small = [small[i].reshape(width) for i in range(6)]
    return (output[None], input_grad[None], proj_grad, *small)


def solution(mesh):
    dp, rep = mesh.shape["dp"], mesh.shape["rep"]
    fine = Mesh(mesh.devices.reshape(dp // 2, 2, rep // 2, 2), ("z", "y", "x", "c"))
    row, seq = ("z", "y"), ("x", "c")
    in_specs = (P(row, seq, None), P(row, None)) + (P(),) * 7 + (P(row, seq, None),)
    out_specs = (P(row, seq, None), P(row, seq, None)) + (P(),) * 7
    return jax.shard_map(
        on_device, mesh=fine, in_specs=in_specs, out_specs=out_specs, check_vma=False
    )
```

```python
import functools

import jax
import jax.numpy as jnp
from jax import lax
from jax.experimental import pallas as pl
from jax.experimental.pallas import tpu as pltpu
from jax.sharding import Mesh
from jax.sharding import PartitionSpec as P

EPS = 1e-05
SWAP = [(0, 1), (1, 0)]
VMEM_BYTES = 56 * 2**20
F32 = jnp.float32
BF16 = jnp.bfloat16


def swap(block, axis):
    return lax.ppermute(block, axis, SWAP)


def xor_permute(block, axis, distance):
    size = lax.axis_size(axis)
    return lax.ppermute(block, axis, [(i, i ^ distance) for i in range(size)])


def any_spec():
    return pl.BlockSpec(memory_space=pl.ANY)


def hbm():
    return pl.BlockSpec(memory_space=pltpu.HBM)


def vmem():
    return pl.BlockSpec(memory_space=pltpu.VMEM)


def smem():
    return pl.BlockSpec(memory_space=pltpu.SMEM)


def shaped(shape, dtype=F32):
    return jax.ShapeDtypeStruct(shape, dtype)


def params(mib):
    return pltpu.CompilerParams(vmem_limit_bytes=mib * 2**20)


def cost(us):
    return pl.CostEstimate(
        flops=int(us * 1.1e9), bytes_accessed=int(us * 3.6e6), transcendentals=0
    )


def own_columns(sel, cols):
    return pl.ds(pl.multiple_of((2 * sel[0] + sel[1]) * cols, cols), cols)


def stored_at(sel, k):
    return 2 * ((k // 2) ^ sel[0]) + ((k % 2) ^ sel[1])


def row_part(sel, row):
    return row if isinstance(row, int) else 2 * (sel[3] ^ row[0]) + (sel[2] ^ row[1])


def tick_kernel(*refs):
    refs[-1][...] = jnp.zeros(refs[-1].shape, F32)


def tick(*values):
    return pl.pallas_call(
        tick_kernel,
        out_shape=shaped((8, 128)),
        in_specs=[any_spec()] * len(values),
        out_specs=vmem(),
        compiler_params=params(1),
        cost_estimate=cost(20),
        name="tick",
    )(*values)


def hold_kernel(*refs):
    del refs


def hold(values, *waits):
    count = len(values)
    return pl.pallas_call(
        hold_kernel,
        out_shape=tuple(shaped(v.shape, v.dtype) for v in values),
        in_specs=[any_spec()] * (count + len(waits)),
        out_specs=(any_spec(),) * count,
        input_output_aliases={i: i for i in range(count)},
        compiler_params=params(1),
        cost_estimate=cost(0.05),
        name="hold",
    )(*values, *waits)


def add_kernel(a_ref, b_ref, *refs):
    refs[-1][...] = a_ref[...] + b_ref[...]


def add(a, b, *waits):
    return pl.pallas_call(
        add_kernel,
        out_shape=shaped(a.shape),
        in_specs=[vmem()] * 2 + [any_spec()] * len(waits),
        out_specs=vmem(),
        compiler_params=params(4),
        cost_estimate=cost(0.05),
        name="add",
    )(a, b, *waits)


def take_weights_kernel(sel, w_ref, mine_ref, sem):
    width, cols = mine_ref.shape[0], mine_ref.shape[1] // 3
    copies = []
    for k in range(3):
        at = pl.multiple_of((2 * sel[0] + sel[1]) * cols + k * width, cols)
        copies.append(
            pltpu.make_async_copy(
                w_ref.at[:, pl.ds(at, cols)], mine_ref.at[:, k * cols : (k + 1) * cols], sem.at[k]
            )
        )
    for c in copies:
        c.start()
    for c in copies:
        c.wait()


def take_weights(sel, w_proj):
    width = w_proj.shape[0]
    return pl.pallas_call(
        take_weights_kernel,
        out_shape=shaped((width, 3 * width // 4), BF16),
        in_specs=[smem(), hbm()],
        out_specs=vmem(),
        scratch_shapes=[pltpu.SemaphoreType.DMA((3,))],
        compiler_params=params(4),
        cost_estimate=cost(0.05),
        name="take_weights",
    )(sel, w_proj)


def widen_cot_kernel(sel, cot_ref, cot_out):
    cols = cot_ref.shape[1] // 4
    for k in range(2):
        at = pl.multiple_of((2 * k + 1 - sel[1]) * cols, cols)
        cot_out[:, k * cols : (k + 1) * cols] = cot_ref[:, pl.ds(at, cols)].astype(F32)


def widen_cot(sel, cot):
    return pl.pallas_call(
        widen_cot_kernel,
        out_shape=shaped((cot.shape[0], cot.shape[1] // 2)),
        in_specs=[smem(), vmem()],
        out_specs=vmem(),
        compiler_params=params(4),
        cost_estimate=cost(0.05),
        name="widen_cot",
    )(sel, cot)


def pack_cot_kernel(sel, cot_ref, sibling_ref, cot_out):
    block, cols = cot_ref.shape[0], cot_ref.shape[1] // 4
    mine = pl.multiple_of((2 * (1 - sel[0]) + sel[1]) * cols, cols)
    cot_out[0:block, :] = cot_ref[:, pl.ds(mine, cols)].astype(F32)
    sibling = pl.multiple_of((1 - sel[0]) * cols, cols)
    cot_out[block:, :] = sibling_ref[:, pl.ds(sibling, cols)]


def pack_cot(sel, cot, sibling):
    return pl.pallas_call(
        pack_cot_kernel,
        out_shape=shaped((2 * cot.shape[0], cot.shape[1] // 4)),
        in_specs=[smem(), vmem(), vmem()],
        out_specs=vmem(),
        compiler_params=params(4),
        cost_estimate=cost(0.05),
        name="pack_cot",
    )(sel, cot, sibling)


def standardized(x):
    mean = jnp.mean(x, axis=-1, keepdims=True)
    centred = x - mean
    rdev = lax.rsqrt(jnp.mean(centred * centred, axis=-1, keepdims=True) + EPS)
    return centred * rdev, rdev


def norm_and_project(sel, toks, norm, w_ref, gates, normed, cand, zf, zr, base):
    cols = cand.shape[1]
    mine = own_columns(sel, cols)
    gain, bias = norm[0][...], norm[1][...]
    fb, rb = gates[2][:, mine], gates[3][:, mine]
    block = toks[0].shape[0]
    step = 16
    for at, tok in enumerate(toks):

        def body(i, carry, tok=tok, at=at):
            here = pl.ds(pl.multiple_of(i * step, step), step)
            there = pl.ds(pl.multiple_of(at * block + i * step, step), step)
            xhat, _ = standardized(tok[here, :])
            normed[there, :] = (xhat * gain + bias).astype(BF16)
            return carry

        lax.fori_loop(0, block // step, body, 0, unroll=True)
    rows = normed[...]
    here = slice(base, base + 2 * block)
    part = lambda k: jnp.dot(
        rows, w_ref[:, k * cols : (k + 1) * cols], preferred_element_type=F32
    )
    cand[here, :] = part(0)
    zf[here, :] = 0.5 * (part(1) + fb)
    zr[here, :] = 0.5 * (part(2) + rb)


def near_kernel(sel, offsets, tok0, tok1, w_ref, *refs):
    gates, norm, (normed, cand, zf, zr, half_keep) = refs[:4], refs[4:6], refs[6:]
    length, cols = half_keep.shape
    block = length // 4
    step = 16
    for b in range(4):
        base = stored_at(sel, b) * block

        def body(i, carry, b=b, base=base):
            at = pl.multiple_of(i * step, step)
            token = base + at + lax.broadcasted_iota(jnp.int32, (step, cols), 0)
            starts = token == offsets[0, 0]
            for k in range(1, offsets.shape[1]):
                starts = starts | (token == offsets[0, k])
            here = pl.ds(pl.multiple_of(b * block + at, step), step)
            half_keep[here, :] = jnp.where(starts, 0.0, 0.5)
            return carry

        lax.fori_loop(0, block // step, body, 0)
    norm_and_project(sel, (tok0, tok1), norm, w_ref, gates, normed, cand, zf, zr, 0)


def run_near(sel, offsets, toks, w_mine, vectors):
    block, width = toks[0].shape
    cols = width // 4
    return pl.pallas_call(
        near_kernel,
        out_shape=(shaped((2 * block, width), BF16),)
        + (shaped((2 * block, cols)),) * 3
        + (shaped((4 * block, cols)),),
        in_specs=[smem()] * 2 + [vmem()] * 9,
        out_specs=(vmem(),) * 5,
        compiler_params=params(16),
        cost_estimate=cost(0.05),
        name="near_blocks",
    )(sel, offsets, *toks, w_mine, *vectors)


def forward_kernel(sel, tok0, tok1, cand_near, zf_near, zr_near, half_keep, w_ref, *refs):
    gates, norm, (normed, cand, zf, zr, state, half_prev) = refs[:4], refs[4:6], refs[6:]
    length, cols = cand.shape
    block = length // 4
    near = slice(0, 2 * block)
    cand[near, :], zf[near, :], zr[near, :] = cand_near[...], zf_near[...], zr_near[...]
    fw = gates[0][:, own_columns(sel, cols)]
    norm_and_project(sel, (tok0, tok1), norm, w_ref, gates, normed, cand, zf, zr, 2 * block)
    c = jnp.zeros((1, cols), F32)
    for k in range(4):
        base = stored_at(sel, k) * block

        def body(i, c, base=base):
            row = pl.ds(base + i, 1)
            half = half_keep[row, :]
            th = jnp.tanh(zf[row, :] + (half * fw) * c)
            hp = half * c
            hc = 0.5 * cand[row, :]
            c = (hp + hc) + (hp - hc) * th
            state[row, :] = c
            half_prev[row, :] = hp
            return c

        c = lax.fori_loop(0, block, body, c, unroll=16)


def run_forward(sel, toks, near, w_mine, vectors):
    block, width = toks[0].shape
    cols = width // 4
    length = 4 * block
    return pl.pallas_call(
        forward_kernel,
        out_shape=(shaped((2 * block, width), BF16),) + (shaped((length, cols)),) * 5,
        in_specs=[smem()] + [vmem()] * 13,
        out_specs=(vmem(),) * 6,
        compiler_params=params(20),
        cost_estimate=cost(0.05),
        name="forward_scan",
    )(sel, *toks, *near, w_mine, *vectors)


def backward_kernel(
    sel,
    x0,
    x1,
    x2,
    x3,
    g0,
    g1,
    g23,
    cand_ref,
    zf_ref,
    zr_ref,
    state,
    half_prev,
    half_keep,
    fw_ref,
    rw_ref,
    near_ref,
    far_ref,
    dproj_ref,
    out_ref,
    dxh_ref,
    small_ref,
    *refs,
    rows,
):
    products, (coef, add_b, add_e, gz, omf) = refs[: len(rows)], refs[len(rows) :]
    length, cols = cand_ref.shape
    block = length // 4
    mine = own_columns(sel, cols)
    half = pl.ds(pl.multiple_of(sel[0] * cols, cols), cols)
    fw, rw = fw_ref[:, mine], rw_ref[:, mine]
    half_fw, half_rw = 0.5 * fw, 0.5 * rw
    step = 16
    zero = jnp.zeros((step, cols), F32)
    sums = (zero, zero)
    everything = slice(0, cols)
    sources = (
        (x0, g0, 0, mine),
        (x1, g1, 0, half),
        (x2, g23, 0, everything),
        (x3, g23, block, everything),
    )
    for b, (x_ref, g_ref, g_at, g_cols) in enumerate(sources):

        def gate_body(i, carry, b=b, x_ref=x_ref, g_ref=g_ref, g_at=g_at, g_cols=g_cols):
            at = pl.multiple_of(i * step, step)
            here = pl.ds(pl.multiple_of(b * block + at, step), step)
            x = x_ref[pl.ds(at, step), mine]
            g = g_ref[pl.ds(pl.multiple_of(g_at + at, step), step), g_cols].astype(F32)
            keep = 2.0 * half_keep[here, :]
            prev = 2.0 * half_prev[here, :]
            c, cd = state[here, :], cand_ref[here, :]
            forget = 0.5 + 0.5 * jnp.tanh(zf_ref[here, :] + half_fw * prev)
            reset = 0.5 + 0.5 * jnp.tanh(zr_ref[here, :] + half_rw * prev)
            not_forget, not_reset = 1.0 - forget, 1.0 - reset
            out_ref[here, :] = reset * c + not_reset * x
            dxh_ref[here, :] = g * not_reset
            dzr = g * (c - x) * reset * not_reset
            slope = (prev - cd) * forget * not_forget
            coef[here, :] = keep * (forget + slope * fw)
            add_b[here, :] = keep * (dzr * rw)
            add_e[here, :] = g * reset
            gz[here, :] = slope
            omf[here, :] = not_forget
            dproj_ref[here, 2 * cols : 3 * cols] = dzr.astype(BF16)
            return (carry[0] + dzr * prev, carry[1] + dzr)

        sums = lax.fori_loop(0, block // step, gate_body, sums, unroll=True)
    rw_sum, rb_sum = sums

    s = jnp.zeros((1, cols), F32)
    for k in range(3, -1, -1):
        last = stored_at(sel, k) * block + block - 1

        def backward_body(i, s, last=last):
            row = pl.ds(last - i, 1)
            total = s + add_e[row, :]
            add_e[row, :] = total
            return coef[row, :] * total + add_b[row, :]

        s = lax.fori_loop(0, block, backward_body, s, unroll=16)

    def grad_body(i, carry):
        here = pl.ds(pl.multiple_of(i * step, step), step)
        total = add_e[here, :]
        prev = 2.0 * half_prev[here, :]
        dzf = total * gz[here, :]
        dproj_ref[here, 0:cols] = (total * omf[here, :]).astype(BF16)
        dproj_ref[here, cols : 2 * cols] = dzf.astype(BF16)
        return (carry[0] + dzf * prev, carry[1] + dzf)

    fw_sum, fb_sum = lax.fori_loop(0, length // step, grad_body, (zero, zero), unroll=4)
    small_ref[...] = jnp.concatenate(
        [jnp.sum(v, axis=0, keepdims=True) for v in (fw_sum, rw_sum, fb_sum, rb_sum)]
        + [jnp.zeros((4, cols), F32)],
        axis=0,
    )
    outer_products(sel, rows, near_ref, far_ref, dproj_ref, products)


def outer_products(sel, rows, near_ref, far_ref, dproj_ref, outs):
    half, width = near_ref.shape
    part = width // 8
    dims = (((0,), (0,)), ((), ()))
    for out, places in zip(outs, rows):
        for k, place_of in enumerate(places):
            at = pl.ds(pl.multiple_of(row_part(sel, place_of) * part, part), part)
            out[k * part : (k + 1) * part, :] = lax.dot_general(
                near_ref[:, at], dproj_ref[0:half, :], dims, preferred_element_type=F32
            ) + lax.dot_general(
                far_ref[:, at], dproj_ref[half:, :], dims, preferred_element_type=F32
            )


def product_shapes(width, rows):
    return tuple(shaped((len(places) * width // 8, 3 * width // 4)) for places in rows)


def run_backward(sel, toks, cots, scanned, half_keep, gates, normed, rows):
    block, width = toks[0].shape
    cols = width // 4
    length = 4 * block
    return pl.pallas_call(
        functools.partial(backward_kernel, rows=rows),
        out_shape=(
            shaped((length, 3 * cols), BF16),
            shaped((length, cols)),
            shaped((length, cols)),
            shaped((8, cols)),
        )
        + product_shapes(width, rows),
        in_specs=[smem()] + [vmem()] * 17,
        out_specs=(vmem(),) * (4 + len(rows)),
        scratch_shapes=[pltpu.VMEM((length, cols), F32)] * 5,
        compiler_params=params(24),
        cost_estimate=cost(0.05),
        name="backward_scan",
    )(sel, *toks, *cots, *scanned, half_keep, *gates[:2], *normed)


def products_kernel(sel, near_ref, far_ref, dproj_ref, *outs, rows):
    outer_products(sel, rows, near_ref, far_ref, dproj_ref, outs)


def run_products(sel, normed, dproj, rows):
    return pl.pallas_call(
        functools.partial(products_kernel, rows=rows),
        out_shape=product_shapes(normed[0].shape[1], rows),
        in_specs=[smem()] + [vmem()] * 3,
        out_specs=(vmem(),) * len(rows),
        compiler_params=params(12),
        cost_estimate=cost(0.05),
        name="products",
    )(sel, *normed, dproj)


def input_kernel(
    sel,
    tok0,
    tok1,
    tok2,
    tok3,
    dproj_ref,
    dxh_ref,
    out_ref,
    gate_small_ref,
    w_ref,
    gain_ref,
    *refs,
):
    mine_ref, send_ref, dnormed = refs[-3:]
    cols = dxh_ref.shape[1]
    block, width = tok0.shape
    gain = gain_ref[...]
    mine = own_columns(sel, cols)
    step = 8
    sums = (jnp.zeros((step, width), F32), jnp.zeros((step, width), F32))
    for b, tok in enumerate((tok0, tok1, tok2, tok3)):
        rows = slice(b * block, (b + 1) * block)
        dnormed[...] = lax.dot_general(
            dproj_ref[rows, :], w_ref[...], (((1,), (1,)), ((), ())), preferred_element_type=F32
        )
        where = send_ref if b % 2 else mine_ref
        base = (b // 2) * block

        def body(i, carry, tok=tok, base=base, where=where):
            here = pl.ds(pl.multiple_of(i * step, step), step)
            there = pl.ds(pl.multiple_of(base + i * step, step), step)
            xhat, rdev = standardized(tok[here, :])
            dn = dnormed[here, :]
            dxhat = dn * gain
            mean1 = jnp.mean(dxhat, axis=-1, keepdims=True)
            mean2 = jnp.mean(dxhat * xhat, axis=-1, keepdims=True)
            where[there, 0:width] = rdev * (dxhat - mean1 - xhat * mean2)
            return (carry[0] + dn * xhat, carry[1] + dn)

        sums = lax.fori_loop(0, block // step, body, sums, unroll=11)
        to = pl.ds(base, block)
        where[to, mine] += dxh_ref[rows, :]
        where[to, width : width + cols] = out_ref[rows, :]
    tail = slice(2 * block, 2 * block + 8)
    mine_ref[tail, :] = jnp.zeros((8, width + cols), F32)
    mine_ref[2 * block : 2 * block + 4, mine] = gate_small_ref[0:4, :]
    for i, v in enumerate(sums):
        row = 2 * block + 4 + i
        mine_ref[row : row + 1, 0:width] = jnp.sum(v, axis=0, keepdims=True)
    send_ref[tail, :] = mine_ref[tail, :]


def run_input(sel, toks, dproj, dxh, out, gate_small, w_mine, gain, *waits):
    block, width = toks[0].shape
    shape = (2 * block + 8, width + width // 4)
    return pl.pallas_call(
        input_kernel,
        out_shape=(shaped(shape), shaped(shape)),
        in_specs=[smem()] + [vmem()] * 10 + [any_spec()] * len(waits),
        out_specs=(vmem(),) * 2,
        scratch_shapes=[pltpu.VMEM((block, width), F32)],
        compiler_params=params(20),
        cost_estimate=cost(0.05),
        name="input_side",
    )(sel, *toks, dproj, dxh, out, gate_small, w_mine, gain, *waits)


def combine_kernel(sel, mine_ref, got_ref, *refs):
    keep_ref, send_ref, small_ref = refs[-3:]
    block, width = keep_ref.shape[0], small_ref.shape[1]
    cols = width // 4
    low = pl.ds(pl.multiple_of(width + sel[1] * cols, cols), cols)
    high = pl.ds(pl.multiple_of(width + (1 - sel[1]) * cols, cols), cols)
    for ref, first in ((keep_ref, 0), (send_ref, block)):
        here = slice(first, first + block)
        ref[:, 0:width] = mine_ref[here, 0:width] + got_ref[here, 0:width]
        ref[:, low] = mine_ref[here, width:]
        ref[:, high] = got_ref[here, width:]
    small_ref[...] = mine_ref[2 * block :, 0:width] + got_ref[2 * block :, 0:width]


def combine(sel, mine, got, *waits):
    block, width = (mine.shape[0] - 8) // 2, mine.shape[1] * 4 // 5
    return pl.pallas_call(
        combine_kernel,
        out_shape=(shaped((block, width * 3 // 2)),) * 2 + (shaped((8, width)),),
        in_specs=[smem(), vmem(), vmem()] + [any_spec()] * len(waits),
        out_specs=(vmem(),) * 3,
        compiler_params=params(16),
        cost_estimate=cost(0.05),
        name="combine",
    )(sel, mine, got, *waits)


def join_kernel(sel, mine_ref, got_ref, out_ref, grad_ref):
    width = out_ref.shape[1]
    half = width // 2
    at = pl.multiple_of(sel[0] * half, half)
    other = pl.multiple_of((1 - sel[0]) * half, half)
    out_ref[:, pl.ds(at, half)] = mine_ref[:, width:].astype(BF16)
    out_ref[:, pl.ds(other, half)] = got_ref[:, width:].astype(BF16)
    grad_ref[...] = (mine_ref[:, 0:width] + got_ref[:, 0:width]).astype(BF16)


def join(sel, mine, got):
    block, width = mine.shape[0], mine.shape[1] * 2 // 3
    return pl.pallas_call(
        join_kernel,
        out_shape=(shaped((block, width), BF16),) * 2,
        in_specs=[smem()] + [vmem()] * 2,
        out_specs=(vmem(),) * 2,
        compiler_params=params(16),
        cost_estimate=cost(0.05),
        name="join",
    )(sel, mine, got)


def fold_small(small):
    rows, cols = 6, small.shape[1] // 4
    tails = [small[i : i + 1, 3 * cols :] for i in range(rows)]
    last = [jnp.concatenate(tails[:3], axis=1), jnp.concatenate(tails[3:], axis=1)]
    return jnp.concatenate([small[0:rows, : 3 * cols]] + last, axis=0)


def finish_kernel(keep_ref, got_ref, a1_ref, a3_ref, small_ref, total_ref):
    part = keep_ref.shape[0]
    total_ref[0:part, :] = keep_ref[...] + got_ref[...] + a1_ref[...] + a3_ref[...]
    total_ref[part:, :] = fold_small(small_ref[...])


def finish(keep, got, a1, a3, small):
    part, cols3 = keep.shape
    return pl.pallas_call(
        finish_kernel,
        out_shape=shaped((part + 8, cols3)),
        in_specs=[vmem()] * 5,
        out_specs=vmem(),
        compiler_params=params(8),
        cost_estimate=cost(0.05),
        name="finish",
    )(keep, got, a1, a3, small)


def stack_kernel(*refs, rows):
    at = 0
    for ref, (first, count) in zip(refs, rows):
        refs[-1][at : at + count, :] = ref[first : first + count, :]
        at += count


def stack(*parts):
    rows = tuple((first, count) for _, first, count in parts)
    return pl.pallas_call(
        functools.partial(stack_kernel, rows=rows),
        out_shape=shaped((sum(count for _, count in rows), parts[0][0].shape[1])),
        in_specs=[vmem()] * len(parts),
        out_specs=vmem(),
        compiler_params=params(6),
        cost_estimate=cost(0.05),
        name="stack",
    )(*(array for array, _, _ in parts))


def small_kernel(*refs, where):
    pieces, outs = refs[:-6], refs[-6:]
    sums = [pieces[i][at : at + 8, :] for i, at in where]
    while len(sums) > 1:
        sums = [a + b for a, b in zip(sums[::2], sums[1::2])]
    total = sums[0]
    cols = total.shape[1] // 3
    for i, out in enumerate(outs):
        out[:, 0 : 3 * cols] = total[i : i + 1, :]
        out[:, 3 * cols :] = total[6 + i // 3 : 7 + i // 3, (i % 3) * cols : (i % 3 + 1) * cols]


def small_sums(pieces, where):
    width = pieces[0].shape[1] // 3 * 4
    return pl.pallas_call(
        functools.partial(small_kernel, where=where),
        out_shape=(shaped((1, width)),) * 6,
        in_specs=[vmem()] * len(pieces),
        out_specs=(vmem(),) * 6,
        compiler_params=params(8),
        cost_estimate=cost(0.05),
        name="small_sums",
    )(*pieces)


def place_kernel(sel, *refs, where, give):
    target, sem = refs[-2 - bool(give)], refs[-1]
    cols = refs[0].shape[1] // 3
    width = target.shape[1] // 3
    part = width // 8
    copies = []

    def copy(src, dst):
        copies.append(pltpu.make_async_copy(src, dst, sem.at[len(copies)]))
        copies[-1].start()

    for at, (array, first, rows, row, row_off, x_off, c_off) in enumerate(where):
        piece = refs[array].at[pl.ds(first, rows)]
        to_row = pl.multiple_of(row_part(sel, row) * part + row_off, 8)
        col = (2 * (sel[0] ^ x_off) + (sel[1] ^ c_off)) * cols
        for k in range(3):
            to = pl.multiple_of(col + k * width, cols)
            copy(piece.at[:, pl.ds(k * cols, cols)], target.at[pl.ds(to_row, rows), pl.ds(to, cols)])
        if at < give:
            copy(piece, refs[-2].at[pl.ds(at * part, part)])
    for c in copies:
        c.wait()


def place(sel, arrays, where, target, width, give, *waits):
    count = len(arrays)
    extra = [] if target is None else [target]
    cols3 = 3 * width // 4
    return pl.pallas_call(
        functools.partial(place_kernel, where=where, give=give),
        out_shape=(shaped((width, 3 * width)),)
        + ((shaped((give * width // 8, cols3)),) if give else ()),
        in_specs=[smem()]
        + [vmem()] * count
        + [hbm()] * len(extra)
        + [any_spec()] * len(waits),
        out_specs=(hbm(), vmem()) if give else (hbm(),),
        scratch_shapes=[pltpu.SemaphoreType.DMA((3 * len(where) + give,))],
        input_output_aliases={1 + count: 0} if extra else {},
        compiler_params=params(8),
        cost_estimate=cost(0.05),
        name="place",
    )(sel, *arrays, *extra, *waits)


def given(array, where):
    return [
        (array, i * rows, rows, row, row_off, x_off, 1)
        for i, (_, _, rows, row, row_off, x_off, _) in enumerate(where)
    ]


def on_device(
    tokens,
    offsets,
    w_proj,
    forget_weight,
    reset_weight,
    forget_bias,
    reset_bias,
    layer_norm_gain,
    layer_norm_bias,
    cotangent,
):
    _, block, width = tokens.shape
    z, y, x, c = (lax.axis_index(a) for a in ("z", "y", "x", "c"))
    tuned = lax.axis_size("z") == 4
    sel = jnp.stack([x, c, y, z]).astype(jnp.int32)
    part = width // 8

    cot = cotangent[0]
    own = lax.optimization_barrier(tokens[0].astype(F32))
    tok_x = swap(own, "x")
    tok_c = swap(own, "c")
    cot_sibling = swap(widen_cot(sel, cot), "c")
    cot_packed = pack_cot(sel, cot, cot_sibling)
    cot_far = swap(cot_packed, "x")

    gates = [
        v.reshape(1, width) for v in (forget_weight, reset_weight, forget_bias, reset_bias)
    ]
    gain = layer_norm_gain.reshape(1, width)
    vectors = (*gates, gain, layer_norm_bias.reshape(1, width))
    w_mine = take_weights(sel, w_proj)
    near = run_near(sel, offsets, (own, tok_c), w_mine, vectors)
    (tok_x,) = hold((tok_x,), near[4], cot_packed)
    tok_xc = swap(tok_x, "c")
    far = run_forward(sel, (tok_x, tok_xc), near[1:], w_mine, vectors)
    normed = (near[0], far[0])
    toks = (own, tok_c, tok_x, tok_xc)
    if tuned:
        rows = [[[(d, 1)] for d in (2, 3, 1, 0)], [[(d, 0)] for d in (2, 3, 1, 0)]]
    else:
        rows = [[[0], [1], [2], [3]], [[4], [5], [6], [7]]]
    dproj, out, dxh, gate_small, s2 = run_backward(
        sel, toks, (cot, cot_sibling, cot_far), far[1:], near[4], gates, normed, rows[0][:1]
    )
    s3, s1, s0 = run_products(sel, normed, dproj, rows[0][1:])
    k2, k3, k1, k0 = run_products(sel, normed, dproj, rows[1])
    input_side = lambda *waits: run_input(
        sel, toks, dproj, dxh, out, gate_small, w_mine, gain, *waits
    )

    if tuned:
        r2, r3, r1, r0 = (swap(piece, "y") for piece in (s2, s3, s1, s0))
        grad_mine, grad_send = input_side()
        q2 = add(k2, r2, s0, grad_send)
        a2 = xor_permute(q2, "z", 1)
        h3 = add(add(k3, r3), a2)
        a3 = xor_permute(h3, "z", 3)
        kept, sent, small = combine(
            sel, grad_mine, swap(grad_send, "c"), q2, tick(grad_send)
        )
        got = swap(sent, "x")
        a1 = xor_permute(add(k1, r1, sent), "z", 1)
        total = finish(k0, r0, a1, a3, small)
        output, input_grad = join(sel, kept, got)

        z3, px0, py0 = xor_permute(total, "z", 3), swap(total, "x"), swap(total, "y")
        z1 = xor_permute(total, "z", 1)
        (px0,) = hold((px0,), input_grad)
        corner0 = swap(px0, "y")
        z3, z1, corner0, py0 = hold((z3, z1, corner0, py0))
        full = part + 8
        z13 = stack((z1, 0, full), (z3, 0, full))
        z2, px13, py13 = xor_permute(z3, "z", 1), swap(z13, "x"), swap(z13, "y")
        corner3 = xor_permute(corner0, "z", 3)
        own = [
            (0, 0, part, (0, 0), 0, 0, 0),
            (1, 0, part, (0, 0), 0, 1, 0),
            (2, 0, part, (0, 1), 0, 0, 0),
            (3, 0, part, (0, 1), 0, 1, 0),
        ]
        proj_grad, give = place(sel, (total, px0, py0, corner0), own, None, width, 4)
        z2, px13, py13, corner3 = hold((z2, px13, py13, corner3), give)
        third = 3 * part // 8
        rest = full - 2 * third
        px2 = swap(stack((z2, 0, full), (py13, 0, third)), "x")
        py2 = swap(stack((z2, 0, full), (px13, third, third)), "y")
        corner12 = xor_permute(stack((corner3, 0, full), (corner0, 2 * third, rest)), "z", 1)
        other = given(3, own)
        own = [
            (array, full * i, part, (d, y_off), 0, x_off, 0)
            for array, y_off, x_off in ((0, 0, 0), (1, 0, 1), (2, 1, 0))
            for i, d in ((0, 1), (1, 3))
        ]
        proj_grad, give = place(
            sel,
            (z13, px13, py13, swap(give, "c")),
            own + other,
            proj_grad,
            width,
            6,
            tick(give),
        )
        other = given(3, own)
        first_give, wait = swap(give, "c"), tick(give)
        own = [(0, 0, part, (2, 0), 0, 0, 0), (1, 0, part, (3, 1), 0, 1, 0)]
        proj_grad, give = place(sel, (z2, corner3), own, proj_grad, width, 2)
        other += given(4, own)
        px2, py2, corner12 = hold((px2, py2, corner12), give)
        own = [
            (0, 0, part, (2, 0), 0, 1, 0),
            (0, full, third, (1, 1), 0, 1, 0),
            (1, 0, part, (2, 1), 0, 0, 0),
            (1, full, third, (1, 1), third, 1, 0),
            (2, 0, part, (2, 1), 0, 1, 0),
            (2, full, rest - 8, (1, 1), 2 * third, 1, 0),
        ]
        arrays = (px2, py2, corner12, first_give, swap(give, "c"))
        (proj_grad,) = place(sel, arrays, own + other, proj_grad, width, 0, wait, tick(give))
        own = [(*place_of[:-1], 1) for place_of in own]
        arrays = [swap(a, "c") for a in (px2, py2, corner12)]
        (proj_grad,) = place(sel, arrays, own, proj_grad, width, 0)
        where = [(0, part), (1, part), (2, part), (3, part)]
        where += [(4, part), (5, part), (6, part), (9, full + rest - 8)]
        where += [(8, part), (7, part), (10, part), (9, part)]
        where += [(array, full + part) for array in (4, 5, 6)] + [(11, part)]
        arrays = (total, px0, py0, corner0, z13, px13, py13, px2, z2, corner12, py2, corner3)
        small = small_sums(arrays, where)
    else:
        grad_mine, grad_send = input_side()
        kept, sent, small = combine(sel, grad_mine, swap(grad_send, "c"))
        got = swap(sent, "x")
        small = lax.psum(small + swap(small, "x"), ("z", "y"))
        pieces = jnp.stack([s2, s3, s1, s0, k2, k3, k1, k0])
        pieces = lax.psum(pieces, ("z", "y"))
        proj_grad = None
        for x_off, held in ((0, pieces), (1, swap(pieces, "x"))):
            own = [(r, 0, part, r, 0, x_off, 0) for r in range(8)]
            proj_grad, give = place(sel, list(held), own, proj_grad, width, 8)
            other = given(0, own)
            (proj_grad,) = place(sel, [swap(give, "c")], other, proj_grad, width, 0)
        output, input_grad = join(sel, kept, got)
    small = [small[i].reshape(width) for i in range(6)]
    return (output[None], input_grad[None], proj_grad, *small)


def solution(mesh):
    dp, rep = mesh.shape["dp"], mesh.shape["rep"]
    fine = Mesh(mesh.devices.reshape(dp // 2, 2, rep // 2, 2), ("z", "y", "x", "c"))
    row, seq = ("z", "y"), ("x", "c")
    in_specs = (P(row, seq, None), P(row, None)) + (P(),) * 7 + (P(row, seq, None),)
    out_specs = (P(row, seq, None), P(row, seq, None)) + (P(),) * 7
    return jax.shard_map(
        on_device, mesh=fine, in_specs=in_specs, out_specs=out_specs, check_vma=False
    )
```

```python
import functools

import jax
import jax.numpy as jnp
from jax import lax
from jax.experimental import pallas as pl
from jax.experimental.pallas import tpu as pltpu
from jax.sharding import Mesh
from jax.sharding import PartitionSpec as P

EPS = 1e-05
LANES = 128
SWAP = [(0, 1), (1, 0)]
VMEM_BYTES = 56 * 2**20
F32 = jnp.float32
BF16 = jnp.bfloat16


def swap(block, axis):
    return lax.ppermute(block, axis, SWAP)


def xor_permute(block, axis, distance):
    size = lax.axis_size(axis)
    return lax.ppermute(block, axis, [(i, i ^ distance) for i in range(size)])


def any_spec():
    return pl.BlockSpec(memory_space=pl.ANY)


def hbm():
    return pl.BlockSpec(memory_space=pltpu.HBM)


def vmem():
    return pl.BlockSpec(memory_space=pltpu.VMEM)


def smem():
    return pl.BlockSpec(memory_space=pltpu.SMEM)


def shaped(shape, dtype=F32):
    return jax.ShapeDtypeStruct(shape, dtype)


def params(mib):
    return pltpu.CompilerParams(vmem_limit_bytes=mib * 2**20)


def cost(us):
    return pl.CostEstimate(
        flops=int(us * 1.1e9), bytes_accessed=int(us * 3.6e6), transcendentals=0
    )


def own_columns(sel, cols):
    return pl.ds(pl.multiple_of((2 * sel[0] + sel[1]) * cols, cols), cols)


def stored_at(sel, k):
    return 2 * ((k // 2) ^ sel[0]) + ((k % 2) ^ sel[1])


def chunks(block):
    unit = block // 88 * 16
    sizes = (unit, 2 * unit, block - 3 * unit)
    return tuple((sum(sizes[:i]), size) for i, size in enumerate(sizes))


def segments(block):
    far = [(b, first, rows) for first, rows in chunks(block) for b in (2, 3)]
    return ((0, 0, block), (1, 0, block), *far)


def stretches(sel, block, k):
    held = stored_at(sel, k)
    near = held < 2
    return tuple(
        (jnp.where(near, held * block + first, 2 * (block + first) + (held - 2) * rows), rows)
        for first, rows in chunks(block)
    )


def row_part(sel, row):
    return row if isinstance(row, int) else 2 * (sel[3] ^ row[0]) + (sel[2] ^ row[1])


def tick_kernel(*refs):
    refs[-1][...] = jnp.zeros(refs[-1].shape, F32)


def tick(*values):
    return pl.pallas_call(
        tick_kernel,
        out_shape=shaped((8, 128)),
        in_specs=[any_spec()] * len(values),
        out_specs=vmem(),
        compiler_params=params(1),
        cost_estimate=cost(20),
        name="tick",
    )(*values)


def hold_kernel(*refs):
    del refs


def hold(values, *waits):
    count = len(values)
    return pl.pallas_call(
        hold_kernel,
        out_shape=tuple(shaped(v.shape, v.dtype) for v in values),
        in_specs=[any_spec()] * (count + len(waits)),
        out_specs=(any_spec(),) * count,
        input_output_aliases={i: i for i in range(count)},
        compiler_params=params(1),
        cost_estimate=cost(0.05),
        name="hold",
    )(*values, *waits)


def add_kernel(a_ref, b_ref, *refs):
    refs[-1][...] = a_ref[...] + b_ref[...]


def add(a, b, *waits):
    return pl.pallas_call(
        add_kernel,
        out_shape=shaped(a.shape),
        in_specs=[vmem()] * 2 + [any_spec()] * len(waits),
        out_specs=vmem(),
        compiler_params=params(4),
        cost_estimate=cost(0.05),
        name="add",
    )(a, b, *waits)


def take_weights_kernel(sel, w_ref, mine_ref, sem):
    width, cols = mine_ref.shape[0], mine_ref.shape[1] // 3
    copies = []
    for k in range(3):
        at = pl.multiple_of((2 * sel[0] + sel[1]) * cols + k * width, cols)
        copies.append(
            pltpu.make_async_copy(
                w_ref.at[:, pl.ds(at, cols)], mine_ref.at[:, k * cols : (k + 1) * cols], sem.at[k]
            )
        )
    for c in copies:
        c.start()
    for c in copies:
        c.wait()


def take_weights(sel, w_proj):
    width = w_proj.shape[0]
    return pl.pallas_call(
        take_weights_kernel,
        out_shape=shaped((width, 3 * width // 4), BF16),
        in_specs=[smem(), hbm()],
        out_specs=vmem(),
        scratch_shapes=[pltpu.SemaphoreType.DMA((3,))],
        compiler_params=params(4),
        cost_estimate=cost(0.05),
        name="take_weights",
    )(sel, w_proj)


def widen_cot_kernel(sel, cot_ref, cot_out):
    cols = cot_ref.shape[1] // 4
    for k in range(2):
        at = pl.multiple_of((2 * k + 1 - sel[1]) * cols, cols)
        cot_out[:, k * cols : (k + 1) * cols] = cot_ref[:, pl.ds(at, cols)].astype(F32)


def widen_cot(sel, cot):
    return pl.pallas_call(
        widen_cot_kernel,
        out_shape=shaped((cot.shape[0], cot.shape[1] // 2)),
        in_specs=[smem(), vmem()],
        out_specs=vmem(),
        compiler_params=params(4),
        cost_estimate=cost(0.05),
        name="widen_cot",
    )(sel, cot)


def pack_cot_kernel(sel, cot_ref, sibling_ref, cot_out):
    block, cols = cot_ref.shape[0], cot_ref.shape[1] // 4
    mine = pl.multiple_of((2 * (1 - sel[0]) + sel[1]) * cols, cols)
    cot_out[0:block, :] = cot_ref[:, pl.ds(mine, cols)].astype(F32)
    sibling = pl.multiple_of((1 - sel[0]) * cols, cols)
    cot_out[block:, :] = sibling_ref[:, pl.ds(sibling, cols)]


def pack_cot(sel, cot, sibling):
    return pl.pallas_call(
        pack_cot_kernel,
        out_shape=shaped((2 * cot.shape[0], cot.shape[1] // 4)),
        in_specs=[smem(), vmem(), vmem()],
        out_specs=vmem(),
        compiler_params=params(4),
        cost_estimate=cost(0.05),
        name="pack_cot",
    )(sel, cot, sibling)


def standardized(x):
    mean = jnp.mean(x, axis=-1, keepdims=True)
    centred = x - mean
    rdev = lax.rsqrt(jnp.mean(centred * centred, axis=-1, keepdims=True) + EPS)
    return centred * rdev, mean, rdev


def norm_and_project(sel, toks, norm, w_ref, gates, normed, stats, cand, zf, zr, first, base):
    cols = cand.shape[1]
    mine = own_columns(sel, cols)
    gain, bias = norm[0][...], norm[1][...]
    fb, rb = gates[2][:, mine], gates[3][:, mine]
    step = 16
    at = first
    for tok in toks:

        def body(i, carry, tok=tok, at=at):
            here = pl.ds(pl.multiple_of(i * step, step), step)
            there = pl.ds(pl.multiple_of(at + i * step, step), step)
            xhat, mean, rdev = standardized(tok[here, :])
            normed[there, :] = (xhat * gain + bias).astype(BF16)
            stats[there, 0:LANES] = jnp.broadcast_to(mean, (step, LANES))
            stats[there, LANES:] = jnp.broadcast_to(rdev, (step, LANES))
            return carry

        lax.fori_loop(0, tok.shape[0] // step, body, 0, unroll=True)
        at += tok.shape[0]
    rows = normed[first:at, :]
    here = slice(base, base + at - first)
    part = lambda k: jnp.dot(
        rows, w_ref[:, k * cols : (k + 1) * cols], preferred_element_type=F32
    )
    cand[here, :] = part(0)
    zf[here, :] = 0.5 * (part(1) + fb)
    zr[here, :] = 0.5 * (part(2) + rb)


def near_kernel(sel, offsets, tok0, tok1, w_ref, *refs):
    gates, norm, (normed, stats, cand, zf, zr, half_keep) = refs[:4], refs[4:6], refs[6:]
    length, cols = half_keep.shape
    block = length // 4
    step = 16
    row = 0
    for b, first, rows in segments(block):
        base = stored_at(sel, b) * block + first

        def body(i, carry, row=row, base=base):
            at = pl.multiple_of(i * step, step)
            token = base + at + lax.broadcasted_iota(jnp.int32, (step, cols), 0)
            starts = token == offsets[0, 0]
            for k in range(1, offsets.shape[1]):
                starts = starts | (token == offsets[0, k])
            half_keep[pl.ds(pl.multiple_of(row + at, step), step), :] = jnp.where(starts, 0.0, 0.5)
            return carry

        lax.fori_loop(0, rows // step, body, 0)
        row += rows
    norm_and_project(sel, (tok0, tok1), norm, w_ref, gates, normed, stats, cand, zf, zr, 0, 0)


def run_near(sel, offsets, toks, w_mine, vectors):
    block, width = toks[0].shape
    cols = width // 4
    return pl.pallas_call(
        near_kernel,
        out_shape=(shaped((2 * block, width), BF16), shaped((2 * block, 2 * LANES)))
        + (shaped((2 * block, cols)),) * 3
        + (shaped((4 * block, cols)),),
        in_specs=[smem()] * 2 + [vmem()] * 9,
        out_specs=(vmem(),) * 6,
        compiler_params=params(16),
        cost_estimate=cost(0.05),
        name="near_blocks",
    )(sel, offsets, *toks, w_mine, *vectors)


def early_kernel(sel, *refs, count):
    toks, w_ref, refs = refs[:count], refs[count], refs[count + 1 :]
    gates, norm, (normed, stats, cand, zf, zr) = refs[:4], refs[4:6], refs[-5:]
    norm_and_project(sel, toks, norm, w_ref, gates, normed, stats, cand, zf, zr, 0, 0)


def run_early(sel, toks, w_mine, vectors):
    rows, width = sum(tok.shape[0] for tok in toks), toks[0].shape[1]
    cols = width // 4
    return pl.pallas_call(
        functools.partial(early_kernel, count=len(toks)),
        out_shape=(shaped((rows, width), BF16), shaped((rows, 2 * LANES)))
        + (shaped((rows, cols)),) * 3,
        in_specs=[smem()] + [vmem()] * (7 + len(toks)),
        out_specs=(vmem(),) * 5,
        compiler_params=params(12),
        cost_estimate=cost(0.05),
        name="early_blocks",
    )(sel, *toks, w_mine, *vectors)


def forward_kernel(
    sel,
    tok0,
    tok1,
    cand_near,
    zf_near,
    zr_near,
    half_keep,
    normed_early,
    stats_early,
    cand_early,
    zf_early,
    zr_early,
    w_ref,
    *refs,
):
    gates, norm, (normed, stats, cand, zf, zr, state, half_prev) = refs[:4], refs[4:6], refs[6:]
    length, cols = cand.shape
    block = length // 4
    early = normed_early.shape[0]
    normed[0:early, :] = normed_early[...]
    stats[0:early, :] = stats_early[...]
    first = 2 * block
    near, mid = slice(0, first), slice(first, first + early)
    cand[near, :], zf[near, :], zr[near, :] = cand_near[...], zf_near[...], zr_near[...]
    cand[mid, :], zf[mid, :], zr[mid, :] = cand_early[...], zf_early[...], zr_early[...]
    fw = gates[0][:, own_columns(sel, cols)]
    norm_and_project(
        sel, (tok0, tok1), norm, w_ref, gates, normed, stats, cand, zf, zr, early, first + early
    )
    zero = jnp.zeros((1, cols), F32)
    carry = (zero, zero, zero)
    for k in range(4):
        for base, rows in stretches(sel, block, k):

            def body(i, carry, base=base):
                middle, spread, th = carry
                row = pl.ds(base + i, 1)
                half = half_keep[row, :]
                weight = half * fw
                last = middle + spread * th
                th = jnp.tanh((zf[row, :] + weight * middle) + (weight * spread) * th)
                hp = half * last
                hc = 0.5 * cand[row, :]
                middle, spread = hp + hc, hp - hc
                state[row, :] = middle + spread * th
                half_prev[row, :] = hp
                return (middle, spread, th)

            carry = lax.fori_loop(0, rows, body, carry, unroll=16)


def run_forward(sel, toks, near, early, w_mine, vectors):
    late, width = toks[0].shape
    cols = width // 4
    length = near[-1].shape[0]
    return pl.pallas_call(
        forward_kernel,
        out_shape=(shaped((length // 2, width), BF16), shaped((length // 2, 2 * LANES)))
        + (shaped((length, cols)),) * 5,
        in_specs=[smem()] + [vmem()] * 18,
        out_specs=(vmem(),) * 7,
        compiler_params=params(20),
        cost_estimate=cost(0.05),
        name="forward_scan",
    )(sel, *toks, *near, *early, w_mine, *vectors)


def backward_kernel(sel, *refs, rows, count):
    toks, refs = refs[:count], refs[count:]
    (g0, g1, g23, cand_ref, zf_ref, zr_ref, state, half_prev), refs = refs[:8], refs[8:]
    (half_keep, fw_ref, rw_ref, near_ref, far_ref), refs = refs[:5], refs[5:]
    (dproj_ref, out_ref, dxh_ref, small_ref), refs = refs[:4], refs[4:]
    products, (coef, add, add_e, gz, omf, states) = refs[: len(rows)], refs[len(rows) :]
    length, cols = cand_ref.shape
    block = length // 4
    mine = own_columns(sel, cols)
    half = pl.ds(pl.multiple_of(sel[0] * cols, cols), cols)
    fw, rw = fw_ref[:, mine], rw_ref[:, mine]
    half_fw, half_rw = 0.5 * fw, 0.5 * rw
    step = 16
    zero = jnp.zeros((step, cols), F32)
    sums = (zero, zero)
    everything = slice(0, cols)
    grads = ((g0, 0, mine), (g1, 0, half), (g23, 0, everything), (g23, block, everything))
    row = 0
    for x_ref, (b, first, count) in zip(toks, segments(block)):
        g_ref, g_at, g_cols = grads[b]

        def gate_body(
            i, carry, row=row, x_ref=x_ref, g_ref=g_ref, g_at=g_at + first, g_cols=g_cols
        ):
            at = pl.multiple_of(i * step, step)
            here = pl.ds(pl.multiple_of(row + at, step), step)
            x = x_ref[pl.ds(at, step), mine]
            g = g_ref[pl.ds(pl.multiple_of(g_at + at, step), step), g_cols].astype(F32)
            keep = 2.0 * half_keep[here, :]
            prev = 2.0 * half_prev[here, :]
            c, cd = state[here, :], cand_ref[here, :]
            forget = 0.5 + 0.5 * jnp.tanh(zf_ref[here, :] + half_fw * prev)
            reset = 0.5 + 0.5 * jnp.tanh(zr_ref[here, :] + half_rw * prev)
            not_forget, not_reset = 1.0 - forget, 1.0 - reset
            out_ref[here, :] = reset * c + not_reset * x
            dxh_ref[here, :] = g * not_reset
            dzr = g * (c - x) * reset * not_reset
            slope = (prev - cd) * forget * not_forget
            back, extra = keep * (forget + slope * fw), g * reset
            coef[here, :] = back
            add[here, :] = back * extra + keep * (dzr * rw)
            add_e[here, :] = extra
            gz[here, :] = slope
            omf[here, :] = not_forget
            dproj_ref[here, 2 * cols : 3 * cols] = dzr.astype(BF16)
            return (carry[0] + dzr * prev, carry[1] + dzr)

        sums = lax.fori_loop(0, count // step, gate_body, sums, unroll=True)
        row += count
    rw_sum, rb_sum = sums

    dc = jnp.zeros((1, cols), F32)
    group = 8
    for k in range(3, -1, -1):
        for first, count in reversed(stretches(sel, block, k)):

            def backward_body(i, dc, end=first + count):
                base = pl.multiple_of(end - (i + 1) * group, group)
                for r in range(group - 1, -1, -1):
                    row = pl.ds(base + r, 1)
                    states[row, :] = dc
                    dc = coef[row, :] * dc + add[row, :]
                return dc

            dc = lax.fori_loop(0, count // group, backward_body, dc, unroll=2)

    def grad_body(i, carry):
        here = pl.ds(pl.multiple_of(i * step, step), step)
        total = states[here, :] + add_e[here, :]
        prev = 2.0 * half_prev[here, :]
        dzf = total * gz[here, :]
        dproj_ref[here, 0:cols] = (total * omf[here, :]).astype(BF16)
        dproj_ref[here, cols : 2 * cols] = dzf.astype(BF16)
        return (carry[0] + dzf * prev, carry[1] + dzf)

    fw_sum, fb_sum = lax.fori_loop(0, length // step, grad_body, (zero, zero), unroll=4)
    small_ref[...] = jnp.concatenate(
        [jnp.sum(v, axis=0, keepdims=True) for v in (fw_sum, rw_sum, fb_sum, rb_sum)]
        + [jnp.zeros((4, cols), F32)],
        axis=0,
    )
    outer_products(sel, rows, near_ref, far_ref, dproj_ref, products)


def outer_products(sel, rows, near_ref, far_ref, dproj_ref, outs):
    half, width = near_ref.shape
    part = width // 8
    dims = (((0,), (0,)), ((), ()))
    for out, places in zip(outs, rows):
        for k, place_of in enumerate(places):
            at = pl.ds(pl.multiple_of(row_part(sel, place_of) * part, part), part)
            out[k * part : (k + 1) * part, :] = lax.dot_general(
                near_ref[:, at], dproj_ref[0:half, :], dims, preferred_element_type=F32
            ) + lax.dot_general(
                far_ref[:, at], dproj_ref[half:, :], dims, preferred_element_type=F32
            )


def product_shapes(width, rows):
    return tuple(shaped((len(places) * width // 8, 3 * width // 4)) for places in rows)


def run_backward(sel, toks, cots, scanned, half_keep, gates, normed, rows):
    length, cols = half_keep.shape
    width = 4 * cols
    return pl.pallas_call(
        functools.partial(backward_kernel, rows=rows, count=len(toks)),
        out_shape=(
            shaped((length, 3 * cols), BF16),
            shaped((length, cols)),
            shaped((length, cols)),
            shaped((8, cols)),
        )
        + product_shapes(width, rows),
        in_specs=[smem()] + [vmem()] * (13 + len(toks)),
        out_specs=(vmem(),) * (4 + len(rows)),
        scratch_shapes=[pltpu.VMEM((length, cols), F32)] * 6,
        compiler_params=params(24),
        cost_estimate=cost(0.05),
        name="backward_scan",
    )(sel, *toks, *cots, *scanned, half_keep, *gates[:2], *normed)


def products_kernel(sel, near_ref, far_ref, dproj_ref, *outs, rows):
    outer_products(sel, rows, near_ref, far_ref, dproj_ref, outs[-len(rows) :])


def run_products(sel, normed, dproj, rows, *waits):
    return pl.pallas_call(
        functools.partial(products_kernel, rows=rows),
        out_shape=product_shapes(normed[0].shape[1], rows),
        in_specs=[smem()] + [vmem()] * 3 + [any_spec()] * len(waits),
        out_specs=(vmem(),) * len(rows),
        compiler_params=params(12),
        cost_estimate=cost(0.05),
        name="products",
    )(sel, *normed, dproj, *waits)


def input_kernel(sel, *refs, count):
    toks, (mine_ref, send_ref, dnormed) = refs[:count], refs[-3:]
    (stats_near, stats_far, dproj_ref, dxh_ref, out_ref), refs = refs[count : count + 5], refs[count + 5 :]
    gate_small_ref, w_ref, gain_ref = refs[:3]
    cols = dxh_ref.shape[1]
    block, width = toks[0].shape
    gain = gain_ref[...]
    mine = own_columns(sel, cols)
    step = 8
    sums = (jnp.zeros((step, width), F32), jnp.zeros((step, width), F32))
    row = 0
    for tok, (b, first, count) in zip(toks, segments(block)):
        if row % (2 * block) == 0:
            dnormed[...] = lax.dot_general(
                dproj_ref[row : row + 2 * block, :],
                w_ref[...],
                (((1,), (1,)), ((), ())),
                preferred_element_type=F32,
            )
        rows = slice(row, row + count)
        where = send_ref if b % 2 else mine_ref
        base = (b // 2) * block + first
        stats, at = (stats_near, row) if b < 2 else (stats_far, row - 2 * block)

        def body(i, carry, tok=tok, base=base, where=where, stats=stats, at=at):
            here = pl.ds(pl.multiple_of(i * step, step), step)
            there = pl.ds(pl.multiple_of(base + i * step, step), step)
            kept = pl.ds(pl.multiple_of(at + i * step, step), step)
            mean, rdev = (
                jnp.concatenate([stats[kept, k : k + LANES]] * (width // LANES), axis=1)
                for k in (0, LANES)
            )
            xhat = (tok[here, :] - mean) * rdev
            dn = dnormed[kept, :]
            dxhat = dn * gain
            mean1 = jnp.mean(dxhat, axis=-1, keepdims=True)
            mean2 = jnp.mean(dxhat * xhat, axis=-1, keepdims=True)
            where[there, 0:width] = rdev * (dxhat - mean1 - xhat * mean2)
            return (carry[0] + dn * xhat, carry[1] + dn)

        sums = lax.fori_loop(0, count // step, body, sums, unroll=11 if count == block else 4)
        to = pl.ds(base, count)
        where[to, mine] += dxh_ref[rows, :]
        where[to, width : width + cols] = out_ref[rows, :]
        row += count
    tail = slice(2 * block, 2 * block + 8)
    mine_ref[tail, :] = jnp.zeros((8, width + cols), F32)
    mine_ref[2 * block : 2 * block + 4, mine] = gate_small_ref[0:4, :]
    for i, v in enumerate(sums):
        row = 2 * block + 4 + i
        mine_ref[row : row + 1, 0:width] = jnp.sum(v, axis=0, keepdims=True)
    send_ref[tail, :] = mine_ref[tail, :]


def run_input(sel, toks, stats, dproj, dxh, out, gate_small, w_mine, gain, *waits):
    block, width = toks[0].shape
    shape = (2 * block + 8, width + width // 4)
    return pl.pallas_call(
        functools.partial(input_kernel, count=len(toks)),
        out_shape=(shaped(shape), shaped(shape)),
        in_specs=[smem()] + [vmem()] * (8 + len(toks)) + [any_spec()] * len(waits),
        out_specs=(vmem(),) * 2,
        scratch_shapes=[pltpu.VMEM((2 * block, width), F32)],
        compiler_params=params(20),
        cost_estimate=cost(0.05),
        name="input_side",
    )(sel, *toks, *stats, dproj, dxh, out, gate_small, w_mine, gain, *waits)


def combine_kernel(sel, mine_ref, got_ref, *refs):
    keep_ref, send_ref, small_ref = refs[-3:]
    block, width = keep_ref.shape[0], small_ref.shape[1]
    cols = width // 4
    low = pl.ds(pl.multiple_of(width + sel[1] * cols, cols), cols)
    high = pl.ds(pl.multiple_of(width + (1 - sel[1]) * cols, cols), cols)
    for ref, first in ((keep_ref, 0), (send_ref, block)):
        here = slice(first, first + block)
        ref[:, 0:width] = mine_ref[here, 0:width] + got_ref[here, 0:width]
        ref[:, low] = mine_ref[here, width:]
        ref[:, high] = got_ref[here, width:]
    small_ref[...] = mine_ref[2 * block :, 0:width] + got_ref[2 * block :, 0:width]


def combine(sel, mine, got, *waits):
    block, width = (mine.shape[0] - 8) // 2, mine.shape[1] * 4 // 5
    return pl.pallas_call(
        combine_kernel,
        out_shape=(shaped((block, width * 3 // 2)),) * 2 + (shaped((8, width)),),
        in_specs=[smem(), vmem(), vmem()] + [any_spec()] * len(waits),
        out_specs=(vmem(),) * 3,
        compiler_params=params(16),
        cost_estimate=cost(0.05),
        name="combine",
    )(sel, mine, got, *waits)


def join_kernel(sel, mine_ref, got_ref, out_ref, grad_ref, done_ref):
    done_ref[...] = jnp.zeros(done_ref.shape, F32)
    width = out_ref.shape[1]
    half = width // 2
    at = pl.multiple_of(sel[0] * half, half)
    other = pl.multiple_of((1 - sel[0]) * half, half)
    out_ref[:, pl.ds(at, half)] = mine_ref[:, width:].astype(BF16)
    out_ref[:, pl.ds(other, half)] = got_ref[:, width:].astype(BF16)
    grad_ref[...] = (mine_ref[:, 0:width] + got_ref[:, 0:width]).astype(BF16)


def join(sel, mine, got):
    block, width = mine.shape[0], mine.shape[1] * 2 // 3
    return pl.pallas_call(
        join_kernel,
        out_shape=(shaped((block, width), BF16),) * 2 + (shaped((8, LANES)),),
        in_specs=[smem()] + [vmem()] * 2,
        out_specs=(vmem(),) * 3,
        compiler_params=params(16),
        cost_estimate=cost(0.05),
        name="join",
    )(sel, mine, got)


def fold_small(small):
    rows, cols = 6, small.shape[1] // 4
    tails = [small[i : i + 1, 3 * cols :] for i in range(rows)]
    last = [jnp.concatenate(tails[:3], axis=1), jnp.concatenate(tails[3:], axis=1)]
    return jnp.concatenate([small[0:rows, : 3 * cols]] + last, axis=0)


def finish_kernel(keep_ref, got_ref, a1_ref, a3_ref, small_ref, both_ref):
    part = keep_ref.shape[0]
    both_ref[0:part, :] = keep_ref[...] + got_ref[...] + a1_ref[...] + a3_ref[...]
    both_ref[part:, :] = fold_small(small_ref[...])


def finish(keep, got, a1, a3, small):
    part, cols3 = keep.shape
    return pl.pallas_call(
        finish_kernel,
        out_shape=shaped((part + 8, cols3)),
        in_specs=[vmem()] * 5,
        out_specs=vmem(),
        compiler_params=params(8),
        cost_estimate=cost(0.05),
        name="finish",
    )(keep, got, a1, a3, small)


def second_kernel(both_ref, px0_ref, py0_ref, corner_ref, z1_ref, z3_ref, z13_ref, zs_ref, cs_ref):
    part = z1_ref.shape[0] - 8
    z13_ref[0:part, :] = z1_ref[0:part, :]
    z13_ref[part:, :] = z3_ref[0:part, :]
    small = (both_ref[part:, :] + px0_ref[part:, :]) + (py0_ref[part:, :] + corner_ref[part:, :])
    for ref, out in ((z3_ref, zs_ref), (corner_ref, cs_ref)):
        out[0:part, :] = ref[0:part, :]
        out[part:, :] = small


def second(*pieces):
    part, cols3 = pieces[-1].shape[0] - 8, pieces[-1].shape[1]
    return pl.pallas_call(
        second_kernel,
        out_shape=(shaped((2 * part, cols3)),) + (shaped((part + 8, cols3)),) * 2,
        in_specs=[vmem()] * 6,
        out_specs=(vmem(),) * 3,
        compiler_params=params(10),
        cost_estimate=cost(0.05),
        name="second",
    )(*pieces)


def stack_kernel(*refs, rows):
    at = 0
    for ref, (first, count) in zip(refs, rows):
        refs[-1][at : at + count, :] = ref[first : first + count, :]
        at += count


def stack(*parts):
    rows = tuple((first, count) for _, first, count in parts)
    return pl.pallas_call(
        functools.partial(stack_kernel, rows=rows),
        out_shape=shaped((sum(count for _, count in rows), parts[0][0].shape[1])),
        in_specs=[vmem()] * len(parts),
        out_specs=vmem(),
        compiler_params=params(6),
        cost_estimate=cost(0.05),
        name="stack",
    )(*(array for array, _, _ in parts))


def small_kernel(*refs, where):
    pieces, outs = refs[:-6], refs[-6:]
    sums = [pieces[i][at : at + 8, :] for i, at in where]
    while len(sums) > 1:
        sums = [a + b for a, b in zip(sums[::2], sums[1::2])]
    total = sums[0]
    cols = total.shape[1] // 3
    for i, out in enumerate(outs):
        out[:, 0 : 3 * cols] = total[i : i + 1, :]
        out[:, 3 * cols :] = total[6 + i // 3 : 7 + i // 3, (i % 3) * cols : (i % 3 + 1) * cols]


def small_sums(pieces, where):
    width = pieces[0].shape[1] // 3 * 4
    return pl.pallas_call(
        functools.partial(small_kernel, where=where),
        out_shape=(shaped((1, width)),) * 6,
        in_specs=[vmem()] * len(pieces),
        out_specs=(vmem(),) * 6,
        compiler_params=params(8),
        cost_estimate=cost(0.05),
        name="small_sums",
    )(*pieces)


def place_kernel(sel, *refs, where, give):
    target, sem = refs[-2 - bool(give)], refs[-1]
    cols = refs[0].shape[1] // 3
    width = target.shape[1] // 3
    part = width // 8
    copies = []

    def copy(src, dst):
        copies.append(pltpu.make_async_copy(src, dst, sem.at[len(copies)]))
        copies[-1].start()

    for at, (array, first, rows, row, row_off, x_off, c_off) in enumerate(where):
        piece = refs[array].at[pl.ds(first, rows)]
        to_row = pl.multiple_of(row_part(sel, row) * part + row_off, 8)
        col = (2 * (sel[0] ^ x_off) + (sel[1] ^ c_off)) * cols
        for k in range(3):
            to = pl.multiple_of(col + k * width, cols)
            copy(piece.at[:, pl.ds(k * cols, cols)], target.at[pl.ds(to_row, rows), pl.ds(to, cols)])
        if at < give:
            copy(piece, refs[-2].at[pl.ds(at * part, part)])
    for c in copies:
        c.wait()


def place(sel, arrays, where, target, width, give, *waits):
    count = len(arrays)
    extra = [] if target is None else [target]
    cols3 = 3 * width // 4
    return pl.pallas_call(
        functools.partial(place_kernel, where=where, give=give),
        out_shape=(shaped((width, 3 * width)),)
        + ((shaped((give * width // 8, cols3)),) if give else ()),
        in_specs=[smem()]
        + [vmem()] * count
        + [hbm()] * len(extra)
        + [any_spec()] * len(waits),
        out_specs=(hbm(), vmem()) if give else (hbm(),),
        scratch_shapes=[pltpu.SemaphoreType.DMA((3 * len(where) + give,))],
        input_output_aliases={1 + count: 0} if extra else {},
        compiler_params=params(8),
        cost_estimate=cost(0.05),
        name="place",
    )(sel, *arrays, *extra, *waits)


def given(array, where):
    return [
        (array, i * rows, rows, row, row_off, x_off, 1)
        for i, (_, _, rows, row, row_off, x_off, _) in enumerate(where)
    ]


def on_device(
    tokens,
    offsets,
    w_proj,
    forget_weight,
    reset_weight,
    forget_bias,
    reset_bias,
    layer_norm_gain,
    layer_norm_bias,
    cotangent,
):
    _, block, width = tokens.shape
    z, y, x, c = (lax.axis_index(a) for a in ("z", "y", "x", "c"))
    tuned = lax.axis_size("z") == 4
    sel = jnp.stack([x, c, y, z]).astype(jnp.int32)
    part = width // 8

    cot = cotangent[0]
    own = tokens[0].astype(F32)
    own, *parts = lax.optimization_barrier(
        (own, *(own[first : first + rows] for first, rows in chunks(block)))
    )
    x_a, x_b, x_c = (swap(piece, "x") for piece in parts)
    tok_c = swap(own, "c")
    cot_sibling = swap(widen_cot(sel, cot), "c")
    cot_far = swap(pack_cot(sel, cot, cot_sibling), "x")

    gates = [
        v.reshape(1, width) for v in (forget_weight, reset_weight, forget_bias, reset_bias)
    ]
    gain = layer_norm_gain.reshape(1, width)
    vectors = (*gates, gain, layer_norm_bias.reshape(1, width))
    w_mine = take_weights(sel, w_proj)
    near = run_near(sel, offsets, (own, tok_c), w_mine, vectors)
    (x_a,) = hold((x_a,), near[5])
    xc_a = swap(x_a, "c")
    (x_b,) = hold((x_b,), xc_a)
    xc_b = swap(x_b, "c")
    early = run_early(sel, (x_a, xc_a, x_b, xc_b), w_mine, vectors)
    (x_c,) = hold((x_c,), early[0])
    xc_c = swap(x_c, "c")
    far = run_forward(sel, (x_c, xc_c), near[2:], early, w_mine, vectors)
    normed = (near[0], far[0])
    toks = (own, tok_c, x_a, xc_a, x_b, xc_b, x_c, xc_c)
    if tuned:
        rows = [[[(d, 1)] for d in (2, 3, 1, 0)], [[(d, 0)] for d in (2, 3, 1, 0)]]
    else:
        rows = [[[0], [1], [2], [3]], [[4], [5], [6], [7]]]
    dproj, out, dxh, gate_small, s2 = run_backward(
        sel, toks, (cot, cot_sibling, cot_far), far[2:], near[5], gates, normed, rows[0][:1]
    )
    s3, k2 = run_products(sel, normed, dproj, (rows[0][1], rows[1][0]))
    grad_mine, grad_send = run_input(
        sel, toks, (near[1], far[1]), dproj, dxh, out, gate_small, w_mine, gain
    )
    late = (*rows[0][2:], *rows[1][1:])

    if tuned:
        s1, s0, k3, k1, k0 = run_products(sel, normed, dproj, late)
        q2 = add(k2, swap(s2, "y"), s3, s0, grad_send)
        r3, r1, r0 = (swap(piece, "y") for piece in (s3, s1, s0))
        a2 = xor_permute(q2, "z", 1)
        h3 = add(add(k3, r3), a2)
        a3 = xor_permute(h3, "z", 3)
        kept, sent, small = combine(
            sel, grad_mine, swap(grad_send, "c"), q2, tick(grad_send)
        )
        got = swap(sent, "x")
        a1 = xor_permute(add(k1, r1, sent), "z", 1)
        both = finish(k0, r0, a1, a3, small)
        output, input_grad, joined = join(sel, kept, got)

        px0, z3, z1, py0 = (
            swap(both, "x"),
            xor_permute(both, "z", 3),
            xor_permute(both, "z", 1),
            swap(both, "y"),
        )
        (px0,) = hold((px0,), joined)
        corner0 = swap(px0, "y")
        z3, z1, corner0, py0 = hold((z3, z1, corner0, py0))
        full = part + 8
        z13, zs, cs = second(both, px0, py0, corner0, z1, z3)
        z2, px13, py13 = xor_permute(zs, "z", 1), swap(z13, "x"), swap(z13, "y")
        corner3 = xor_permute(cs, "z", 3)
        own = [
            (0, 0, part, (0, 0), 0, 0, 0),
            (1, 0, part, (0, 0), 0, 1, 0),
            (2, 0, part, (0, 1), 0, 0, 0),
            (3, 0, part, (0, 1), 0, 1, 0),
        ]
        proj_grad, give = place(sel, (both, px0, py0, corner0), own, None, width, 4)
        z2, px13, py13, corner3 = hold((z2, px13, py13, corner3), give)
        third = 3 * part // 8
        rest = part - 2 * third
        px2 = swap(stack((z2, 0, part), (py13, 0, third)), "x")
        py2 = swap(stack((z2, 0, part), (px13, third, third)), "y")
        corner12 = xor_permute(
            stack((corner3, 0, part), (corner0, 2 * third, rest), (corner3, part, 8)), "z", 1
        )
        other = given(3, own)
        own = [
            (array, part * i, part, (d, y_off), 0, x_off, 0)
            for array, y_off, x_off in ((0, 0, 0), (1, 0, 1), (2, 1, 0))
            for i, d in ((0, 1), (1, 3))
        ]
        proj_grad, give = place(
            sel,
            (z13, px13, py13, swap(give, "c")),
            own + other,
            proj_grad,
            width,
            6,
            tick(give, corner3),
        )
        other = given(3, own)
        first_give, marked = swap(give, "c"), give
        own = [(0, 0, part, (2, 0), 0, 0, 0), (1, 0, part, (3, 1), 0, 1, 0)]
        proj_grad, give = place(sel, (z2, corner3), own, proj_grad, width, 2)
        other += given(4, own)
        px2, py2, corner12 = hold((px2, py2, corner12), give)
        own = [
            (0, 0, part, (2, 0), 0, 1, 0),
            (0, part, third, (1, 1), 0, 1, 0),
            (1, 0, part, (2, 1), 0, 0, 0),
            (1, part, third, (1, 1), third, 1, 0),
            (2, 0, part, (2, 1), 0, 1, 0),
            (2, part, rest, (1, 1), 2 * third, 1, 0),
        ]
        arrays = (px2, py2, corner12, first_give, swap(give, "c"))
        (proj_grad,) = place(
            sel, arrays, own + other, proj_grad, width, 0, tick(marked, give, px2)
        )
        own = [(*place_of[:-1], 1) for place_of in own]
        arrays = [swap(a, "c") for a in (px2, py2, corner12)]
        (proj_grad,) = place(sel, arrays, own, proj_grad, width, 0)
        where = [(0, part), (1, part), (2, part + rest), (3, part)]
        small = small_sums((zs, z2, corner12, corner3), where)
    else:
        s1, s0, k3, k1, k0 = run_products(sel, normed, dproj, late)
        kept, sent, small = combine(sel, grad_mine, swap(grad_send, "c"))
        got = swap(sent, "x")
        small = lax.psum(small + swap(small, "x"), ("z", "y"))
        pieces = jnp.stack([s2, s3, s1, s0, k2, k3, k1, k0])
        pieces = lax.psum(pieces, ("z", "y"))
        proj_grad = None
        for x_off, held in ((0, pieces), (1, swap(pieces, "x"))):
            own = [(r, 0, part, r, 0, x_off, 0) for r in range(8)]
            proj_grad, give = place(sel, list(held), own, proj_grad, width, 8)
            other = given(0, own)
            (proj_grad,) = place(sel, [swap(give, "c")], other, proj_grad, width, 0)
        output, input_grad, _ = join(sel, kept, got)
    small = [small[i].reshape(width) for i in range(6)]
    return (output[None], input_grad[None], proj_grad, *small)


def solution(mesh):
    dp, rep = mesh.shape["dp"], mesh.shape["rep"]
    fine = Mesh(mesh.devices.reshape(dp // 2, 2, rep // 2, 2), ("z", "y", "x", "c"))
    row, seq = ("z", "y"), ("x", "c")
    in_specs = (P(row, seq, None), P(row, None)) + (P(),) * 7 + (P(row, seq, None),)
    out_specs = (P(row, seq, None), P(row, seq, None)) + (P(),) * 7
    return jax.shard_map(
        on_device, mesh=fine, in_specs=in_specs, out_specs=out_specs, check_vma=False
    )
```

```python
import functools

import jax
import jax.numpy as jnp
from jax import lax
from jax.experimental import pallas as pl
from jax.experimental.pallas import tpu as pltpu
from jax.sharding import Mesh
from jax.sharding import PartitionSpec as P

EPS = 1e-05
LANES = 128
SWAP = [(0, 1), (1, 0)]
VMEM_BYTES = 56 * 2**20
F32 = jnp.float32
BF16 = jnp.bfloat16


def swap(block, axis):
    return lax.ppermute(block, axis, SWAP)


def xor_permute(block, axis, distance):
    size = lax.axis_size(axis)
    return lax.ppermute(block, axis, [(i, i ^ distance) for i in range(size)])


def any_spec():
    return pl.BlockSpec(memory_space=pl.ANY)


def hbm():
    return pl.BlockSpec(memory_space=pltpu.HBM)


def vmem():
    return pl.BlockSpec(memory_space=pltpu.VMEM)


def smem():
    return pl.BlockSpec(memory_space=pltpu.SMEM)


def shaped(shape, dtype=F32):
    return jax.ShapeDtypeStruct(shape, dtype)


def params(mib):
    return pltpu.CompilerParams(vmem_limit_bytes=mib * 2**20)


def cost(us):
    return pl.CostEstimate(
        flops=int(us * 1.1e9), bytes_accessed=int(us * 3.6e6), transcendentals=0
    )


def own_columns(sel, cols):
    return pl.ds(pl.multiple_of((2 * sel[0] + sel[1]) * cols, cols), cols)


def stored_at(sel, k):
    return 2 * ((k // 2) ^ sel[0]) + ((k % 2) ^ sel[1])


def chunks(block):
    unit = block // 88 * 16
    sizes = (unit, 2 * unit, block - 3 * unit)
    return tuple((sum(sizes[:i]), size) for i, size in enumerate(sizes))


def segments(block):
    far = [(b, first, rows) for first, rows in chunks(block) for b in (2, 3)]
    return ((0, 0, block), (1, 0, block), *far)


def stretches(sel, block, k):
    held = stored_at(sel, k)
    near = held < 2
    return tuple(
        (jnp.where(near, held * block + first, 2 * (block + first) + (held - 2) * rows), rows)
        for first, rows in chunks(block)
    )


def row_part(sel, row):
    return row if isinstance(row, int) else 2 * (sel[3] ^ row[0]) + (sel[2] ^ row[1])


def tick_kernel(*refs):
    refs[-1][...] = jnp.zeros(refs[-1].shape, F32)


def tick(*values):
    return pl.pallas_call(
        tick_kernel,
        out_shape=shaped((8, 128)),
        in_specs=[any_spec()] * len(values),
        out_specs=vmem(),
        compiler_params=params(1),
        cost_estimate=cost(20),
        name="tick",
    )(*values)


def hold_kernel(*refs):
    del refs


def hold(values, *waits):
    count = len(values)
    return pl.pallas_call(
        hold_kernel,
        out_shape=tuple(shaped(v.shape, v.dtype) for v in values),
        in_specs=[any_spec()] * (count + len(waits)),
        out_specs=(any_spec(),) * count,
        input_output_aliases={i: i for i in range(count)},
        compiler_params=params(1),
        cost_estimate=cost(0.05),
        name="hold",
    )(*values, *waits)


def add_kernel(a_ref, b_ref, *refs):
    refs[-1][...] = a_ref[...] + b_ref[...]


def add(a, b, *waits):
    return pl.pallas_call(
        add_kernel,
        out_shape=shaped(a.shape),
        in_specs=[vmem()] * 2 + [any_spec()] * len(waits),
        out_specs=vmem(),
        compiler_params=params(4),
        cost_estimate=cost(0.05),
        name="add",
    )(a, b, *waits)


def take_weights_kernel(sel, w_ref, mine_ref, sem):
    width, cols = mine_ref.shape[0], mine_ref.shape[1] // 3
    copies = []
    for k in range(3):
        at = pl.multiple_of((2 * sel[0] + sel[1]) * cols + k * width, cols)
        copies.append(
            pltpu.make_async_copy(
                w_ref.at[:, pl.ds(at, cols)], mine_ref.at[:, k * cols : (k + 1) * cols], sem.at[k]
            )
        )
    for c in copies:
        c.start()
    for c in copies:
        c.wait()


def take_weights(sel, w_proj):
    width = w_proj.shape[0]
    return pl.pallas_call(
        take_weights_kernel,
        out_shape=shaped((width, 3 * width // 4), BF16),
        in_specs=[smem(), hbm()],
        out_specs=vmem(),
        scratch_shapes=[pltpu.SemaphoreType.DMA((3,))],
        compiler_params=params(4),
        cost_estimate=cost(0.05),
        name="take_weights",
    )(sel, w_proj)


def widen_cot_kernel(sel, cot_ref, cot_out):
    cols = cot_ref.shape[1] // 4
    for k in range(2):
        at = pl.multiple_of((2 * k + 1 - sel[1]) * cols, cols)
        cot_out[:, k * cols : (k + 1) * cols] = cot_ref[:, pl.ds(at, cols)].astype(F32)


def widen_cot(sel, cot):
    return pl.pallas_call(
        widen_cot_kernel,
        out_shape=shaped((cot.shape[0], cot.shape[1] // 2)),
        in_specs=[smem(), vmem()],
        out_specs=vmem(),
        compiler_params=params(4),
        cost_estimate=cost(0.05),
        name="widen_cot",
    )(sel, cot)


def pack_cot_kernel(sel, cot_ref, sibling_ref, cot_out):
    block, cols = cot_ref.shape[0], cot_ref.shape[1] // 4
    mine = pl.multiple_of((2 * (1 - sel[0]) + sel[1]) * cols, cols)
    cot_out[0:block, :] = cot_ref[:, pl.ds(mine, cols)].astype(F32)
    sibling = pl.multiple_of((1 - sel[0]) * cols, cols)
    cot_out[block:, :] = sibling_ref[:, pl.ds(sibling, cols)]


def pack_cot(sel, cot, sibling):
    return pl.pallas_call(
        pack_cot_kernel,
        out_shape=shaped((2 * cot.shape[0], cot.shape[1] // 4)),
        in_specs=[smem(), vmem(), vmem()],
        out_specs=vmem(),
        compiler_params=params(4),
        cost_estimate=cost(0.05),
        name="pack_cot",
    )(sel, cot, sibling)


def standardized(x):
    mean = jnp.mean(x, axis=-1, keepdims=True)
    centred = x - mean
    rdev = lax.rsqrt(jnp.mean(centred * centred, axis=-1, keepdims=True) + EPS)
    return centred * rdev, mean, rdev


def norm_and_project(sel, toks, norm, w_ref, gates, normed, stats, cand, zf, zr, first, base):
    cols = cand.shape[1]
    mine = own_columns(sel, cols)
    gain, bias = norm[0][...], norm[1][...]
    fb, rb = gates[2][:, mine], gates[3][:, mine]
    step = 16
    at = first
    for tok in toks:

        def body(i, carry, tok=tok, at=at):
            here = pl.ds(pl.multiple_of(i * step, step), step)
            there = pl.ds(pl.multiple_of(at + i * step, step), step)
            xhat, mean, rdev = standardized(tok[here, :])
            normed[there, :] = (xhat * gain + bias).astype(BF16)
            stats[there, 0:LANES] = jnp.broadcast_to(mean, (step, LANES))
            stats[there, LANES:] = jnp.broadcast_to(rdev, (step, LANES))
            return carry

        lax.fori_loop(0, tok.shape[0] // step, body, 0, unroll=True)
        at += tok.shape[0]
    rows = normed[first:at, :]
    here = slice(base, base + at - first)
    part = lambda k: jnp.dot(
        rows, w_ref[:, k * cols : (k + 1) * cols], preferred_element_type=F32
    )
    cand[here, :] = part(0)
    zf[here, :] = 0.5 * (part(1) + fb)
    zr[here, :] = 0.5 * (part(2) + rb)


def near_kernel(sel, offsets, tok0, tok1, w_ref, *refs):
    gates, norm, (normed, stats, cand, zf, zr, half_keep) = refs[:4], refs[4:6], refs[6:]
    length, cols = half_keep.shape
    block = length // 4
    step = 16
    row = 0
    for b, first, rows in segments(block):
        base = stored_at(sel, b) * block + first

        def body(i, carry, row=row, base=base):
            at = pl.multiple_of(i * step, step)
            token = base + at + lax.broadcasted_iota(jnp.int32, (step, cols), 0)
            starts = token == offsets[0, 0]
            for k in range(1, offsets.shape[1]):
                starts = starts | (token == offsets[0, k])
            half_keep[pl.ds(pl.multiple_of(row + at, step), step), :] = jnp.where(starts, 0.0, 0.5)
            return carry

        lax.fori_loop(0, rows // step, body, 0)
        row += rows
    norm_and_project(sel, (tok0, tok1), norm, w_ref, gates, normed, stats, cand, zf, zr, 0, 0)


def run_near(sel, offsets, toks, w_mine, vectors):
    block, width = toks[0].shape
    cols = width // 4
    return pl.pallas_call(
        near_kernel,
        out_shape=(shaped((2 * block, width), BF16), shaped((2 * block, 2 * LANES)))
        + (shaped((2 * block, cols)),) * 3
        + (shaped((4 * block, cols)),),
        in_specs=[smem()] * 2 + [vmem()] * 9,
        out_specs=(vmem(),) * 6,
        compiler_params=params(16),
        cost_estimate=cost(0.05),
        name="near_blocks",
    )(sel, offsets, *toks, w_mine, *vectors)


def early_kernel(sel, *refs, count):
    toks, w_ref, refs = refs[:count], refs[count], refs[count + 1 :]
    gates, norm, (normed, stats, cand, zf, zr) = refs[:4], refs[4:6], refs[-5:]
    norm_and_project(sel, toks, norm, w_ref, gates, normed, stats, cand, zf, zr, 0, 0)


def run_early(sel, toks, w_mine, vectors):
    rows, width = sum(tok.shape[0] for tok in toks), toks[0].shape[1]
    cols = width // 4
    return pl.pallas_call(
        functools.partial(early_kernel, count=len(toks)),
        out_shape=(shaped((rows, width), BF16), shaped((rows, 2 * LANES)))
        + (shaped((rows, cols)),) * 3,
        in_specs=[smem()] + [vmem()] * (7 + len(toks)),
        out_specs=(vmem(),) * 5,
        compiler_params=params(12),
        cost_estimate=cost(0.05),
        name="early_blocks",
    )(sel, *toks, w_mine, *vectors)


def forward_kernel(
    sel,
    tok0,
    tok1,
    cand_near,
    zf_near,
    zr_near,
    half_keep,
    normed_early,
    stats_early,
    cand_early,
    zf_early,
    zr_early,
    w_ref,
    *refs,
):
    gates, norm, (normed, stats, cand, zf, zr, state, half_prev) = refs[:4], refs[4:6], refs[6:]
    length, cols = cand.shape
    block = length // 4
    early = normed_early.shape[0]
    normed[0:early, :] = normed_early[...]
    stats[0:early, :] = stats_early[...]
    first = 2 * block
    near, mid = slice(0, first), slice(first, first + early)
    cand[near, :], zf[near, :], zr[near, :] = cand_near[...], zf_near[...], zr_near[...]
    cand[mid, :], zf[mid, :], zr[mid, :] = cand_early[...], zf_early[...], zr_early[...]
    fw = gates[0][:, own_columns(sel, cols)]
    norm_and_project(
        sel, (tok0, tok1), norm, w_ref, gates, normed, stats, cand, zf, zr, early, first + early
    )
    zero = jnp.zeros((1, cols), F32)
    carry = (zero, zero, zero)
    for k in range(4):
        for base, rows in stretches(sel, block, k):

            def body(i, carry, base=base):
                middle, spread, th = carry
                row = pl.ds(base + i, 1)
                half = half_keep[row, :]
                weight = half * fw
                last = middle + spread * th
                th = jnp.tanh((zf[row, :] + weight * middle) + (weight * spread) * th)
                hp = half * last
                hc = 0.5 * cand[row, :]
                middle, spread = hp + hc, hp - hc
                state[row, :] = middle + spread * th
                half_prev[row, :] = hp
                return (middle, spread, th)

            carry = lax.fori_loop(0, rows, body, carry, unroll=16)


def run_forward(sel, toks, near, early, w_mine, vectors):
    late, width = toks[0].shape
    cols = width // 4
    length = near[-1].shape[0]
    return pl.pallas_call(
        forward_kernel,
        out_shape=(shaped((length // 2, width), BF16), shaped((length // 2, 2 * LANES)))
        + (shaped((length, cols)),) * 5,
        in_specs=[smem()] + [vmem()] * 18,
        out_specs=(vmem(),) * 7,
        compiler_params=params(20),
        cost_estimate=cost(0.05),
        name="forward_scan",
    )(sel, *toks, *near, *early, w_mine, *vectors)


def backward_kernel(sel, *refs, rows, count):
    toks, refs = refs[:count], refs[count:]
    (g0, g1, g23, cand_ref, zf_ref, zr_ref, state, half_prev), refs = refs[:8], refs[8:]
    (half_keep, fw_ref, rw_ref, near_ref, far_ref), refs = refs[:5], refs[5:]
    (dproj_ref, out_ref, dxh_ref, small_ref), refs = refs[:4], refs[4:]
    products, (coef, add, add_e, gz, omf, states) = refs[: len(rows)], refs[len(rows) :]
    length, cols = cand_ref.shape
    block = length // 4
    mine = own_columns(sel, cols)
    half = pl.ds(pl.multiple_of(sel[0] * cols, cols), cols)
    fw, rw = fw_ref[:, mine], rw_ref[:, mine]
    half_fw, half_rw = 0.5 * fw, 0.5 * rw
    step = 16
    zero = jnp.zeros((step, cols), F32)
    sums = (zero, zero)
    everything = slice(0, cols)
    grads = ((g0, 0, mine), (g1, 0, half), (g23, 0, everything), (g23, block, everything))
    row = 0
    for x_ref, (b, first, count) in zip(toks, segments(block)):
        g_ref, g_at, g_cols = grads[b]

        def gate_body(
            i, carry, row=row, x_ref=x_ref, g_ref=g_ref, g_at=g_at + first, g_cols=g_cols
        ):
            at = pl.multiple_of(i * step, step)
            here = pl.ds(pl.multiple_of(row + at, step), step)
            x = x_ref[pl.ds(at, step), mine]
            g = g_ref[pl.ds(pl.multiple_of(g_at + at, step), step), g_cols].astype(F32)
            keep = 2.0 * half_keep[here, :]
            prev = 2.0 * half_prev[here, :]
            c, cd = state[here, :], cand_ref[here, :]
            forget = 0.5 + 0.5 * jnp.tanh(zf_ref[here, :] + half_fw * prev)
            reset = 0.5 + 0.5 * jnp.tanh(zr_ref[here, :] + half_rw * prev)
            not_forget, not_reset = 1.0 - forget, 1.0 - reset
            out_ref[here, :] = reset * c + not_reset * x
            dxh_ref[here, :] = g * not_reset
            dzr = g * (c - x) * reset * not_reset
            slope = (prev - cd) * forget * not_forget
            back, extra = keep * (forget + slope * fw), g * reset
            coef[here, :] = back
            add[here, :] = back * extra + keep * (dzr * rw)
            add_e[here, :] = extra
            gz[here, :] = slope
            omf[here, :] = not_forget
            dproj_ref[here, 2 * cols : 3 * cols] = dzr.astype(BF16)
            return (carry[0] + dzr * prev, carry[1] + dzr)

        sums = lax.fori_loop(0, count // step, gate_body, sums, unroll=True)
        row += count
    rw_sum, rb_sum = sums

    dc = jnp.zeros((1, cols), F32)
    group = 8
    for k in range(3, -1, -1):
        for first, count in reversed(stretches(sel, block, k)):

            def backward_body(i, dc, end=first + count):
                base = pl.multiple_of(end - (i + 1) * group, group)
                for r in range(group - 1, -1, -1):
                    row = pl.ds(base + r, 1)
                    states[row, :] = dc
                    dc = coef[row, :] * dc + add[row, :]
                return dc

            dc = lax.fori_loop(0, count // group, backward_body, dc, unroll=2)

    def grad_body(i, carry):
        here = pl.ds(pl.multiple_of(i * step, step), step)
        total = states[here, :] + add_e[here, :]
        prev = 2.0 * half_prev[here, :]
        dzf = total * gz[here, :]
        dproj_ref[here, 0:cols] = (total * omf[here, :]).astype(BF16)
        dproj_ref[here, cols : 2 * cols] = dzf.astype(BF16)
        return (carry[0] + dzf * prev, carry[1] + dzf)

    fw_sum, fb_sum = lax.fori_loop(0, length // step, grad_body, (zero, zero), unroll=4)
    small_ref[...] = jnp.concatenate(
        [jnp.sum(v, axis=0, keepdims=True) for v in (fw_sum, rw_sum, fb_sum, rb_sum)]
        + [jnp.zeros((4, cols), F32)],
        axis=0,
    )
    outer_products(sel, rows, near_ref, far_ref, dproj_ref, products)


def outer_products(sel, rows, near_ref, far_ref, dproj_ref, outs):
    half, width = near_ref.shape
    part = width // 8
    dims = (((0,), (0,)), ((), ()))
    for out, places in zip(outs, rows):
        for k, place_of in enumerate(places):
            at = pl.ds(pl.multiple_of(row_part(sel, place_of) * part, part), part)
            out[k * part : (k + 1) * part, :] = lax.dot_general(
                near_ref[:, at], dproj_ref[0:half, :], dims, preferred_element_type=F32
            ) + lax.dot_general(
                far_ref[:, at], dproj_ref[half:, :], dims, preferred_element_type=F32
            )


def product_shapes(width, rows):
    return tuple(shaped((len(places) * width // 8, 3 * width // 4)) for places in rows)


def run_backward(sel, toks, cots, scanned, half_keep, gates, normed, rows):
    length, cols = half_keep.shape
    width = 4 * cols
    return pl.pallas_call(
        functools.partial(backward_kernel, rows=rows, count=len(toks)),
        out_shape=(
            shaped((length, 3 * cols), BF16),
            shaped((length, cols)),
            shaped((length, cols)),
            shaped((8, cols)),
        )
        + product_shapes(width, rows),
        in_specs=[smem()] + [vmem()] * (13 + len(toks)),
        out_specs=(vmem(),) * (4 + len(rows)),
        scratch_shapes=[pltpu.VMEM((length, cols), F32)] * 6,
        compiler_params=params(24),
        cost_estimate=cost(0.05),
        name="backward_scan",
    )(sel, *toks, *cots, *scanned, half_keep, *gates[:2], *normed)


def products_kernel(sel, near_ref, far_ref, dproj_ref, *outs, rows):
    outer_products(sel, rows, near_ref, far_ref, dproj_ref, outs[-len(rows) :])


def run_products(sel, normed, dproj, rows, *waits):
    return pl.pallas_call(
        functools.partial(products_kernel, rows=rows),
        out_shape=product_shapes(normed[0].shape[1], rows),
        in_specs=[smem()] + [vmem()] * 3 + [any_spec()] * len(waits),
        out_specs=(vmem(),) * len(rows),
        compiler_params=params(12),
        cost_estimate=cost(0.05),
        name="products",
    )(sel, *normed, dproj, *waits)


def input_kernel(sel, *refs, count):
    toks, (mine_ref, send_ref, dnormed) = refs[:count], refs[-3:]
    (stats_near, stats_far, dproj_ref, dxh_ref, out_ref), refs = refs[count : count + 5], refs[count + 5 :]
    gate_small_ref, w_ref, gain_ref = refs[:3]
    cols = dxh_ref.shape[1]
    block, width = toks[0].shape
    gain = gain_ref[...]
    mine = own_columns(sel, cols)
    step = 8
    sums = (jnp.zeros((step, width), F32), jnp.zeros((step, width), F32))
    row = 0
    for tok, (b, first, count) in zip(toks, segments(block)):
        if row % (2 * block) == 0:
            dnormed[...] = lax.dot_general(
                dproj_ref[row : row + 2 * block, :],
                w_ref[...],
                (((1,), (1,)), ((), ())),
                preferred_element_type=F32,
            )
        rows = slice(row, row + count)
        where = send_ref if b % 2 else mine_ref
        base = (b // 2) * block + first
        stats, at = (stats_near, row) if b < 2 else (stats_far, row - 2 * block)

        def body(i, carry, tok=tok, base=base, where=where, stats=stats, at=at):
            here = pl.ds(pl.multiple_of(i * step, step), step)
            there = pl.ds(pl.multiple_of(base + i * step, step), step)
            kept = pl.ds(pl.multiple_of(at + i * step, step), step)
            mean, rdev = (
                jnp.concatenate([stats[kept, k : k + LANES]] * (width // LANES), axis=1)
                for k in (0, LANES)
            )
            xhat = (tok[here, :] - mean) * rdev
            dn = dnormed[kept, :]
            dxhat = dn * gain
            mean1 = jnp.mean(dxhat, axis=-1, keepdims=True)
            mean2 = jnp.mean(dxhat * xhat, axis=-1, keepdims=True)
            where[there, 0:width] = rdev * (dxhat - mean1 - xhat * mean2)
            return (carry[0] + dn * xhat, carry[1] + dn)

        sums = lax.fori_loop(0, count // step, body, sums, unroll=11 if count == block else 4)
        to = pl.ds(base, count)
        where[to, mine] += dxh_ref[rows, :]
        where[to, width : width + cols] = out_ref[rows, :]
        row += count
    tail = slice(2 * block, 2 * block + 8)
    mine_ref[tail, :] = jnp.zeros((8, width + cols), F32)
    mine_ref[2 * block : 2 * block + 4, mine] = gate_small_ref[0:4, :]
    for i, v in enumerate(sums):
        row = 2 * block + 4 + i
        mine_ref[row : row + 1, 0:width] = jnp.sum(v, axis=0, keepdims=True)
    send_ref[tail, :] = mine_ref[tail, :]


def run_input(sel, toks, stats, dproj, dxh, out, gate_small, w_mine, gain, *waits):
    block, width = toks[0].shape
    shape = (2 * block + 8, width + width // 4)
    return pl.pallas_call(
        functools.partial(input_kernel, count=len(toks)),
        out_shape=(shaped(shape), shaped(shape)),
        in_specs=[smem()] + [vmem()] * (8 + len(toks)) + [any_spec()] * len(waits),
        out_specs=(vmem(),) * 2,
        scratch_shapes=[pltpu.VMEM((2 * block, width), F32)],
        compiler_params=params(20),
        cost_estimate=cost(0.05),
        name="input_side",
    )(sel, *toks, *stats, dproj, dxh, out, gate_small, w_mine, gain, *waits)


def combine_kernel(sel, mine_ref, got_ref, *refs):
    keep_grad, keep_out, send_grad, send_out, small_ref = refs[-5:]
    block, width = keep_grad.shape
    cols = width // 4
    low = pl.ds(pl.multiple_of(sel[1] * cols, cols), cols)
    high = pl.ds(pl.multiple_of((1 - sel[1]) * cols, cols), cols)
    for grad, out, first in ((keep_grad, keep_out, 0), (send_grad, send_out, block)):
        here = slice(first, first + block)
        grad[...] = mine_ref[here, 0:width] + got_ref[here, 0:width]
        out[:, low] = mine_ref[here, width:]
        out[:, high] = got_ref[here, width:]
    small_ref[...] = mine_ref[2 * block :, 0:width] + got_ref[2 * block :, 0:width]


def combine(sel, mine, got, *waits):
    block, width = (mine.shape[0] - 8) // 2, mine.shape[1] * 4 // 5
    return pl.pallas_call(
        combine_kernel,
        out_shape=(shaped((block, width)), shaped((block, width // 2))) * 2 + (shaped((8, width)),),
        in_specs=[smem(), vmem(), vmem()] + [any_spec()] * len(waits),
        out_specs=(vmem(),) * 5,
        compiler_params=params(16),
        cost_estimate=cost(0.05),
        name="combine",
    )(sel, mine, got, *waits)


def join_grad_kernel(mine_ref, got_ref, grad_ref, done_ref):
    done_ref[...] = jnp.zeros(done_ref.shape, F32)
    grad_ref[...] = (mine_ref[...] + got_ref[...]).astype(BF16)


def join_grad(mine, got):
    return pl.pallas_call(
        join_grad_kernel,
        out_shape=(shaped(mine.shape, BF16), shaped((8, LANES))),
        in_specs=[vmem()] * 2,
        out_specs=(vmem(),) * 2,
        compiler_params=params(8),
        cost_estimate=cost(0.05),
        name="join_grad",
    )(mine, got)


def join_out_kernel(sel, mine_ref, got_ref, out_ref):
    half = mine_ref.shape[1]
    at = pl.multiple_of(sel[0] * half, half)
    other = pl.multiple_of((1 - sel[0]) * half, half)
    out_ref[:, pl.ds(at, half)] = mine_ref[...].astype(BF16)
    out_ref[:, pl.ds(other, half)] = got_ref[...].astype(BF16)


def join_out(sel, mine, got):
    block, half = mine.shape
    return pl.pallas_call(
        join_out_kernel,
        out_shape=shaped((block, 2 * half), BF16),
        in_specs=[smem()] + [vmem()] * 2,
        out_specs=vmem(),
        compiler_params=params(8),
        cost_estimate=cost(0.05),
        name="join_out",
    )(sel, mine, got)


def fold_small(small):
    rows, cols = 6, small.shape[1] // 4
    tails = [small[i : i + 1, 3 * cols :] for i in range(rows)]
    last = [jnp.concatenate(tails[:3], axis=1), jnp.concatenate(tails[3:], axis=1)]
    return jnp.concatenate([small[0:rows, : 3 * cols]] + last, axis=0)


def finish_kernel(keep_ref, got_ref, a1_ref, a3_ref, small_ref, both_ref):
    part = keep_ref.shape[0]
    both_ref[0:part, :] = keep_ref[...] + got_ref[...] + a1_ref[...] + a3_ref[...]
    both_ref[part:, :] = fold_small(small_ref[...])


def finish(keep, got, a1, a3, small):
    part, cols3 = keep.shape
    return pl.pallas_call(
        finish_kernel,
        out_shape=shaped((part + 8, cols3)),
        in_specs=[vmem()] * 5,
        out_specs=vmem(),
        compiler_params=params(8),
        cost_estimate=cost(0.05),
        name="finish",
    )(keep, got, a1, a3, small)


def second_kernel(both_ref, px0_ref, py0_ref, corner_ref, z1_ref, z3_ref, z13_ref, zs_ref, cs_ref):
    part = z1_ref.shape[0] - 8
    z13_ref[0:part, :] = z1_ref[0:part, :]
    z13_ref[part:, :] = z3_ref[0:part, :]
    small = (both_ref[part:, :] + px0_ref[part:, :]) + (py0_ref[part:, :] + corner_ref[part:, :])
    for ref, out in ((z3_ref, zs_ref), (corner_ref, cs_ref)):
        out[0:part, :] = ref[0:part, :]
        out[part:, :] = small


def second(*pieces):
    part, cols3 = pieces[-1].shape[0] - 8, pieces[-1].shape[1]
    return pl.pallas_call(
        second_kernel,
        out_shape=(shaped((2 * part, cols3)),) + (shaped((part + 8, cols3)),) * 2,
        in_specs=[vmem()] * 6,
        out_specs=(vmem(),) * 3,
        compiler_params=params(10),
        cost_estimate=cost(0.05),
        name="second",
    )(*pieces)


def stack_kernel(*refs, rows):
    at = 0
    for ref, (first, count) in zip(refs, rows):
        refs[-1][at : at + count, :] = ref[first : first + count, :]
        at += count


def stack(*parts):
    rows = tuple((first, count) for _, first, count in parts)
    return pl.pallas_call(
        functools.partial(stack_kernel, rows=rows),
        out_shape=shaped((sum(count for _, count in rows), parts[0][0].shape[1])),
        in_specs=[vmem()] * len(parts),
        out_specs=vmem(),
        compiler_params=params(6),
        cost_estimate=cost(0.05),
        name="stack",
    )(*(array for array, _, _ in parts))


def small_kernel(*refs, where):
    pieces, outs = refs[:-6], refs[-6:]
    sums = [pieces[i][at : at + 8, :] for i, at in where]
    while len(sums) > 1:
        sums = [a + b for a, b in zip(sums[::2], sums[1::2])]
    total = sums[0]
    cols = total.shape[1] // 3
    for i, out in enumerate(outs):
        out[:, 0 : 3 * cols] = total[i : i + 1, :]
        out[:, 3 * cols :] = total[6 + i // 3 : 7 + i // 3, (i % 3) * cols : (i % 3 + 1) * cols]


def small_sums(pieces, where):
    width = pieces[0].shape[1] // 3 * 4
    return pl.pallas_call(
        functools.partial(small_kernel, where=where),
        out_shape=(shaped((1, width)),) * 6,
        in_specs=[vmem()] * len(pieces),
        out_specs=(vmem(),) * 6,
        compiler_params=params(8),
        cost_estimate=cost(0.05),
        name="small_sums",
    )(*pieces)


def place_kernel(sel, *refs, where, give):
    target, sem = refs[-2 - bool(give)], refs[-1]
    cols = refs[0].shape[1] // 3
    width = target.shape[1] // 3
    part = width // 8
    copies = []

    def copy(src, dst):
        copies.append(pltpu.make_async_copy(src, dst, sem.at[len(copies)]))
        copies[-1].start()

    for at, (array, first, rows, row, row_off, x_off, c_off) in enumerate(where):
        piece = refs[array].at[pl.ds(first, rows)]
        to_row = pl.multiple_of(row_part(sel, row) * part + row_off, 8)
        col = (2 * (sel[0] ^ x_off) + (sel[1] ^ c_off)) * cols
        for k in range(3):
            to = pl.multiple_of(col + k * width, cols)
            copy(piece.at[:, pl.ds(k * cols, cols)], target.at[pl.ds(to_row, rows), pl.ds(to, cols)])
        if at < give:
            copy(piece, refs[-2].at[pl.ds(at * part, part)])
    for c in copies:
        c.wait()


def place(sel, arrays, where, target, width, give, *waits):
    count = len(arrays)
    extra = [] if target is None else [target]
    cols3 = 3 * width // 4
    return pl.pallas_call(
        functools.partial(place_kernel, where=where, give=give),
        out_shape=(shaped((width, 3 * width)),)
        + ((shaped((give * width // 8, cols3)),) if give else ()),
        in_specs=[smem()]
        + [vmem()] * count
        + [hbm()] * len(extra)
        + [any_spec()] * len(waits),
        out_specs=(hbm(), vmem()) if give else (hbm(),),
        scratch_shapes=[pltpu.SemaphoreType.DMA((3 * len(where) + give,))],
        input_output_aliases={1 + count: 0} if extra else {},
        compiler_params=params(8),
        cost_estimate=cost(0.05),
        name="place",
    )(sel, *arrays, *extra, *waits)


def given(array, where):
    return [
        (array, i * rows, rows, row, row_off, x_off, 1)
        for i, (_, _, rows, row, row_off, x_off, _) in enumerate(where)
    ]


def on_device(
    tokens,
    offsets,
    w_proj,
    forget_weight,
    reset_weight,
    forget_bias,
    reset_bias,
    layer_norm_gain,
    layer_norm_bias,
    cotangent,
):
    _, block, width = tokens.shape
    z, y, x, c = (lax.axis_index(a) for a in ("z", "y", "x", "c"))
    tuned = lax.axis_size("z") == 4
    sel = jnp.stack([x, c, y, z]).astype(jnp.int32)
    part = width // 8

    cot = cotangent[0]
    own = tokens[0].astype(F32)
    own, *parts = lax.optimization_barrier(
        (own, *(own[first : first + rows] for first, rows in chunks(block)))
    )
    x_a, x_b, x_c = (swap(piece, "x") for piece in parts)
    tok_c = swap(own, "c")
    cot_sibling = swap(widen_cot(sel, cot), "c")
    cot_far = swap(pack_cot(sel, cot, cot_sibling), "x")

    gates = [
        v.reshape(1, width) for v in (forget_weight, reset_weight, forget_bias, reset_bias)
    ]
    gain = layer_norm_gain.reshape(1, width)
    vectors = (*gates, gain, layer_norm_bias.reshape(1, width))
    w_mine = take_weights(sel, w_proj)
    near = run_near(sel, offsets, (own, tok_c), w_mine, vectors)
    (x_a,) = hold((x_a,), near[5])
    xc_a = swap(x_a, "c")
    (x_b,) = hold((x_b,), xc_a)
    xc_b = swap(x_b, "c")
    early = run_early(sel, (x_a, xc_a, x_b, xc_b), w_mine, vectors)
    (x_c,) = hold((x_c,), early[0])
    xc_c = swap(x_c, "c")
    far = run_forward(sel, (x_c, xc_c), near[2:], early, w_mine, vectors)
    normed = (near[0], far[0])
    toks = (own, tok_c, x_a, xc_a, x_b, xc_b, x_c, xc_c)
    if tuned:
        rows = [[[(d, 1)] for d in (2, 3, 1, 0)], [[(d, 0)] for d in (2, 3, 1, 0)]]
    else:
        rows = [[[0], [1], [2], [3]], [[4], [5], [6], [7]]]
    dproj, out, dxh, gate_small, s2 = run_backward(
        sel, toks, (cot, cot_sibling, cot_far), far[2:], near[5], gates, normed, rows[0][:1]
    )
    s1, s3, k2 = run_products(sel, normed, dproj, (rows[0][2], rows[0][1], rows[1][0]))
    grad_mine, grad_send = run_input(
        sel, toks, (near[1], far[1]), dproj, dxh, out, gate_small, w_mine, gain
    )
    late = (rows[0][3], *rows[1][1:])

    if tuned:
        s0, k3, k1, k0 = run_products(sel, normed, dproj, late)
        q2 = add(k2, swap(s2, "y"), s3, s0, grad_send)
        r3 = swap(s3, "y")
        r0 = swap(add(s0, xor_permute(s1, "z", 1), q2), "y")
        a2 = xor_permute(q2, "z", 1)
        h3 = add(add(k3, r3), a2)
        a3 = xor_permute(h3, "z", 3)
        kept, kept_out, sent, sent_out, small = combine(
            sel, grad_mine, swap(grad_send, "c"), q2, tick(grad_send)
        )
        got = swap(sent, "x")
        a1 = xor_permute(k1, "z", 1)
        both = finish(k0, r0, a1, a3, small)
        input_grad, joined = join_grad(kept, got)

        px0, z3, z1, py0 = (
            swap(both, "x"),
            xor_permute(both, "z", 3),
            xor_permute(both, "z", 1),
            swap(both, "y"),
        )
        (px0,) = hold((px0,), joined)
        corner0 = swap(px0, "y")
        (sent_out,) = hold((sent_out,), px0)
        got_out = swap(sent_out, "x")
        z3, z1, corner0, py0, got_out = hold((z3, z1, corner0, py0, got_out))
        output = join_out(sel, kept_out, got_out)
        full = part + 8
        z13, zs, cs = second(both, px0, py0, corner0, z1, z3)
        z2, px13, py13 = xor_permute(zs, "z", 1), swap(z13, "x"), swap(z13, "y")
        corner3 = xor_permute(cs, "z", 3)
        own = [
            (0, 0, part, (0, 0), 0, 0, 0),
            (1, 0, part, (0, 0), 0, 1, 0),
            (2, 0, part, (0, 1), 0, 0, 0),
            (3, 0, part, (0, 1), 0, 1, 0),
        ]
        proj_grad, give = place(sel, (both, px0, py0, corner0), own, None, width, 4)
        z2, px13, py13, corner3 = hold((z2, px13, py13, corner3), give)
        by_x, by_y = part // 4, 3 * part // 8
        rest = part - by_x - by_y
        px2 = swap(stack((z2, 0, part), (py13, 0, by_x)), "x")
        py2 = swap(stack((z2, 0, part), (px13, by_x, by_y)), "y")
        corner12 = xor_permute(
            stack((corner3, 0, part), (corner0, by_x + by_y, rest), (corner3, part, 8)), "z", 1
        )
        other = given(3, own)
        own = [
            (array, part * i, part, (d, y_off), 0, x_off, 0)
            for array, y_off, x_off in ((0, 0, 0), (1, 0, 1), (2, 1, 0))
            for i, d in ((0, 1), (1, 3))
        ]
        proj_grad, give = place(
            sel,
            (z13, px13, py13, swap(give, "c")),
            own + other,
            proj_grad,
            width,
            6,
            tick(give, corner3),
        )
        other = given(3, own)
        first_give, marked = swap(give, "c"), give
        own = [(0, 0, part, (2, 0), 0, 0, 0), (1, 0, part, (3, 1), 0, 1, 0)]
        proj_grad, give = place(sel, (z2, corner3), own, proj_grad, width, 2)
        other += given(4, own)
        px2, py2, corner12 = hold((px2, py2, corner12), give)
        own = [
            (0, 0, part, (2, 0), 0, 1, 0),
            (0, part, by_x, (1, 1), 0, 1, 0),
            (1, 0, part, (2, 1), 0, 0, 0),
            (1, part, by_y, (1, 1), by_x, 1, 0),
            (2, 0, part, (2, 1), 0, 1, 0),
            (2, part, rest, (1, 1), by_x + by_y, 1, 0),
        ]
        arrays = (px2, py2, corner12, first_give, swap(give, "c"))
        (proj_grad,) = place(
            sel, arrays, own + other, proj_grad, width, 0, tick(marked, give, px2)
        )
        own = [(*place_of[:-1], 1) for place_of in own]
        arrays = [swap(a, "c") for a in (px2, py2, corner12)]
        (proj_grad,) = place(sel, arrays, own, proj_grad, width, 0)
        where = [(0, part), (1, part), (2, part + rest), (3, part)]
        small = small_sums((zs, z2, corner12, corner3), where)
    else:
        s0, k3, k1, k0 = run_products(sel, normed, dproj, late)
        kept, kept_out, sent, sent_out, small = combine(sel, grad_mine, swap(grad_send, "c"))
        input_grad, _ = join_grad(kept, swap(sent, "x"))
        output = join_out(sel, kept_out, swap(sent_out, "x"))
        small = lax.psum(small + swap(small, "x"), ("z", "y"))
        pieces = jnp.stack([s2, s3, s1, s0, k2, k3, k1, k0])
        pieces = lax.psum(pieces, ("z", "y"))
        proj_grad = None
        for x_off, held in ((0, pieces), (1, swap(pieces, "x"))):
            own = [(r, 0, part, r, 0, x_off, 0) for r in range(8)]
            proj_grad, give = place(sel, list(held), own, proj_grad, width, 8)
            other = given(0, own)
            (proj_grad,) = place(sel, [swap(give, "c")], other, proj_grad, width, 0)
    small = [small[i].reshape(width) for i in range(6)]
    return (output[None], input_grad[None], proj_grad, *small)


def solution(mesh):
    dp, rep = mesh.shape["dp"], mesh.shape["rep"]
    fine = Mesh(mesh.devices.reshape(dp // 2, 2, rep // 2, 2), ("z", "y", "x", "c"))
    row, seq = ("z", "y"), ("x", "c")
    in_specs = (P(row, seq, None), P(row, None)) + (P(),) * 7 + (P(row, seq, None),)
    out_specs = (P(row, seq, None), P(row, seq, None)) + (P(),) * 7
    return jax.shard_map(
        on_device, mesh=fine, in_specs=in_specs, out_specs=out_specs, check_vma=False
    )
```

```python
import functools

import jax
import jax.numpy as jnp
from jax import lax
from jax.experimental import pallas as pl
from jax.experimental.pallas import tpu as pltpu
from jax.sharding import Mesh
from jax.sharding import PartitionSpec as P

EPS = 1e-05
LANES = 128
SWAP = [(0, 1), (1, 0)]
VMEM_BYTES = 56 * 2**20
F32 = jnp.float32
BF16 = jnp.bfloat16


def swap(block, axis):
    return lax.ppermute(block, axis, SWAP)


def xor_permute(block, axis, distance):
    size = lax.axis_size(axis)
    return lax.ppermute(block, axis, [(i, i ^ distance) for i in range(size)])


def any_spec():
    return pl.BlockSpec(memory_space=pl.ANY)


def hbm():
    return pl.BlockSpec(memory_space=pltpu.HBM)


def vmem():
    return pl.BlockSpec(memory_space=pltpu.VMEM)


def smem():
    return pl.BlockSpec(memory_space=pltpu.SMEM)


def shaped(shape, dtype=F32):
    return jax.ShapeDtypeStruct(shape, dtype)


def params(mib):
    return pltpu.CompilerParams(vmem_limit_bytes=mib * 2**20)


def cost(us):
    return pl.CostEstimate(
        flops=int(us * 1.1e9), bytes_accessed=int(us * 3.6e6), transcendentals=0
    )


def own_columns(sel, cols):
    return pl.ds(pl.multiple_of((2 * sel[0] + sel[1]) * cols, cols), cols)


def stored_at(sel, k):
    return 2 * ((k // 2) ^ sel[0]) + ((k % 2) ^ sel[1])


def chunks(block):
    unit = block // 88 * 16
    sizes = (unit, 2 * unit, block - 3 * unit)
    return tuple((sum(sizes[:i]), size) for i, size in enumerate(sizes))


def segments(block):
    far = [(b, first, rows) for first, rows in chunks(block) for b in (2, 3)]
    return ((0, 0, block), (1, 0, block), *far)


def stretches(sel, block, k):
    held = stored_at(sel, k)
    near = held < 2
    return tuple(
        (jnp.where(near, held * block + first, 2 * (block + first) + (held - 2) * rows), rows)
        for first, rows in chunks(block)
    )


def row_part(sel, row):
    return row if isinstance(row, int) else 2 * (sel[3] ^ row[0]) + (sel[2] ^ row[1])


def tick_kernel(*refs):
    refs[-1][...] = jnp.zeros(refs[-1].shape, F32)


def tick(*values):
    return pl.pallas_call(
        tick_kernel,
        out_shape=shaped((8, 128)),
        in_specs=[any_spec()] * len(values),
        out_specs=vmem(),
        compiler_params=params(1),
        cost_estimate=cost(20),
        name="tick",
    )(*values)


def hold_kernel(*refs):
    del refs


def hold(values, *waits):
    count = len(values)
    return pl.pallas_call(
        hold_kernel,
        out_shape=tuple(shaped(v.shape, v.dtype) for v in values),
        in_specs=[any_spec()] * (count + len(waits)),
        out_specs=(any_spec(),) * count,
        input_output_aliases={i: i for i in range(count)},
        compiler_params=params(1),
        cost_estimate=cost(0.05),
        name="hold",
    )(*values, *waits)


def add_kernel(a_ref, b_ref, *refs):
    refs[-1][...] = a_ref[...] + b_ref[...]


def add(a, b, *waits):
    return pl.pallas_call(
        add_kernel,
        out_shape=shaped(a.shape),
        in_specs=[vmem()] * 2 + [any_spec()] * len(waits),
        out_specs=vmem(),
        compiler_params=params(4),
        cost_estimate=cost(0.05),
        name="add",
    )(a, b, *waits)


def take_weights_kernel(sel, w_ref, mine_ref, sem):
    width, cols = mine_ref.shape[0], mine_ref.shape[1] // 3
    copies = []
    for k in range(3):
        at = pl.multiple_of((2 * sel[0] + sel[1]) * cols + k * width, cols)
        copies.append(
            pltpu.make_async_copy(
                w_ref.at[:, pl.ds(at, cols)], mine_ref.at[:, k * cols : (k + 1) * cols], sem.at[k]
            )
        )
    for c in copies:
        c.start()
    for c in copies:
        c.wait()


def take_weights(sel, w_proj):
    width = w_proj.shape[0]
    return pl.pallas_call(
        take_weights_kernel,
        out_shape=shaped((width, 3 * width // 4), BF16),
        in_specs=[smem(), hbm()],
        out_specs=vmem(),
        scratch_shapes=[pltpu.SemaphoreType.DMA((3,))],
        compiler_params=params(4),
        cost_estimate=cost(0.05),
        name="take_weights",
    )(sel, w_proj)


def widen_cot_kernel(sel, cot_ref, cot_out):
    cols = cot_ref.shape[1] // 4
    for k in range(2):
        at = pl.multiple_of((2 * k + 1 - sel[1]) * cols, cols)
        cot_out[:, k * cols : (k + 1) * cols] = cot_ref[:, pl.ds(at, cols)].astype(F32)


def widen_cot(sel, cot):
    return pl.pallas_call(
        widen_cot_kernel,
        out_shape=shaped((cot.shape[0], cot.shape[1] // 2)),
        in_specs=[smem(), vmem()],
        out_specs=vmem(),
        compiler_params=params(4),
        cost_estimate=cost(0.05),
        name="widen_cot",
    )(sel, cot)


def pack_cot_kernel(sel, cot_ref, sibling_ref, cot_out):
    block, cols = cot_ref.shape[0], cot_ref.shape[1] // 4
    mine = pl.multiple_of((2 * (1 - sel[0]) + sel[1]) * cols, cols)
    cot_out[0:block, :] = cot_ref[:, pl.ds(mine, cols)].astype(F32)
    sibling = pl.multiple_of((1 - sel[0]) * cols, cols)
    cot_out[block:, :] = sibling_ref[:, pl.ds(sibling, cols)]


def pack_cot(sel, cot, sibling):
    return pl.pallas_call(
        pack_cot_kernel,
        out_shape=shaped((2 * cot.shape[0], cot.shape[1] // 4)),
        in_specs=[smem(), vmem(), vmem()],
        out_specs=vmem(),
        compiler_params=params(4),
        cost_estimate=cost(0.05),
        name="pack_cot",
    )(sel, cot, sibling)


def standardized(x):
    mean = jnp.mean(x, axis=-1, keepdims=True)
    centred = x - mean
    rdev = lax.rsqrt(jnp.mean(centred * centred, axis=-1, keepdims=True) + EPS)
    return centred * rdev, mean, rdev


def norm_and_project(sel, toks, norm, w_ref, gates, normed, stats, cand, zf, zr, first, base):
    cols = cand.shape[1]
    mine = own_columns(sel, cols)
    gain, bias = norm[0][...], norm[1][...]
    fb, rb = gates[2][:, mine], gates[3][:, mine]
    step = 16
    at = first
    for tok in toks:

        def body(i, carry, tok=tok, at=at):
            here = pl.ds(pl.multiple_of(i * step, step), step)
            there = pl.ds(pl.multiple_of(at + i * step, step), step)
            xhat, mean, rdev = standardized(tok[here, :])
            normed[there, :] = (xhat * gain + bias).astype(BF16)
            stats[there, 0:LANES] = jnp.broadcast_to(mean, (step, LANES))
            stats[there, LANES:] = jnp.broadcast_to(rdev, (step, LANES))
            return carry

        lax.fori_loop(0, tok.shape[0] // step, body, 0, unroll=True)
        at += tok.shape[0]
    rows = normed[first:at, :]
    here = slice(base, base + at - first)
    part = lambda k: jnp.dot(
        rows, w_ref[:, k * cols : (k + 1) * cols], preferred_element_type=F32
    )
    cand[here, :] = part(0)
    zf[here, :] = 0.5 * (part(1) + fb)
    zr[here, :] = 0.5 * (part(2) + rb)


def near_kernel(sel, offsets, tok0, tok1, w_ref, *refs):
    gates, norm, (normed, stats, cand, zf, zr, half_keep) = refs[:4], refs[4:6], refs[6:]
    length, cols = half_keep.shape
    block = length // 4
    step = 16
    row = 0
    for b, first, rows in segments(block):
        base = stored_at(sel, b) * block + first

        def body(i, carry, row=row, base=base):
            at = pl.multiple_of(i * step, step)
            token = base + at + lax.broadcasted_iota(jnp.int32, (step, cols), 0)
            starts = token == offsets[0, 0]
            for k in range(1, offsets.shape[1]):
                starts = starts | (token == offsets[0, k])
            half_keep[pl.ds(pl.multiple_of(row + at, step), step), :] = jnp.where(starts, 0.0, 0.5)
            return carry

        lax.fori_loop(0, rows // step, body, 0)
        row += rows
    norm_and_project(sel, (tok0, tok1), norm, w_ref, gates, normed, stats, cand, zf, zr, 0, 0)


def run_near(sel, offsets, toks, w_mine, vectors):
    block, width = toks[0].shape
    cols = width // 4
    return pl.pallas_call(
        near_kernel,
        out_shape=(shaped((2 * block, width), BF16), shaped((2 * block, 2 * LANES)))
        + (shaped((2 * block, cols)),) * 3
        + (shaped((4 * block, cols)),),
        in_specs=[smem()] * 2 + [vmem()] * 9,
        out_specs=(vmem(),) * 6,
        compiler_params=params(16),
        cost_estimate=cost(0.05),
        name="near_blocks",
    )(sel, offsets, *toks, w_mine, *vectors)


def early_kernel(sel, *refs, count):
    toks, w_ref, refs = refs[:count], refs[count], refs[count + 1 :]
    gates, norm, (normed, stats, cand, zf, zr) = refs[:4], refs[4:6], refs[-5:]
    norm_and_project(sel, toks, norm, w_ref, gates, normed, stats, cand, zf, zr, 0, 0)


def run_early(sel, toks, w_mine, vectors):
    rows, width = sum(tok.shape[0] for tok in toks), toks[0].shape[1]
    cols = width // 4
    return pl.pallas_call(
        functools.partial(early_kernel, count=len(toks)),
        out_shape=(shaped((rows, width), BF16), shaped((rows, 2 * LANES)))
        + (shaped((rows, cols)),) * 3,
        in_specs=[smem()] + [vmem()] * (7 + len(toks)),
        out_specs=(vmem(),) * 5,
        compiler_params=params(12),
        cost_estimate=cost(0.05),
        name="early_blocks",
    )(sel, *toks, w_mine, *vectors)


def forward_kernel(
    sel,
    tok0,
    tok1,
    cand_near,
    zf_near,
    zr_near,
    half_keep,
    normed_early,
    stats_early,
    cand_early,
    zf_early,
    zr_early,
    w_ref,
    *refs,
):
    gates, norm, (normed, stats, cand, zf, zr, state, half_prev) = refs[:4], refs[4:6], refs[6:]
    length, cols = cand.shape
    block = length // 4
    early = normed_early.shape[0]
    normed[0:early, :] = normed_early[...]
    stats[0:early, :] = stats_early[...]
    first = 2 * block
    near, mid = slice(0, first), slice(first, first + early)
    cand[near, :], zf[near, :], zr[near, :] = cand_near[...], zf_near[...], zr_near[...]
    cand[mid, :], zf[mid, :], zr[mid, :] = cand_early[...], zf_early[...], zr_early[...]
    fw = gates[0][:, own_columns(sel, cols)]
    norm_and_project(
        sel, (tok0, tok1), norm, w_ref, gates, normed, stats, cand, zf, zr, early, first + early
    )
    zero = jnp.zeros((1, cols), F32)
    carry = (zero, zero, zero)
    for k in range(4):
        for base, rows in stretches(sel, block, k):

            def body(i, carry, base=base):
                middle, spread, th = carry
                row = pl.ds(base + i, 1)
                half = half_keep[row, :]
                weight = half * fw
                last = middle + spread * th
                th = jnp.tanh((zf[row, :] + weight * middle) + (weight * spread) * th)
                hp = half * last
                hc = 0.5 * cand[row, :]
                middle, spread = hp + hc, hp - hc
                state[row, :] = middle + spread * th
                half_prev[row, :] = hp
                return (middle, spread, th)

            carry = lax.fori_loop(0, rows, body, carry, unroll=16)


def run_forward(sel, toks, near, early, w_mine, vectors):
    late, width = toks[0].shape
    cols = width // 4
    length = near[-1].shape[0]
    return pl.pallas_call(
        forward_kernel,
        out_shape=(shaped((length // 2, width), BF16), shaped((length // 2, 2 * LANES)))
        + (shaped((length, cols)),) * 5,
        in_specs=[smem()] + [vmem()] * 18,
        out_specs=(vmem(),) * 7,
        compiler_params=params(20),
        cost_estimate=cost(0.05),
        name="forward_scan",
    )(sel, *toks, *near, *early, w_mine, *vectors)


def backward_kernel(sel, *refs, rows, count):
    toks, refs = refs[:count], refs[count:]
    (g0, g1, g23, cand_ref, zf_ref, zr_ref, state, half_prev), refs = refs[:8], refs[8:]
    (half_keep, fw_ref, rw_ref, near_ref, far_ref), refs = refs[:5], refs[5:]
    (dproj_ref, out_ref, dxh_ref, small_ref), refs = refs[:4], refs[4:]
    products, (coef, add, add_e, gz, omf, states) = refs[: len(rows)], refs[len(rows) :]
    length, cols = cand_ref.shape
    block = length // 4
    mine = own_columns(sel, cols)
    half = pl.ds(pl.multiple_of(sel[0] * cols, cols), cols)
    fw, rw = fw_ref[:, mine], rw_ref[:, mine]
    half_fw, half_rw = 0.5 * fw, 0.5 * rw
    step = 16
    zero = jnp.zeros((step, cols), F32)
    sums = (zero, zero)
    everything = slice(0, cols)
    grads = ((g0, 0, mine), (g1, 0, half), (g23, 0, everything), (g23, block, everything))
    row = 0
    for x_ref, (b, first, count) in zip(toks, segments(block)):
        g_ref, g_at, g_cols = grads[b]

        def gate_body(
            i, carry, row=row, x_ref=x_ref, g_ref=g_ref, g_at=g_at + first, g_cols=g_cols
        ):
            at = pl.multiple_of(i * step, step)
            here = pl.ds(pl.multiple_of(row + at, step), step)
            x = x_ref[pl.ds(at, step), mine]
            g = g_ref[pl.ds(pl.multiple_of(g_at + at, step), step), g_cols].astype(F32)
            keep = 2.0 * half_keep[here, :]
            prev = 2.0 * half_prev[here, :]
            c, cd = state[here, :], cand_ref[here, :]
            forget = 0.5 + 0.5 * jnp.tanh(zf_ref[here, :] + half_fw * prev)
            reset = 0.5 + 0.5 * jnp.tanh(zr_ref[here, :] + half_rw * prev)
            not_forget, not_reset = 1.0 - forget, 1.0 - reset
            out_ref[here, :] = reset * c + not_reset * x
            dxh_ref[here, :] = g * not_reset
            dzr = g * (c - x) * reset * not_reset
            slope = (prev - cd) * forget * not_forget
            back, extra = keep * (forget + slope * fw), g * reset
            coef[here, :] = back
            add[here, :] = back * extra + keep * (dzr * rw)
            add_e[here, :] = extra
            gz[here, :] = slope
            omf[here, :] = not_forget
            dproj_ref[here, 2 * cols : 3 * cols] = dzr.astype(BF16)
            return (carry[0] + dzr * prev, carry[1] + dzr)

        sums = lax.fori_loop(0, count // step, gate_body, sums, unroll=True)
        row += count
    rw_sum, rb_sum = sums

    dc = jnp.zeros((1, cols), F32)
    group = 8
    for k in range(3, -1, -1):
        for first, count in reversed(stretches(sel, block, k)):

            def backward_body(i, dc, end=first + count):
                base = pl.multiple_of(end - (i + 1) * group, group)
                for r in range(group - 1, -1, -1):
                    row = pl.ds(base + r, 1)
                    states[row, :] = dc
                    dc = coef[row, :] * dc + add[row, :]
                return dc

            dc = lax.fori_loop(0, count // group, backward_body, dc, unroll=2)

    def grad_body(i, carry):
        here = pl.ds(pl.multiple_of(i * step, step), step)
        total = states[here, :] + add_e[here, :]
        prev = 2.0 * half_prev[here, :]
        dzf = total * gz[here, :]
        dproj_ref[here, 0:cols] = (total * omf[here, :]).astype(BF16)
        dproj_ref[here, cols : 2 * cols] = dzf.astype(BF16)
        return (carry[0] + dzf * prev, carry[1] + dzf)

    fw_sum, fb_sum = lax.fori_loop(0, length // step, grad_body, (zero, zero), unroll=4)
    small_ref[...] = jnp.concatenate(
        [jnp.sum(v, axis=0, keepdims=True) for v in (fw_sum, rw_sum, fb_sum, rb_sum)]
        + [jnp.zeros((4, cols), F32)],
        axis=0,
    )
    outer_products(sel, rows, near_ref, far_ref, dproj_ref, products)


def outer_products(sel, rows, near_ref, far_ref, dproj_ref, outs):
    half, width = near_ref.shape
    part = width // 8
    dims = (((0,), (0,)), ((), ()))
    for out, places in zip(outs, rows):
        for k, place_of in enumerate(places):
            at = pl.ds(pl.multiple_of(row_part(sel, place_of) * part, part), part)
            out[k * part : (k + 1) * part, :] = lax.dot_general(
                near_ref[:, at], dproj_ref[0:half, :], dims, preferred_element_type=F32
            ) + lax.dot_general(
                far_ref[:, at], dproj_ref[half:, :], dims, preferred_element_type=F32
            )


def product_shapes(width, rows):
    return tuple(shaped((len(places) * width // 8, 3 * width // 4)) for places in rows)


def run_backward(sel, toks, cots, scanned, half_keep, gates, normed, rows):
    length, cols = half_keep.shape
    width = 4 * cols
    return pl.pallas_call(
        functools.partial(backward_kernel, rows=rows, count=len(toks)),
        out_shape=(
            shaped((length, 3 * cols), BF16),
            shaped((length, cols)),
            shaped((length, cols)),
            shaped((8, cols)),
        )
        + product_shapes(width, rows),
        in_specs=[smem()] + [vmem()] * (13 + len(toks)),
        out_specs=(vmem(),) * (4 + len(rows)),
        scratch_shapes=[pltpu.VMEM((length, cols), F32)] * 6,
        compiler_params=params(24),
        cost_estimate=cost(0.05),
        name="backward_scan",
    )(sel, *toks, *cots, *scanned, half_keep, *gates[:2], *normed)


def products_kernel(sel, near_ref, far_ref, dproj_ref, *outs, rows):
    outer_products(sel, rows, near_ref, far_ref, dproj_ref, outs[-len(rows) :])


def run_products(sel, normed, dproj, rows, *waits):
    return pl.pallas_call(
        functools.partial(products_kernel, rows=rows),
        out_shape=product_shapes(normed[0].shape[1], rows),
        in_specs=[smem()] + [vmem()] * 3 + [any_spec()] * len(waits),
        out_specs=(vmem(),) * len(rows),
        compiler_params=params(12),
        cost_estimate=cost(0.05),
        name="products",
    )(sel, *normed, dproj, *waits)


def input_kernel(sel, *refs, count):
    toks, (mine_ref, send_ref, dnormed) = refs[:count], refs[-3:]
    (stats_near, stats_far, dproj_ref, dxh_ref, out_ref), refs = refs[count : count + 5], refs[count + 5 :]
    gate_small_ref, w_ref, gain_ref = refs[:3]
    cols = dxh_ref.shape[1]
    block, width = toks[0].shape
    gain = gain_ref[...]
    mine = own_columns(sel, cols)
    step = 16
    sums = (jnp.zeros((step, width), F32), jnp.zeros((step, width), F32))
    row = 0
    for tok, (b, first, count) in zip(toks, segments(block)):
        if row % (2 * block) == 0:
            dnormed[...] = lax.dot_general(
                dproj_ref[row : row + 2 * block, :],
                w_ref[...],
                (((1,), (1,)), ((), ())),
                preferred_element_type=F32,
            )
        rows = slice(row, row + count)
        where = send_ref if b % 2 else mine_ref
        base = (b // 2) * block + first
        stats, at = (stats_near, row) if b < 2 else (stats_far, row - 2 * block)

        def body(i, carry, tok=tok, base=base, where=where, stats=stats, at=at):
            here = pl.ds(pl.multiple_of(i * step, step), step)
            there = pl.ds(pl.multiple_of(base + i * step, step), step)
            kept = pl.ds(pl.multiple_of(at + i * step, step), step)
            mean, rdev = (
                jnp.concatenate([stats[kept, k : k + LANES]] * (width // LANES), axis=1)
                for k in (0, LANES)
            )
            xhat = (tok[here, :] - mean) * rdev
            dn = dnormed[kept, :]
            dxhat = dn * gain
            mean1 = jnp.mean(dxhat, axis=-1, keepdims=True)
            mean2 = jnp.mean(dxhat * xhat, axis=-1, keepdims=True)
            where[there, 0:width] = rdev * (dxhat - mean1 - xhat * mean2)
            return (carry[0] + dn * xhat, carry[1] + dn)

        sums = lax.fori_loop(0, count // step, body, sums, unroll=True if count < block else 11)
        to = pl.ds(base, count)
        where[to, mine] += dxh_ref[rows, :]
        where[to, width : width + cols] = out_ref[rows, :]
        row += count
    tail = slice(2 * block, 2 * block + 8)
    mine_ref[tail, :] = jnp.zeros((8, width + cols), F32)
    mine_ref[2 * block : 2 * block + 4, mine] = gate_small_ref[0:4, :]
    for i, v in enumerate(sums):
        row = 2 * block + 4 + i
        mine_ref[row : row + 1, 0:width] = jnp.sum(v, axis=0, keepdims=True)
    send_ref[tail, :] = mine_ref[tail, :]


def run_input(sel, toks, stats, dproj, dxh, out, gate_small, w_mine, gain, *waits):
    block, width = toks[0].shape
    shape = (2 * block + 8, width + width // 4)
    return pl.pallas_call(
        functools.partial(input_kernel, count=len(toks)),
        out_shape=(shaped(shape), shaped(shape)),
        in_specs=[smem()] + [vmem()] * (8 + len(toks)) + [any_spec()] * len(waits),
        out_specs=(vmem(),) * 2,
        scratch_shapes=[pltpu.VMEM((2 * block, width), F32)],
        compiler_params=params(20),
        cost_estimate=cost(0.05),
        name="input_side",
    )(sel, *toks, *stats, dproj, dxh, out, gate_small, w_mine, gain, *waits)


def combine_kernel(sel, mine_ref, got_ref, *refs):
    keep_grad, keep_out, send_grad, send_out, small_ref = refs[-5:]
    block, width = keep_grad.shape
    cols = width // 4
    low = pl.ds(pl.multiple_of(sel[1] * cols, cols), cols)
    high = pl.ds(pl.multiple_of((1 - sel[1]) * cols, cols), cols)
    for grad, out, first in ((keep_grad, keep_out, 0), (send_grad, send_out, block)):
        here = slice(first, first + block)
        grad[...] = mine_ref[here, 0:width] + got_ref[here, 0:width]
        out[:, low] = mine_ref[here, width:]
        out[:, high] = got_ref[here, width:]
    small_ref[...] = mine_ref[2 * block :, 0:width] + got_ref[2 * block :, 0:width]


def combine(sel, mine, got, *waits):
    block, width = (mine.shape[0] - 8) // 2, mine.shape[1] * 4 // 5
    return pl.pallas_call(
        combine_kernel,
        out_shape=(shaped((block, width)), shaped((block, width // 2))) * 2 + (shaped((8, width)),),
        in_specs=[smem(), vmem(), vmem()] + [any_spec()] * len(waits),
        out_specs=(vmem(),) * 5,
        compiler_params=params(16),
        cost_estimate=cost(0.05),
        name="combine",
    )(sel, mine, got, *waits)


def join_grad_kernel(mine_ref, got_ref, grad_ref, done_ref):
    done_ref[...] = jnp.zeros(done_ref.shape, F32)
    grad_ref[...] = (mine_ref[...] + got_ref[...]).astype(BF16)


def join_grad(mine, got):
    return pl.pallas_call(
        join_grad_kernel,
        out_shape=(shaped(mine.shape, BF16), shaped((8, LANES))),
        in_specs=[vmem()] * 2,
        out_specs=(vmem(),) * 2,
        compiler_params=params(8),
        cost_estimate=cost(0.05),
        name="join_grad",
    )(mine, got)


def join_out_kernel(sel, mine_ref, got_ref, out_ref):
    half = mine_ref.shape[1]
    at = pl.multiple_of(sel[0] * half, half)
    other = pl.multiple_of((1 - sel[0]) * half, half)
    out_ref[:, pl.ds(at, half)] = mine_ref[...].astype(BF16)
    out_ref[:, pl.ds(other, half)] = got_ref[...].astype(BF16)


def join_out(sel, mine, got):
    block, half = mine.shape
    return pl.pallas_call(
        join_out_kernel,
        out_shape=shaped((block, 2 * half), BF16),
        in_specs=[smem()] + [vmem()] * 2,
        out_specs=vmem(),
        compiler_params=params(8),
        cost_estimate=cost(0.05),
        name="join_out",
    )(sel, mine, got)


def fold_small(small):
    rows, cols = 6, small.shape[1] // 4
    tails = [small[i : i + 1, 3 * cols :] for i in range(rows)]
    last = [jnp.concatenate(tails[:3], axis=1), jnp.concatenate(tails[3:], axis=1)]
    return jnp.concatenate([small[0:rows, : 3 * cols]] + last, axis=0)


def finish_kernel(keep_ref, got_ref, a1_ref, a3_ref, small_ref, both_ref):
    part = keep_ref.shape[0]
    both_ref[0:part, :] = keep_ref[...] + got_ref[...] + a1_ref[...] + a3_ref[...]
    both_ref[part:, :] = fold_small(small_ref[...])


def finish(keep, got, a1, a3, small):
    part, cols3 = keep.shape
    return pl.pallas_call(
        finish_kernel,
        out_shape=shaped((part + 8, cols3)),
        in_specs=[vmem()] * 5,
        out_specs=vmem(),
        compiler_params=params(8),
        cost_estimate=cost(0.05),
        name="finish",
    )(keep, got, a1, a3, small)


def second_kernel(both_ref, px0_ref, py0_ref, corner_ref, z1_ref, z3_ref, z13_ref, zs_ref, cs_ref):
    part = z1_ref.shape[0] - 8
    z13_ref[0:part, :] = z1_ref[0:part, :]
    z13_ref[part:, :] = z3_ref[0:part, :]
    small = (both_ref[part:, :] + px0_ref[part:, :]) + (py0_ref[part:, :] + corner_ref[part:, :])
    for ref, out in ((z3_ref, zs_ref), (corner_ref, cs_ref)):
        out[0:part, :] = ref[0:part, :]
        out[part:, :] = small


def second(*pieces):
    part, cols3 = pieces[-1].shape[0] - 8, pieces[-1].shape[1]
    return pl.pallas_call(
        second_kernel,
        out_shape=(shaped((2 * part, cols3)),) + (shaped((part + 8, cols3)),) * 2,
        in_specs=[vmem()] * 6,
        out_specs=(vmem(),) * 3,
        compiler_params=params(10),
        cost_estimate=cost(0.05),
        name="second",
    )(*pieces)


def stack_kernel(*refs, rows):
    at = 0
    for ref, (first, count) in zip(refs, rows):
        refs[-1][at : at + count, :] = ref[first : first + count, :]
        at += count


def stack(*parts):
    rows = tuple((first, count) for _, first, count in parts)
    return pl.pallas_call(
        functools.partial(stack_kernel, rows=rows),
        out_shape=shaped((sum(count for _, count in rows), parts[0][0].shape[1])),
        in_specs=[vmem()] * len(parts),
        out_specs=vmem(),
        compiler_params=params(6),
        cost_estimate=cost(0.05),
        name="stack",
    )(*(array for array, _, _ in parts))


def small_kernel(*refs, where):
    pieces, outs = refs[:-6], refs[-6:]
    sums = [pieces[i][at : at + 8, :] for i, at in where]
    while len(sums) > 1:
        sums = [a + b for a, b in zip(sums[::2], sums[1::2])]
    total = sums[0]
    cols = total.shape[1] // 3
    for i, out in enumerate(outs):
        out[:, 0 : 3 * cols] = total[i : i + 1, :]
        out[:, 3 * cols :] = total[6 + i // 3 : 7 + i // 3, (i % 3) * cols : (i % 3 + 1) * cols]


def small_sums(pieces, where):
    width = pieces[0].shape[1] // 3 * 4
    return pl.pallas_call(
        functools.partial(small_kernel, where=where),
        out_shape=(shaped((1, width)),) * 6,
        in_specs=[vmem()] * len(pieces),
        out_specs=(vmem(),) * 6,
        compiler_params=params(8),
        cost_estimate=cost(0.05),
        name="small_sums",
    )(*pieces)


def place_kernel(sel, *refs, where, give):
    target, sem = refs[-2 - bool(give)], refs[-1]
    cols = refs[0].shape[1] // 3
    width = target.shape[1] // 3
    part = width // 8
    copies = []

    def copy(src, dst):
        copies.append(pltpu.make_async_copy(src, dst, sem.at[len(copies)]))
        copies[-1].start()

    for at, (array, first, rows, row, row_off, x_off, c_off) in enumerate(where):
        piece = refs[array].at[pl.ds(first, rows)]
        to_row = pl.multiple_of(row_part(sel, row) * part + row_off, 8)
        col = (2 * (sel[0] ^ x_off) + (sel[1] ^ c_off)) * cols
        for k in range(3):
            to = pl.multiple_of(col + k * width, cols)
            copy(piece.at[:, pl.ds(k * cols, cols)], target.at[pl.ds(to_row, rows), pl.ds(to, cols)])
        if at < give:
            copy(piece, refs[-2].at[pl.ds(at * part, part)])
    for c in copies:
        c.wait()


def place(sel, arrays, where, target, width, give, *waits):
    count = len(arrays)
    extra = [] if target is None else [target]
    cols3 = 3 * width // 4
    return pl.pallas_call(
        functools.partial(place_kernel, where=where, give=give),
        out_shape=(shaped((width, 3 * width)),)
        + ((shaped((give * width // 8, cols3)),) if give else ()),
        in_specs=[smem()]
        + [vmem()] * count
        + [hbm()] * len(extra)
        + [any_spec()] * len(waits),
        out_specs=(hbm(), vmem()) if give else (hbm(),),
        scratch_shapes=[pltpu.SemaphoreType.DMA((3 * len(where) + give,))],
        input_output_aliases={1 + count: 0} if extra else {},
        compiler_params=params(8),
        cost_estimate=cost(0.05),
        name="place",
    )(sel, *arrays, *extra, *waits)


def given(array, where):
    return [
        (array, i * rows, rows, row, row_off, x_off, 1)
        for i, (_, _, rows, row, row_off, x_off, _) in enumerate(where)
    ]


def on_device(
    tokens,
    offsets,
    w_proj,
    forget_weight,
    reset_weight,
    forget_bias,
    reset_bias,
    layer_norm_gain,
    layer_norm_bias,
    cotangent,
):
    _, block, width = tokens.shape
    z, y, x, c = (lax.axis_index(a) for a in ("z", "y", "x", "c"))
    tuned = lax.axis_size("z") == 4
    sel = jnp.stack([x, c, y, z]).astype(jnp.int32)
    part = width // 8

    cot = cotangent[0]
    own = tokens[0].astype(F32)
    own, *parts = lax.optimization_barrier(
        (own, *(own[first : first + rows] for first, rows in chunks(block)))
    )
    x_a, x_b, x_c = (swap(piece, "x") for piece in parts)
    tok_c = swap(own, "c")
    cot_sibling = swap(widen_cot(sel, cot), "c")
    cot_far = swap(pack_cot(sel, cot, cot_sibling), "x")

    gates = [
        v.reshape(1, width) for v in (forget_weight, reset_weight, forget_bias, reset_bias)
    ]
    gain = layer_norm_gain.reshape(1, width)
    vectors = (*gates, gain, layer_norm_bias.reshape(1, width))
    w_mine = take_weights(sel, w_proj)
    near = run_near(sel, offsets, (own, tok_c), w_mine, vectors)
    (x_a,) = hold((x_a,), near[5])
    xc_a = swap(x_a, "c")
    (x_b,) = hold((x_b,), xc_a)
    xc_b = swap(x_b, "c")
    early = run_early(sel, (x_a, xc_a, x_b, xc_b), w_mine, vectors)
    (x_c,) = hold((x_c,), early[0])
    xc_c = swap(x_c, "c")
    far = run_forward(sel, (x_c, xc_c), near[2:], early, w_mine, vectors)
    normed = (near[0], far[0])
    toks = (own, tok_c, x_a, xc_a, x_b, xc_b, x_c, xc_c)
    if tuned:
        rows = [[[(d, 1)] for d in (2, 3, 1, 0)], [[(d, 0)] for d in (2, 3, 1, 0)]]
    else:
        rows = [[[0], [1], [2], [3]], [[4], [5], [6], [7]]]
    dproj, out, dxh, gate_small, s2, s1 = run_backward(
        sel, toks, (cot, cot_sibling, cot_far), far[2:], near[5], gates, normed, (rows[0][0], rows[0][2])
    )
    s3, k2 = run_products(sel, normed, dproj, (rows[0][1], rows[1][0]))
    grad_mine, grad_send = run_input(
        sel, toks, (near[1], far[1]), dproj, dxh, out, gate_small, w_mine, gain
    )
    late = (rows[0][3], *rows[1][1:])

    if tuned:
        s0, k3, k1, k0 = run_products(sel, normed, dproj, late)
        q2 = add(k2, swap(s2, "y"), s3, s0, grad_send)
        r3 = swap(s3, "y")
        r0 = swap(add(s0, xor_permute(s1, "z", 1), q2), "y")
        a2 = xor_permute(q2, "z", 1)
        h3 = add(add(k3, r3), a2)
        a3 = xor_permute(h3, "z", 3)
        kept, kept_out, sent, sent_out, small = combine(
            sel, grad_mine, swap(grad_send, "c"), q2, tick(grad_send)
        )
        got = swap(sent, "x")
        a1 = xor_permute(k1, "z", 1)
        both = finish(k0, r0, a1, a3, small)
        input_grad, joined = join_grad(kept, got)

        px0, z3, z1, py0 = (
            swap(both, "x"),
            xor_permute(both, "z", 3),
            xor_permute(both, "z", 1),
            swap(both, "y"),
        )
        (px0,) = hold((px0,), joined)
        corner0 = swap(px0, "y")
        (sent_out,) = hold((sent_out,), px0)
        got_out = swap(sent_out, "x")
        z3, z1, corner0, py0, got_out = hold((z3, z1, corner0, py0, got_out))
        output = join_out(sel, kept_out, got_out)
        full = part + 8
        z13, zs, cs = second(both, px0, py0, corner0, z1, z3)
        z2, px13, py13 = xor_permute(zs, "z", 1), swap(z13, "x"), swap(z13, "y")
        corner3 = xor_permute(cs, "z", 3)
        own = [
            (0, 0, part, (0, 0), 0, 0, 0),
            (1, 0, part, (0, 0), 0, 1, 0),
            (2, 0, part, (0, 1), 0, 0, 0),
            (3, 0, part, (0, 1), 0, 1, 0),
            (4, 0, part, (1, 0), 0, 0, 0),
            (4, part, part, (3, 0), 0, 0, 0),
        ]
        proj_grad, give = place(sel, (both, px0, py0, corner0, z13), own, None, width, 6)
        z2, px13, py13, corner3 = hold((z2, px13, py13, corner3), give)
        by_x, by_y = 3 * part // 8, 3 * part // 8
        rest = part - by_x - by_y
        px2 = swap(stack((z2, 0, part), (py13, 0, by_x)), "x")
        py2 = swap(stack((z2, 0, part), (px13, by_x, by_y)), "y")
        corner12 = xor_permute(
            stack((corner3, 0, part), (corner0, by_x + by_y, rest), (corner3, part, 8)), "z", 1
        )
        other = given(2, own)
        own = [
            (array, part * i, part, (d, y_off), 0, x_off, 0)
            for array, y_off, x_off in ((0, 0, 1), (1, 1, 0))
            for i, d in ((0, 1), (1, 3))
        ]
        proj_grad, give = place(
            sel,
            (px13, py13, swap(give, "c")),
            own + other,
            proj_grad,
            width,
            4,
            tick(give, corner3),
        )
        other = given(3, own)
        first_give, marked = swap(give, "c"), give
        own = [(0, 0, part, (2, 0), 0, 0, 0), (1, 0, part, (3, 1), 0, 1, 0)]
        proj_grad, give = place(sel, (z2, corner3), own, proj_grad, width, 2)
        other += given(4, own)
        px2, py2, corner12 = hold((px2, py2, corner12), give)
        own = [
            (0, 0, part, (2, 0), 0, 1, 0),
            (0, part, by_x, (1, 1), 0, 1, 0),
            (1, 0, part, (2, 1), 0, 0, 0),
            (1, part, by_y, (1, 1), by_x, 1, 0),
            (2, 0, part, (2, 1), 0, 1, 0),
            (2, part, rest, (1, 1), by_x + by_y, 1, 0),
        ]
        arrays = (px2, py2, corner12, first_give, swap(give, "c"))
        (proj_grad,) = place(
            sel, arrays, own + other, proj_grad, width, 0, tick(marked, give, px2)
        )
        own = [(*place_of[:-1], 1) for place_of in own]
        arrays = [swap(a, "c") for a in (px2, py2, corner12)]
        (proj_grad,) = place(sel, arrays, own, proj_grad, width, 0)
        where = [(0, part), (1, part), (2, part + rest), (3, part)]
        small = small_sums((zs, z2, corner12, corner3), where)
    else:
        s0, k3, k1, k0 = run_products(sel, normed, dproj, late)
        kept, kept_out, sent, sent_out, small = combine(sel, grad_mine, swap(grad_send, "c"))
        input_grad, _ = join_grad(kept, swap(sent, "x"))
        output = join_out(sel, kept_out, swap(sent_out, "x"))
        small = lax.psum(small + swap(small, "x"), ("z", "y"))
        pieces = jnp.stack([s2, s3, s1, s0, k2, k3, k1, k0])
        pieces = lax.psum(pieces, ("z", "y"))
        proj_grad = None
        for x_off, held in ((0, pieces), (1, swap(pieces, "x"))):
            own = [(r, 0, part, r, 0, x_off, 0) for r in range(8)]
            proj_grad, give = place(sel, list(held), own, proj_grad, width, 8)
            other = given(0, own)
            (proj_grad,) = place(sel, [swap(give, "c")], other, proj_grad, width, 0)
    small = [small[i].reshape(width) for i in range(6)]
    return (output[None], input_grad[None], proj_grad, *small)


def solution(mesh):
    dp, rep = mesh.shape["dp"], mesh.shape["rep"]
    fine = Mesh(mesh.devices.reshape(dp // 2, 2, rep // 2, 2), ("z", "y", "x", "c"))
    row, seq = ("z", "y"), ("x", "c")
    in_specs = (P(row, seq, None), P(row, None)) + (P(),) * 7 + (P(row, seq, None),)
    out_specs = (P(row, seq, None), P(row, seq, None)) + (P(),) * 7
    return jax.shard_map(
        on_device, mesh=fine, in_specs=in_specs, out_specs=out_specs, check_vma=False
    )
```

```python
import functools

import jax
import jax.numpy as jnp
from jax import lax
from jax.experimental import pallas as pl
from jax.experimental.pallas import tpu as pltpu
from jax.sharding import Mesh
from jax.sharding import PartitionSpec as P

EPS = 1e-05
LANES = 128
SWAP = [(0, 1), (1, 0)]
VMEM_BYTES = 56 * 2**20
F32 = jnp.float32
BF16 = jnp.bfloat16


def swap(block, axis):
    return lax.ppermute(block, axis, SWAP)


def xor_permute(block, axis, distance):
    size = lax.axis_size(axis)
    return lax.ppermute(block, axis, [(i, i ^ distance) for i in range(size)])


def any_spec():
    return pl.BlockSpec(memory_space=pl.ANY)


def hbm():
    return pl.BlockSpec(memory_space=pltpu.HBM)


def vmem():
    return pl.BlockSpec(memory_space=pltpu.VMEM)


def smem():
    return pl.BlockSpec(memory_space=pltpu.SMEM)


def shaped(shape, dtype=F32):
    return jax.ShapeDtypeStruct(shape, dtype)


def params(mib):
    return pltpu.CompilerParams(vmem_limit_bytes=mib * 2**20)


def cost(us):
    return pl.CostEstimate(
        flops=int(us * 1.1e9), bytes_accessed=int(us * 3.6e6), transcendentals=0
    )


def own_columns(sel, cols):
    return pl.ds(pl.multiple_of((2 * sel[0] + sel[1]) * cols, cols), cols)


def stored_at(sel, k):
    return 2 * ((k // 2) ^ sel[0]) + ((k % 2) ^ sel[1])


def chunks(block):
    unit = block // 88 * 16
    sizes = (unit, 2 * unit, block - 3 * unit)
    return tuple((sum(sizes[:i]), size) for i, size in enumerate(sizes))


def segments(block):
    far = [(b, first, rows) for first, rows in chunks(block) for b in (2, 3)]
    return ((0, 0, block), (1, 0, block), *far)


def stretches(sel, block, k):
    held = stored_at(sel, k)
    near = held < 2
    return tuple(
        (jnp.where(near, held * block + first, 2 * (block + first) + (held - 2) * rows), rows)
        for first, rows in chunks(block)
    )


def row_part(sel, row):
    return row if isinstance(row, int) else 2 * (sel[3] ^ row[0]) + (sel[2] ^ row[1])


def tick_kernel(*refs):
    refs[-1][...] = jnp.zeros(refs[-1].shape, F32)


def tick(*values):
    return pl.pallas_call(
        tick_kernel,
        out_shape=shaped((8, 128)),
        in_specs=[any_spec()] * len(values),
        out_specs=vmem(),
        compiler_params=params(1),
        cost_estimate=cost(20),
        name="tick",
    )(*values)


def hold_kernel(*refs):
    del refs


def hold(values, *waits):
    count = len(values)
    return pl.pallas_call(
        hold_kernel,
        out_shape=tuple(shaped(v.shape, v.dtype) for v in values),
        in_specs=[any_spec()] * (count + len(waits)),
        out_specs=(any_spec(),) * count,
        input_output_aliases={i: i for i in range(count)},
        compiler_params=params(1),
        cost_estimate=cost(0.05),
        name="hold",
    )(*values, *waits)


def add_kernel(a_ref, b_ref, *refs):
    refs[-1][...] = a_ref[...] + b_ref[...]


def add(a, b, *waits):
    return pl.pallas_call(
        add_kernel,
        out_shape=shaped(a.shape),
        in_specs=[vmem()] * 2 + [any_spec()] * len(waits),
        out_specs=vmem(),
        compiler_params=params(4),
        cost_estimate=cost(0.05),
        name="add",
    )(a, b, *waits)


def take_weights_kernel(sel, w_ref, mine_ref, sem):
    width, cols = mine_ref.shape[0], mine_ref.shape[1] // 3
    copies = []
    for k in range(3):
        at = pl.multiple_of((2 * sel[0] + sel[1]) * cols + k * width, cols)
        copies.append(
            pltpu.make_async_copy(
                w_ref.at[:, pl.ds(at, cols)], mine_ref.at[:, k * cols : (k + 1) * cols], sem.at[k]
            )
        )
    for c in copies:
        c.start()
    for c in copies:
        c.wait()


def take_weights(sel, w_proj):
    width = w_proj.shape[0]
    return pl.pallas_call(
        take_weights_kernel,
        out_shape=shaped((width, 3 * width // 4), BF16),
        in_specs=[smem(), hbm()],
        out_specs=vmem(),
        scratch_shapes=[pltpu.SemaphoreType.DMA((3,))],
        compiler_params=params(4),
        cost_estimate=cost(0.05),
        name="take_weights",
    )(sel, w_proj)


def widen_cot_kernel(sel, cot_ref, cot_out):
    cols = cot_ref.shape[1] // 4
    for k in range(2):
        at = pl.multiple_of((2 * k + 1 - sel[1]) * cols, cols)
        cot_out[:, k * cols : (k + 1) * cols] = cot_ref[:, pl.ds(at, cols)].astype(F32)


def widen_cot(sel, cot):
    return pl.pallas_call(
        widen_cot_kernel,
        out_shape=shaped((cot.shape[0], cot.shape[1] // 2)),
        in_specs=[smem(), vmem()],
        out_specs=vmem(),
        compiler_params=params(4),
        cost_estimate=cost(0.05),
        name="widen_cot",
    )(sel, cot)


def pack_cot_kernel(sel, cot_ref, sibling_ref, cot_out):
    block, cols = cot_ref.shape[0], cot_ref.shape[1] // 4
    mine = pl.multiple_of((2 * (1 - sel[0]) + sel[1]) * cols, cols)
    cot_out[0:block, :] = cot_ref[:, pl.ds(mine, cols)].astype(F32)
    sibling = pl.multiple_of((1 - sel[0]) * cols, cols)
    cot_out[block:, :] = sibling_ref[:, pl.ds(sibling, cols)]


def pack_cot(sel, cot, sibling):
    return pl.pallas_call(
        pack_cot_kernel,
        out_shape=shaped((2 * cot.shape[0], cot.shape[1] // 4)),
        in_specs=[smem(), vmem(), vmem()],
        out_specs=vmem(),
        compiler_params=params(4),
        cost_estimate=cost(0.05),
        name="pack_cot",
    )(sel, cot, sibling)


def standardized(x):
    mean = jnp.mean(x, axis=-1, keepdims=True)
    centred = x - mean
    rdev = lax.rsqrt(jnp.mean(centred * centred, axis=-1, keepdims=True) + EPS)
    return centred * rdev, mean, rdev


def norm_and_project(sel, toks, norm, w_ref, gates, normed, stats, cand, zf, zr, first, base):
    cols = cand.shape[1]
    mine = own_columns(sel, cols)
    gain, bias = norm[0][...], norm[1][...]
    fb, rb = gates[2][:, mine], gates[3][:, mine]
    step = 16
    at = first
    for tok in toks:

        def body(i, carry, tok=tok, at=at):
            here = pl.ds(pl.multiple_of(i * step, step), step)
            there = pl.ds(pl.multiple_of(at + i * step, step), step)
            xhat, mean, rdev = standardized(tok[here, :])
            normed[there, :] = (xhat * gain + bias).astype(BF16)
            stats[there, 0:LANES] = jnp.broadcast_to(mean, (step, LANES))
            stats[there, LANES:] = jnp.broadcast_to(rdev, (step, LANES))
            return carry

        lax.fori_loop(0, tok.shape[0] // step, body, 0, unroll=True)
        at += tok.shape[0]
    rows = normed[first:at, :]
    here = slice(base, base + at - first)
    part = lambda k: jnp.dot(
        rows, w_ref[:, k * cols : (k + 1) * cols], preferred_element_type=F32
    )
    cand[here, :] = part(0)
    zf[here, :] = 0.5 * (part(1) + fb)
    zr[here, :] = 0.5 * (part(2) + rb)


def near_kernel(sel, offsets, tok0, tok1, w_ref, *refs):
    gates, norm, (normed, stats, cand, zf, zr, half_keep) = refs[:4], refs[4:6], refs[6:]
    length, cols = half_keep.shape
    block = length // 4
    step = 16
    row = 0
    for b, first, rows in segments(block):
        base = stored_at(sel, b) * block + first

        def body(i, carry, row=row, base=base):
            at = pl.multiple_of(i * step, step)
            token = base + at + lax.broadcasted_iota(jnp.int32, (step, cols), 0)
            starts = token == offsets[0, 0]
            for k in range(1, offsets.shape[1]):
                starts = starts | (token == offsets[0, k])
            half_keep[pl.ds(pl.multiple_of(row + at, step), step), :] = jnp.where(starts, 0.0, 0.5)
            return carry

        lax.fori_loop(0, rows // step, body, 0)
        row += rows
    norm_and_project(sel, (tok0, tok1), norm, w_ref, gates, normed, stats, cand, zf, zr, 0, 0)


def run_near(sel, offsets, toks, w_mine, vectors):
    block, width = toks[0].shape
    cols = width // 4
    return pl.pallas_call(
        near_kernel,
        out_shape=(shaped((2 * block, width), BF16), shaped((2 * block, 2 * LANES)))
        + (shaped((2 * block, cols)),) * 3
        + (shaped((4 * block, cols)),),
        in_specs=[smem()] * 2 + [vmem()] * 9,
        out_specs=(vmem(),) * 6,
        compiler_params=params(16),
        cost_estimate=cost(0.05),
        name="near_blocks",
    )(sel, offsets, *toks, w_mine, *vectors)


def early_kernel(sel, *refs, count):
    toks, w_ref, refs = refs[:count], refs[count], refs[count + 1 :]
    gates, norm, (normed, stats, cand, zf, zr) = refs[:4], refs[4:6], refs[-5:]
    norm_and_project(sel, toks, norm, w_ref, gates, normed, stats, cand, zf, zr, 0, 0)


def run_early(sel, toks, w_mine, vectors):
    rows, width = sum(tok.shape[0] for tok in toks), toks[0].shape[1]
    cols = width // 4
    return pl.pallas_call(
        functools.partial(early_kernel, count=len(toks)),
        out_shape=(shaped((rows, width), BF16), shaped((rows, 2 * LANES)))
        + (shaped((rows, cols)),) * 3,
        in_specs=[smem()] + [vmem()] * (7 + len(toks)),
        out_specs=(vmem(),) * 5,
        compiler_params=params(12),
        cost_estimate=cost(0.05),
        name="early_blocks",
    )(sel, *toks, w_mine, *vectors)


def forward_kernel(
    sel,
    tok0,
    tok1,
    cand_near,
    zf_near,
    zr_near,
    half_keep,
    normed_early,
    stats_early,
    cand_early,
    zf_early,
    zr_early,
    w_ref,
    *refs,
):
    gates, norm, (normed, stats, cand, zf, zr, state, half_prev) = refs[:4], refs[4:6], refs[6:]
    length, cols = cand.shape
    block = length // 4
    early = normed_early.shape[0]
    normed[0:early, :] = normed_early[...]
    stats[0:early, :] = stats_early[...]
    first = 2 * block
    near, mid = slice(0, first), slice(first, first + early)
    cand[near, :], zf[near, :], zr[near, :] = cand_near[...], zf_near[...], zr_near[...]
    cand[mid, :], zf[mid, :], zr[mid, :] = cand_early[...], zf_early[...], zr_early[...]
    fw = gates[0][:, own_columns(sel, cols)]
    norm_and_project(
        sel, (tok0, tok1), norm, w_ref, gates, normed, stats, cand, zf, zr, early, first + early
    )
    zero = jnp.zeros((1, cols), F32)
    carry = (zero, zero, zero)
    for k in range(4):
        for base, rows in stretches(sel, block, k):

            def body(i, carry, base=base):
                middle, spread, th = carry
                row = pl.ds(base + i, 1)
                half = half_keep[row, :]
                weight = half * fw
                last = middle + spread * th
                th = jnp.tanh((zf[row, :] + weight * middle) + (weight * spread) * th)
                hp = half * last
                hc = 0.5 * cand[row, :]
                middle, spread = hp + hc, hp - hc
                state[row, :] = middle + spread * th
                half_prev[row, :] = hp
                return (middle, spread, th)

            carry = lax.fori_loop(0, rows, body, carry, unroll=16)


def run_forward(sel, toks, near, early, w_mine, vectors):
    late, width = toks[0].shape
    cols = width // 4
    length = near[-1].shape[0]
    return pl.pallas_call(
        forward_kernel,
        out_shape=(shaped((length // 2, width), BF16), shaped((length // 2, 2 * LANES)))
        + (shaped((length, cols)),) * 5,
        in_specs=[smem()] + [vmem()] * 18,
        out_specs=(vmem(),) * 7,
        compiler_params=params(20),
        cost_estimate=cost(0.05),
        name="forward_scan",
    )(sel, *toks, *near, *early, w_mine, *vectors)


def backward_kernel(sel, *refs, rows, count):
    toks, refs = refs[:count], refs[count:]
    (g0, g1, g23, cand_ref, zf_ref, zr_ref, state, half_prev), refs = refs[:8], refs[8:]
    (half_keep, fw_ref, rw_ref, near_ref, far_ref), refs = refs[:5], refs[5:]
    (dproj_ref, out_ref, dxh_ref, small_ref), refs = refs[:4], refs[4:]
    products, (coef, add, add_e, gz, omf, states) = refs[: len(rows)], refs[len(rows) :]
    length, cols = cand_ref.shape
    block = length // 4
    mine = own_columns(sel, cols)
    half = pl.ds(pl.multiple_of(sel[0] * cols, cols), cols)
    fw, rw = fw_ref[:, mine], rw_ref[:, mine]
    half_fw, half_rw = 0.5 * fw, 0.5 * rw
    step = 16
    zero = jnp.zeros((step, cols), F32)
    sums = (zero, zero)
    everything = slice(0, cols)
    grads = ((g0, 0, mine), (g1, 0, half), (g23, 0, everything), (g23, block, everything))
    row = 0
    for x_ref, (b, first, count) in zip(toks, segments(block)):
        g_ref, g_at, g_cols = grads[b]

        def gate_body(
            i, carry, row=row, x_ref=x_ref, g_ref=g_ref, g_at=g_at + first, g_cols=g_cols
        ):
            at = pl.multiple_of(i * step, step)
            here = pl.ds(pl.multiple_of(row + at, step), step)
            x = x_ref[pl.ds(at, step), mine]
            g = g_ref[pl.ds(pl.multiple_of(g_at + at, step), step), g_cols].astype(F32)
            keep = 2.0 * half_keep[here, :]
            prev = 2.0 * half_prev[here, :]
            c, cd = state[here, :], cand_ref[here, :]
            forget = 0.5 + 0.5 * jnp.tanh(zf_ref[here, :] + half_fw * prev)
            reset = 0.5 + 0.5 * jnp.tanh(zr_ref[here, :] + half_rw * prev)
            not_forget, not_reset = 1.0 - forget, 1.0 - reset
            out_ref[here, :] = reset * c + not_reset * x
            dxh_ref[here, :] = g * not_reset
            dzr = g * (c - x) * reset * not_reset
            slope = (prev - cd) * forget * not_forget
            back, extra = keep * (forget + slope * fw), g * reset
            coef[here, :] = back
            add[here, :] = back * extra + keep * (dzr * rw)
            add_e[here, :] = extra
            gz[here, :] = slope
            omf[here, :] = not_forget
            dproj_ref[here, 2 * cols : 3 * cols] = dzr.astype(BF16)
            return (carry[0] + dzr * prev, carry[1] + dzr)

        sums = lax.fori_loop(0, count // step, gate_body, sums, unroll=True)
        row += count
    rw_sum, rb_sum = sums

    dc = jnp.zeros((1, cols), F32)
    group = 8
    for k in range(3, -1, -1):
        for first, count in reversed(stretches(sel, block, k)):

            def backward_body(i, dc, end=first + count):
                base = pl.multiple_of(end - (i + 1) * group, group)
                for r in range(group - 1, -1, -1):
                    row = pl.ds(base + r, 1)
                    states[row, :] = dc
                    dc = coef[row, :] * dc + add[row, :]
                return dc

            dc = lax.fori_loop(0, count // group, backward_body, dc, unroll=2)

    def grad_body(i, carry):
        here = pl.ds(pl.multiple_of(i * step, step), step)
        total = states[here, :] + add_e[here, :]
        prev = 2.0 * half_prev[here, :]
        dzf = total * gz[here, :]
        dproj_ref[here, 0:cols] = (total * omf[here, :]).astype(BF16)
        dproj_ref[here, cols : 2 * cols] = dzf.astype(BF16)
        return (carry[0] + dzf * prev, carry[1] + dzf)

    fw_sum, fb_sum = lax.fori_loop(0, length // step, grad_body, (zero, zero), unroll=4)
    small_ref[...] = jnp.concatenate(
        [jnp.sum(v, axis=0, keepdims=True) for v in (fw_sum, rw_sum, fb_sum, rb_sum)]
        + [jnp.zeros((4, cols), F32)],
        axis=0,
    )
    outer_products(sel, rows, near_ref, far_ref, dproj_ref, products)


def outer_products(sel, rows, near_ref, far_ref, dproj_ref, outs):
    half, width = near_ref.shape
    part = width // 8
    dims = (((0,), (0,)), ((), ()))
    for out, places in zip(outs, rows):
        for k, place_of in enumerate(places):
            at = pl.ds(pl.multiple_of(row_part(sel, place_of) * part, part), part)
            out[k * part : (k + 1) * part, :] = lax.dot_general(
                near_ref[:, at], dproj_ref[0:half, :], dims, preferred_element_type=F32
            ) + lax.dot_general(
                far_ref[:, at], dproj_ref[half:, :], dims, preferred_element_type=F32
            )


def product_shapes(width, rows):
    return tuple(shaped((len(places) * width // 8, 3 * width // 4)) for places in rows)


def run_backward(sel, toks, cots, scanned, half_keep, gates, normed, rows):
    length, cols = half_keep.shape
    width = 4 * cols
    return pl.pallas_call(
        functools.partial(backward_kernel, rows=rows, count=len(toks)),
        out_shape=(
            shaped((length, 3 * cols), BF16),
            shaped((length, cols)),
            shaped((length, cols)),
            shaped((8, cols)),
        )
        + product_shapes(width, rows),
        in_specs=[smem()] + [vmem()] * (13 + len(toks)),
        out_specs=(vmem(),) * (4 + len(rows)),
        scratch_shapes=[pltpu.VMEM((length, cols), F32)] * 6,
        compiler_params=params(24),
        cost_estimate=cost(0.05),
        name="backward_scan",
    )(sel, *toks, *cots, *scanned, half_keep, *gates[:2], *normed)


def products_kernel(sel, near_ref, far_ref, dproj_ref, *outs, rows):
    outer_products(sel, rows, near_ref, far_ref, dproj_ref, outs[-len(rows) :])


def run_products(sel, normed, dproj, rows, *waits):
    return pl.pallas_call(
        functools.partial(products_kernel, rows=rows),
        out_shape=product_shapes(normed[0].shape[1], rows),
        in_specs=[smem()] + [vmem()] * 3 + [any_spec()] * len(waits),
        out_specs=(vmem(),) * len(rows),
        compiler_params=params(12),
        cost_estimate=cost(0.05),
        name="products",
    )(sel, *normed, dproj, *waits)


def input_kernel(sel, *refs, count):
    toks, (mine_ref, send_ref, dnormed) = refs[:count], refs[-3:]
    (stats_near, stats_far, dproj_ref, dxh_ref, out_ref), refs = refs[count : count + 5], refs[count + 5 :]
    gate_small_ref, w_ref, gain_ref = refs[:3]
    cols = dxh_ref.shape[1]
    block, width = toks[0].shape
    gain = gain_ref[...]
    mine = own_columns(sel, cols)
    step = 16
    sums = (jnp.zeros((step, width), F32), jnp.zeros((step, width), F32))
    row = 0
    for tok, (b, first, count) in zip(toks, segments(block)):
        if row % (2 * block) == 0:
            dnormed[...] = lax.dot_general(
                dproj_ref[row : row + 2 * block, :],
                w_ref[...],
                (((1,), (1,)), ((), ())),
                preferred_element_type=F32,
            )
        rows = slice(row, row + count)
        where = send_ref if b % 2 else mine_ref
        base = (b // 2) * block + first
        stats, at = (stats_near, row) if b < 2 else (stats_far, row - 2 * block)

        def body(i, carry, tok=tok, base=base, where=where, stats=stats, at=at):
            here = pl.ds(pl.multiple_of(i * step, step), step)
            there = pl.ds(pl.multiple_of(base + i * step, step), step)
            kept = pl.ds(pl.multiple_of(at + i * step, step), step)
            mean, rdev = (
                jnp.concatenate([stats[kept, k : k + LANES]] * (width // LANES), axis=1)
                for k in (0, LANES)
            )
            xhat = (tok[here, :] - mean) * rdev
            dn = dnormed[kept, :]
            dxhat = dn * gain
            mean1 = jnp.mean(dxhat, axis=-1, keepdims=True)
            mean2 = jnp.mean(dxhat * xhat, axis=-1, keepdims=True)
            where[there, 0:width] = rdev * (dxhat - mean1 - xhat * mean2)
            return (carry[0] + dn * xhat, carry[1] + dn)

        sums = lax.fori_loop(0, count // step, body, sums, unroll=True if count < block else 11)
        to = pl.ds(base, count)
        where[to, mine] += dxh_ref[rows, :]
        where[to, width : width + cols] = out_ref[rows, :]
        row += count
    tail = slice(2 * block, 2 * block + 8)
    mine_ref[tail, :] = jnp.zeros((8, width + cols), F32)
    mine_ref[2 * block : 2 * block + 4, mine] = gate_small_ref[0:4, :]
    for i, v in enumerate(sums):
        row = 2 * block + 4 + i
        mine_ref[row : row + 1, 0:width] = jnp.sum(v, axis=0, keepdims=True)
    send_ref[tail, :] = mine_ref[tail, :]


def run_input(sel, toks, stats, dproj, dxh, out, gate_small, w_mine, gain, *waits):
    block, width = toks[0].shape
    shape = (2 * block + 8, width + width // 4)
    return pl.pallas_call(
        functools.partial(input_kernel, count=len(toks)),
        out_shape=(shaped(shape), shaped(shape)),
        in_specs=[smem()] + [vmem()] * (8 + len(toks)) + [any_spec()] * len(waits),
        out_specs=(vmem(),) * 2,
        scratch_shapes=[pltpu.VMEM((2 * block, width), F32)],
        compiler_params=params(20),
        cost_estimate=cost(0.05),
        name="input_side",
    )(sel, *toks, *stats, dproj, dxh, out, gate_small, w_mine, gain, *waits)


def combine_kernel(sel, mine_ref, got_ref, *refs):
    keep_grad, keep_out, send_grad, send_out, small_ref = refs[-5:]
    block, width = keep_grad.shape
    cols = width // 4
    low = pl.ds(pl.multiple_of(sel[1] * cols, cols), cols)
    high = pl.ds(pl.multiple_of((1 - sel[1]) * cols, cols), cols)
    for grad, out, first in ((keep_grad, keep_out, 0), (send_grad, send_out, block)):
        here = slice(first, first + block)
        grad[...] = mine_ref[here, 0:width] + got_ref[here, 0:width]
        out[:, low] = mine_ref[here, width:]
        out[:, high] = got_ref[here, width:]
    small_ref[...] = mine_ref[2 * block :, 0:width] + got_ref[2 * block :, 0:width]


def combine(sel, mine, got, *waits):
    block, width = (mine.shape[0] - 8) // 2, mine.shape[1] * 4 // 5
    return pl.pallas_call(
        combine_kernel,
        out_shape=(shaped((block, width)), shaped((block, width // 2))) * 2 + (shaped((8, width)),),
        in_specs=[smem(), vmem(), vmem()] + [any_spec()] * len(waits),
        out_specs=(vmem(),) * 5,
        compiler_params=params(16),
        cost_estimate=cost(0.05),
        name="combine",
    )(sel, mine, got, *waits)


def join_grad_kernel(mine_ref, got_ref, grad_ref, done_ref):
    done_ref[...] = jnp.zeros(done_ref.shape, F32)
    grad_ref[...] = (mine_ref[...] + got_ref[...]).astype(BF16)


def join_grad(mine, got):
    return pl.pallas_call(
        join_grad_kernel,
        out_shape=(shaped(mine.shape, BF16), shaped((8, LANES))),
        in_specs=[vmem()] * 2,
        out_specs=(vmem(),) * 2,
        compiler_params=params(8),
        cost_estimate=cost(0.05),
        name="join_grad",
    )(mine, got)


def join_out_kernel(sel, mine_ref, got_ref, out_ref):
    half = mine_ref.shape[1]
    at = pl.multiple_of(sel[0] * half, half)
    other = pl.multiple_of((1 - sel[0]) * half, half)
    out_ref[:, pl.ds(at, half)] = mine_ref[...].astype(BF16)
    out_ref[:, pl.ds(other, half)] = got_ref[...].astype(BF16)


def join_out(sel, mine, got):
    block, half = mine.shape
    return pl.pallas_call(
        join_out_kernel,
        out_shape=shaped((block, 2 * half), BF16),
        in_specs=[smem()] + [vmem()] * 2,
        out_specs=vmem(),
        compiler_params=params(8),
        cost_estimate=cost(0.05),
        name="join_out",
    )(sel, mine, got)


def fold_small(small):
    rows, cols = 6, small.shape[1] // 4
    tails = [small[i : i + 1, 3 * cols :] for i in range(rows)]
    last = [jnp.concatenate(tails[:3], axis=1), jnp.concatenate(tails[3:], axis=1)]
    return jnp.concatenate([small[0:rows, : 3 * cols]] + last, axis=0)


def finish_kernel(keep_ref, got_ref, a1_ref, a3_ref, small_ref, both_ref):
    part = keep_ref.shape[0]
    both_ref[0:part, :] = keep_ref[...] + got_ref[...] + a1_ref[...] + a3_ref[...]
    both_ref[part:, :] = fold_small(small_ref[...])


def finish(keep, got, a1, a3, small):
    part, cols3 = keep.shape
    return pl.pallas_call(
        finish_kernel,
        out_shape=shaped((part + 8, cols3)),
        in_specs=[vmem()] * 5,
        out_specs=vmem(),
        compiler_params=params(8),
        cost_estimate=cost(0.05),
        name="finish",
    )(keep, got, a1, a3, small)


def second_kernel(both_ref, px0_ref, py0_ref, corner_ref, z1_ref, z3_ref, z13_ref, zs_ref, cs_ref):
    part = z1_ref.shape[0] - 8
    z13_ref[0:part, :] = z1_ref[0:part, :]
    z13_ref[part:, :] = z3_ref[0:part, :]
    small = (both_ref[part:, :] + px0_ref[part:, :]) + (py0_ref[part:, :] + corner_ref[part:, :])
    for ref, out in ((z3_ref, zs_ref), (corner_ref, cs_ref)):
        out[0:part, :] = ref[0:part, :]
        out[part:, :] = small


def second(*pieces):
    part, cols3 = pieces[-1].shape[0] - 8, pieces[-1].shape[1]
    return pl.pallas_call(
        second_kernel,
        out_shape=(shaped((2 * part, cols3)),) + (shaped((part + 8, cols3)),) * 2,
        in_specs=[vmem()] * 6,
        out_specs=(vmem(),) * 3,
        compiler_params=params(10),
        cost_estimate=cost(0.05),
        name="second",
    )(*pieces)


def stack_kernel(*refs, rows):
    at = 0
    for ref, (first, count) in zip(refs, rows):
        refs[-1][at : at + count, :] = ref[first : first + count, :]
        at += count


def stack(*parts):
    rows = tuple((first, count) for _, first, count in parts)
    return pl.pallas_call(
        functools.partial(stack_kernel, rows=rows),
        out_shape=shaped((sum(count for _, count in rows), parts[0][0].shape[1])),
        in_specs=[vmem()] * len(parts),
        out_specs=vmem(),
        compiler_params=params(6),
        cost_estimate=cost(0.05),
        name="stack",
    )(*(array for array, _, _ in parts))


def add_small(places, outs):
    sums = [array[at : at + 8, :] for array, at in places]
    while len(sums) > 1:
        sums = [a + b for a, b in zip(sums[::2], sums[1::2])]
    total = sums[0]
    cols = total.shape[1] // 3
    for i, out in enumerate(outs):
        out[:, 0 : 3 * cols] = total[i : i + 1, :]
        out[:, 3 * cols :] = total[6 + i // 3 : 7 + i // 3, (i % 3) * cols : (i % 3 + 1) * cols]


def place_kernel(sel, *refs, where, give, count, small):
    tails = 6 if small else 0
    outs, scratch = refs[len(refs) - 2 - bool(give) - 2 * tails :], refs[len(refs) - 1 - tails :]
    target, sem, sums = outs[0], scratch[0], scratch[1:]
    cols = refs[0].shape[1] // 3
    width = target.shape[1] // 3
    part = width // 8
    copies = []

    def copy(src, dst):
        copies.append(pltpu.make_async_copy(src, dst, sem.at[len(copies)]))
        copies[-1].start()

    for at, (array, first, rows, row, row_off, x_off, c_off) in enumerate(where):
        piece = refs[array].at[pl.ds(first, rows)]
        to_row = pl.multiple_of(row_part(sel, row) * part + row_off, 8)
        col = (2 * (sel[0] ^ x_off) + (sel[1] ^ c_off)) * cols
        for k in range(3):
            to = pl.multiple_of(col + k * width, cols)
            copy(piece.at[:, pl.ds(k * cols, cols)], target.at[pl.ds(to_row, rows), pl.ds(to, cols)])
        if at < give:
            copy(piece, outs[1].at[pl.ds(at * part, part)])
    if small:
        add_small([(refs[count + i], at) for i, at in small], sums)
        for i in range(tails):
            copy(sums[i], outs[1 + i])
    for c in copies:
        c.wait()


def place(sel, arrays, where, target, width, give, *waits, small=()):
    count = len(arrays)
    extra = [] if target is None else [target]
    outs = [shaped((width, 3 * width))]
    outs += [shaped((give * width // 8, 3 * width // 4))] if give else []
    outs += [shaped((1, width))] * 6 if small else []
    scratch = [pltpu.SemaphoreType.DMA((3 * len(where) + give + (6 if small else 0),))]
    scratch += [pltpu.VMEM((1, width), F32)] * 6 if small else []
    return pl.pallas_call(
        functools.partial(
            place_kernel,
            where=where,
            give=give,
            count=count,
            small=tuple((i, at) for i, (_, at) in enumerate(small)),
        ),
        out_shape=tuple(outs),
        in_specs=[smem()]
        + [vmem()] * (count + len(small))
        + [hbm()] * len(extra)
        + [any_spec()] * len(waits),
        out_specs=(hbm(),) + ((vmem(),) if give else ()) + ((hbm(),) * 6 if small else ()),
        scratch_shapes=scratch,
        input_output_aliases={1 + count + len(small): 0} if extra else {},
        compiler_params=params(8),
        cost_estimate=cost(0.05),
        name="place",
    )(sel, *arrays, *(array for array, _ in small), *extra, *waits)


def given(array, where):
    return [
        (array, i * rows, rows, row, row_off, x_off, 1)
        for i, (_, _, rows, row, row_off, x_off, _) in enumerate(where)
    ]


def on_device(
    tokens,
    offsets,
    w_proj,
    forget_weight,
    reset_weight,
    forget_bias,
    reset_bias,
    layer_norm_gain,
    layer_norm_bias,
    cotangent,
):
    _, block, width = tokens.shape
    z, y, x, c = (lax.axis_index(a) for a in ("z", "y", "x", "c"))
    tuned = lax.axis_size("z") == 4
    sel = jnp.stack([x, c, y, z]).astype(jnp.int32)
    part = width // 8

    cot = cotangent[0]
    own = tokens[0].astype(F32)
    own, *parts = lax.optimization_barrier(
        (own, *(own[first : first + rows] for first, rows in chunks(block)))
    )
    x_a, x_b, x_c = (swap(piece, "x") for piece in parts)
    tok_c = swap(own, "c")
    cot_sibling = swap(widen_cot(sel, cot), "c")
    cot_far = swap(pack_cot(sel, cot, cot_sibling), "x")

    gates = [
        v.reshape(1, width) for v in (forget_weight, reset_weight, forget_bias, reset_bias)
    ]
    gain = layer_norm_gain.reshape(1, width)
    vectors = (*gates, gain, layer_norm_bias.reshape(1, width))
    w_mine = take_weights(sel, w_proj)
    near = run_near(sel, offsets, (own, tok_c), w_mine, vectors)
    (x_a,) = hold((x_a,), near[5])
    xc_a = swap(x_a, "c")
    (x_b,) = hold((x_b,), xc_a)
    xc_b = swap(x_b, "c")
    early = run_early(sel, (x_a, xc_a, x_b, xc_b), w_mine, vectors)
    (x_c,) = hold((x_c,), early[0])
    xc_c = swap(x_c, "c")
    far = run_forward(sel, (x_c, xc_c), near[2:], early, w_mine, vectors)
    normed = (near[0], far[0])
    toks = (own, tok_c, x_a, xc_a, x_b, xc_b, x_c, xc_c)
    if tuned:
        rows = [[[(d, 1)] for d in (2, 3, 1, 0)], [[(d, 0)] for d in (2, 3, 1, 0)]]
    else:
        rows = [[[0], [1], [2], [3]], [[4], [5], [6], [7]]]
    dproj, out, dxh, gate_small, s2, s1 = run_backward(
        sel, toks, (cot, cot_sibling, cot_far), far[2:], near[5], gates, normed, (rows[0][0], rows[0][2])
    )
    s3, k2 = run_products(sel, normed, dproj, (rows[0][1], rows[1][0]))
    grad_mine, grad_send = run_input(
        sel, toks, (near[1], far[1]), dproj, dxh, out, gate_small, w_mine, gain
    )
    late = (rows[0][3], *rows[1][1:])

    if tuned:
        s0, k3, k1, k0 = run_products(sel, normed, dproj, late)
        q2 = add(k2, swap(s2, "y"), s3, s0, grad_send)
        r3 = swap(s3, "y")
        r0 = swap(add(s0, xor_permute(s1, "z", 1), q2), "y")
        a2 = xor_permute(q2, "z", 1)
        h3 = add(add(k3, r3), a2)
        a3 = xor_permute(h3, "z", 3)
        kept, kept_out, sent, sent_out, small = combine(
            sel, grad_mine, swap(grad_send, "c"), q2, tick(grad_send)
        )
        got = swap(sent, "x")
        a1 = xor_permute(k1, "z", 1)
        both = finish(k0, r0, a1, a3, small)
        input_grad, joined = join_grad(kept, got)

        px0, z3, z1, py0 = (
            swap(both, "x"),
            xor_permute(both, "z", 3),
            xor_permute(both, "z", 1),
            swap(both, "y"),
        )
        (px0,) = hold((px0,), joined)
        corner0 = swap(px0, "y")
        (sent_out,) = hold((sent_out,), px0)
        got_out = swap(sent_out, "x")
        z3, z1, corner0, py0, got_out = hold((z3, z1, corner0, py0, got_out))
        output = join_out(sel, kept_out, got_out)
        full = part + 8
        z13, zs, cs = second(both, px0, py0, corner0, z1, z3)
        z2, px13, py13 = xor_permute(zs, "z", 1), swap(z13, "x"), swap(z13, "y")
        corner3 = xor_permute(cs, "z", 3)
        own = [
            (0, 0, part, (0, 0), 0, 0, 0),
            (1, 0, part, (0, 0), 0, 1, 0),
            (2, 0, part, (0, 1), 0, 0, 0),
            (3, 0, part, (0, 1), 0, 1, 0),
            (4, 0, part, (1, 0), 0, 0, 0),
            (4, part, part, (3, 0), 0, 0, 0),
        ]
        proj_grad, give = place(sel, (both, px0, py0, corner0, z13), own, None, width, 6)
        z2, px13, py13, corner3 = hold((z2, px13, py13, corner3), give)
        by_x, by_y = 3 * part // 8, 3 * part // 8
        rest = part - by_x - by_y
        px2 = swap(stack((z2, 0, part), (py13, 0, by_x)), "x")
        py2 = swap(stack((z2, 0, part), (px13, by_x, by_y)), "y")
        corner12 = xor_permute(
            stack((corner3, 0, part), (corner0, by_x + by_y, rest), (corner3, part, 8)), "z", 1
        )
        other = given(2, own)
        own = [
            (array, part * i, part, (d, y_off), 0, x_off, 0)
            for array, y_off, x_off in ((0, 0, 1), (1, 1, 0))
            for i, d in ((0, 1), (1, 3))
        ]
        proj_grad, give = place(
            sel,
            (px13, py13, swap(give, "c")),
            own + other,
            proj_grad,
            width,
            4,
            tick(give, corner3),
        )
        other = given(3, own)
        first_give, marked = swap(give, "c"), give
        own = [(0, 0, part, (2, 0), 0, 0, 0), (1, 0, part, (3, 1), 0, 1, 0)]
        proj_grad, give = place(sel, (z2, corner3), own, proj_grad, width, 2)
        last = given(3, own)
        px2, py2, corner12 = hold((px2, py2, corner12), give)
        own = [
            (0, 0, part, (2, 0), 0, 1, 0),
            (0, part, by_x, (1, 1), 0, 1, 0),
            (1, 0, part, (2, 1), 0, 0, 0),
            (1, part, by_y, (1, 1), by_x, 1, 0),
            (2, 0, part, (2, 1), 0, 1, 0),
            (2, part, rest, (1, 1), by_x + by_y, 1, 0),
        ]
        small = ((zs, part), (z2, part), (corner12, part + rest), (corner3, part))
        arrays = (px2, py2, corner12, first_give)
        proj_grad, *small = place(
            sel, arrays, own + other, proj_grad, width, 0, tick(marked, give, px2), small=small
        )
        own = [(*place_of[:-1], 1) for place_of in own]
        arrays = [swap(a, "c") for a in (px2, py2, corner12, give)]
        (proj_grad,) = place(sel, arrays, own + last, proj_grad, width, 0)
    else:
        s0, k3, k1, k0 = run_products(sel, normed, dproj, late)
        kept, kept_out, sent, sent_out, small = combine(sel, grad_mine, swap(grad_send, "c"))
        input_grad, _ = join_grad(kept, swap(sent, "x"))
        output = join_out(sel, kept_out, swap(sent_out, "x"))
        small = lax.psum(small + swap(small, "x"), ("z", "y"))
        pieces = jnp.stack([s2, s3, s1, s0, k2, k3, k1, k0])
        pieces = lax.psum(pieces, ("z", "y"))
        proj_grad = None
        for x_off, held in ((0, pieces), (1, swap(pieces, "x"))):
            own = [(r, 0, part, r, 0, x_off, 0) for r in range(8)]
            proj_grad, give = place(sel, list(held), own, proj_grad, width, 8)
            other = given(0, own)
            (proj_grad,) = place(sel, [swap(give, "c")], other, proj_grad, width, 0)
    small = [small[i].reshape(width) for i in range(6)]
    return (output[None], input_grad[None], proj_grad, *small)


def solution(mesh):
    dp, rep = mesh.shape["dp"], mesh.shape["rep"]
    fine = Mesh(mesh.devices.reshape(dp // 2, 2, rep // 2, 2), ("z", "y", "x", "c"))
    row, seq = ("z", "y"), ("x", "c")
    in_specs = (P(row, seq, None), P(row, None)) + (P(),) * 7 + (P(row, seq, None),)
    out_specs = (P(row, seq, None), P(row, seq, None)) + (P(),) * 7
    return jax.shard_map(
        on_device, mesh=fine, in_specs=in_specs, out_specs=out_specs, check_vma=False
    )
```

```python
import functools

import jax
import jax.numpy as jnp
from jax import lax
from jax.experimental import pallas as pl
from jax.experimental.pallas import tpu as pltpu
from jax.sharding import Mesh
from jax.sharding import PartitionSpec as P

EPS = 1e-05
LANES = 128
SWAP = [(0, 1), (1, 0)]
VMEM_BYTES = 56 * 2**20
F32 = jnp.float32
BF16 = jnp.bfloat16


def swap(block, axis):
    return lax.ppermute(block, axis, SWAP)


def xor_permute(block, axis, distance):
    size = lax.axis_size(axis)
    return lax.ppermute(block, axis, [(i, i ^ distance) for i in range(size)])


def any_spec():
    return pl.BlockSpec(memory_space=pl.ANY)


def hbm():
    return pl.BlockSpec(memory_space=pltpu.HBM)


def vmem():
    return pl.BlockSpec(memory_space=pltpu.VMEM)


def smem():
    return pl.BlockSpec(memory_space=pltpu.SMEM)


def shaped(shape, dtype=F32):
    return jax.ShapeDtypeStruct(shape, dtype)


def params(mib):
    return pltpu.CompilerParams(vmem_limit_bytes=mib * 2**20)


def cost(us):
    return pl.CostEstimate(
        flops=int(us * 1.1e9), bytes_accessed=int(us * 3.6e6), transcendentals=0
    )


def own_columns(sel, cols):
    return pl.ds(pl.multiple_of((2 * sel[0] + sel[1]) * cols, cols), cols)


def stored_at(sel, k):
    return 2 * ((k // 2) ^ sel[0]) + ((k % 2) ^ sel[1])


def chunks(block):
    unit = block // 88 * 16
    sizes = (unit, 2 * unit, block - 3 * unit)
    return tuple((sum(sizes[:i]), size) for i, size in enumerate(sizes))


def segments(block):
    far = [(b, first, rows) for first, rows in chunks(block) for b in (2, 3)]
    return ((0, 0, block), (1, 0, block), *far)


def stretches(sel, block, k):
    held = stored_at(sel, k)
    near = held < 2
    return tuple(
        (jnp.where(near, held * block + first, 2 * (block + first) + (held - 2) * rows), rows)
        for first, rows in chunks(block)
    )


def row_part(sel, row):
    return row if isinstance(row, int) else 2 * (sel[3] ^ row[0]) + (sel[2] ^ row[1])


def tick_kernel(*refs):
    refs[-1][...] = jnp.zeros(refs[-1].shape, F32)


def tick(*values):
    return pl.pallas_call(
        tick_kernel,
        out_shape=shaped((8, 128)),
        in_specs=[any_spec()] * len(values),
        out_specs=vmem(),
        compiler_params=params(1),
        cost_estimate=cost(20),
        name="tick",
    )(*values)


def hold_kernel(*refs):
    del refs


def hold(values, *waits):
    count = len(values)
    return pl.pallas_call(
        hold_kernel,
        out_shape=tuple(shaped(v.shape, v.dtype) for v in values),
        in_specs=[any_spec()] * (count + len(waits)),
        out_specs=(any_spec(),) * count,
        input_output_aliases={i: i for i in range(count)},
        compiler_params=params(1),
        cost_estimate=cost(0.05),
        name="hold",
    )(*values, *waits)


def add_kernel(a_ref, b_ref, *refs):
    refs[-1][...] = a_ref[...] + b_ref[...]


def add(a, b, *waits):
    return pl.pallas_call(
        add_kernel,
        out_shape=shaped(a.shape),
        in_specs=[vmem()] * 2 + [any_spec()] * len(waits),
        out_specs=vmem(),
        compiler_params=params(4),
        cost_estimate=cost(0.05),
        name="add",
    )(a, b, *waits)


def take_weights_kernel(sel, w_ref, mine_ref, sem):
    width, cols = mine_ref.shape[0], mine_ref.shape[1] // 3
    copies = []
    for k in range(3):
        at = pl.multiple_of((2 * sel[0] + sel[1]) * cols + k * width, cols)
        copies.append(
            pltpu.make_async_copy(
                w_ref.at[:, pl.ds(at, cols)], mine_ref.at[:, k * cols : (k + 1) * cols], sem.at[k]
            )
        )
    for c in copies:
        c.start()
    for c in copies:
        c.wait()


def take_weights(sel, w_proj):
    width = w_proj.shape[0]
    return pl.pallas_call(
        take_weights_kernel,
        out_shape=shaped((width, 3 * width // 4), BF16),
        in_specs=[smem(), hbm()],
        out_specs=vmem(),
        scratch_shapes=[pltpu.SemaphoreType.DMA((3,))],
        compiler_params=params(4),
        cost_estimate=cost(0.05),
        name="take_weights",
    )(sel, w_proj)


def widen_cot_kernel(sel, cot_ref, cot_out):
    cols = cot_ref.shape[1] // 4
    for k in range(2):
        at = pl.multiple_of((2 * k + 1 - sel[1]) * cols, cols)
        cot_out[:, k * cols : (k + 1) * cols] = cot_ref[:, pl.ds(at, cols)].astype(F32)


def widen_cot(sel, cot):
    return pl.pallas_call(
        widen_cot_kernel,
        out_shape=shaped((cot.shape[0], cot.shape[1] // 2)),
        in_specs=[smem(), vmem()],
        out_specs=vmem(),
        compiler_params=params(4),
        cost_estimate=cost(0.05),
        name="widen_cot",
    )(sel, cot)


def pack_cot_kernel(sel, cot_ref, sibling_ref, cot_out):
    block, cols = cot_ref.shape[0], cot_ref.shape[1] // 4
    mine = pl.multiple_of((2 * (1 - sel[0]) + sel[1]) * cols, cols)
    cot_out[0:block, :] = cot_ref[:, pl.ds(mine, cols)].astype(F32)
    sibling = pl.multiple_of((1 - sel[0]) * cols, cols)
    cot_out[block:, :] = sibling_ref[:, pl.ds(sibling, cols)]


def pack_cot(sel, cot, sibling):
    return pl.pallas_call(
        pack_cot_kernel,
        out_shape=shaped((2 * cot.shape[0], cot.shape[1] // 4)),
        in_specs=[smem(), vmem(), vmem()],
        out_specs=vmem(),
        compiler_params=params(4),
        cost_estimate=cost(0.05),
        name="pack_cot",
    )(sel, cot, sibling)


def standardized(x):
    mean = jnp.mean(x, axis=-1, keepdims=True)
    centred = x - mean
    rdev = lax.rsqrt(jnp.mean(centred * centred, axis=-1, keepdims=True) + EPS)
    return centred * rdev, mean, rdev


def norm_and_project(sel, toks, norm, w_ref, gates, normed, stats, cand, zf, zr, first, base):
    cols = cand.shape[1]
    mine = own_columns(sel, cols)
    gain, bias = norm[0][...], norm[1][...]
    fb, rb = gates[2][:, mine], gates[3][:, mine]
    step = 16
    at = first
    for tok in toks:

        def body(i, carry, tok=tok, at=at):
            here = pl.ds(pl.multiple_of(i * step, step), step)
            there = pl.ds(pl.multiple_of(at + i * step, step), step)
            xhat, mean, rdev = standardized(tok[here, :])
            normed[there, :] = (xhat * gain + bias).astype(BF16)
            stats[there, 0:LANES] = jnp.broadcast_to(mean, (step, LANES))
            stats[there, LANES:] = jnp.broadcast_to(rdev, (step, LANES))
            return carry

        lax.fori_loop(0, tok.shape[0] // step, body, 0, unroll=True)
        at += tok.shape[0]
    rows = normed[first:at, :]
    here = slice(base, base + at - first)
    part = lambda k: jnp.dot(
        rows, w_ref[:, k * cols : (k + 1) * cols], preferred_element_type=F32
    )
    cand[here, :] = part(0)
    zf[here, :] = 0.5 * (part(1) + fb)
    zr[here, :] = 0.5 * (part(2) + rb)


def near_kernel(sel, offsets, tok0, tok1, w_ref, *refs):
    gates, norm, (normed, stats, cand, zf, zr, half_keep) = refs[:4], refs[4:6], refs[6:]
    length, cols = half_keep.shape
    block = length // 4
    step = 16
    row = 0
    for b, first, rows in segments(block):
        base = stored_at(sel, b) * block + first

        def body(i, carry, row=row, base=base):
            at = pl.multiple_of(i * step, step)
            token = base + at + lax.broadcasted_iota(jnp.int32, (step, cols), 0)
            starts = token == offsets[0, 0]
            for k in range(1, offsets.shape[1]):
                starts = starts | (token == offsets[0, k])
            half_keep[pl.ds(pl.multiple_of(row + at, step), step), :] = jnp.where(starts, 0.0, 0.5)
            return carry

        lax.fori_loop(0, rows // step, body, 0)
        row += rows
    norm_and_project(sel, (tok0, tok1), norm, w_ref, gates, normed, stats, cand, zf, zr, 0, 0)


def run_near(sel, offsets, toks, w_mine, vectors):
    block, width = toks[0].shape
    cols = width // 4
    return pl.pallas_call(
        near_kernel,
        out_shape=(shaped((2 * block, width), BF16), shaped((2 * block, 2 * LANES)))
        + (shaped((2 * block, cols)),) * 3
        + (shaped((4 * block, cols)),),
        in_specs=[smem()] * 2 + [vmem()] * 9,
        out_specs=(vmem(),) * 6,
        compiler_params=params(16),
        cost_estimate=cost(0.05),
        name="near_blocks",
    )(sel, offsets, *toks, w_mine, *vectors)


def early_kernel(sel, *refs, count):
    toks, w_ref, refs = refs[:count], refs[count], refs[count + 1 :]
    gates, norm, (normed, stats, cand, zf, zr) = refs[:4], refs[4:6], refs[-5:]
    norm_and_project(sel, toks, norm, w_ref, gates, normed, stats, cand, zf, zr, 0, 0)


def run_early(sel, toks, w_mine, vectors):
    rows, width = sum(tok.shape[0] for tok in toks), toks[0].shape[1]
    cols = width // 4
    return pl.pallas_call(
        functools.partial(early_kernel, count=len(toks)),
        out_shape=(shaped((rows, width), BF16), shaped((rows, 2 * LANES)))
        + (shaped((rows, cols)),) * 3,
        in_specs=[smem()] + [vmem()] * (7 + len(toks)),
        out_specs=(vmem(),) * 5,
        compiler_params=params(12),
        cost_estimate=cost(0.05),
        name="early_blocks",
    )(sel, *toks, w_mine, *vectors)


def forward_kernel(
    sel,
    tok0,
    tok1,
    cand_near,
    zf_near,
    zr_near,
    half_keep,
    normed_early,
    stats_early,
    cand_early,
    zf_early,
    zr_early,
    w_ref,
    *refs,
):
    gates, norm, (normed, stats, cand, zf, zr, state, half_prev) = refs[:4], refs[4:6], refs[6:]
    length, cols = cand.shape
    block = length // 4
    early = normed_early.shape[0]
    normed[0:early, :] = normed_early[...]
    stats[0:early, :] = stats_early[...]
    first = 2 * block
    near, mid = slice(0, first), slice(first, first + early)
    cand[near, :], zf[near, :], zr[near, :] = cand_near[...], zf_near[...], zr_near[...]
    cand[mid, :], zf[mid, :], zr[mid, :] = cand_early[...], zf_early[...], zr_early[...]
    fw = gates[0][:, own_columns(sel, cols)]
    norm_and_project(
        sel, (tok0, tok1), norm, w_ref, gates, normed, stats, cand, zf, zr, early, first + early
    )
    zero = jnp.zeros((1, cols), F32)
    carry = (zero, zero, zero)
    for k in range(4):
        for base, rows in stretches(sel, block, k):

            def body(i, carry, base=base):
                middle, spread, th = carry
                row = pl.ds(base + i, 1)
                half = half_keep[row, :]
                weight = half * fw
                last = middle + spread * th
                th = jnp.tanh((zf[row, :] + weight * middle) + (weight * spread) * th)
                hp = half * last
                hc = 0.5 * cand[row, :]
                middle, spread = hp + hc, hp - hc
                state[row, :] = middle + spread * th
                half_prev[row, :] = hp
                return (middle, spread, th)

            carry = lax.fori_loop(0, rows, body, carry, unroll=16)


def run_forward(sel, toks, near, early, w_mine, vectors):
    late, width = toks[0].shape
    cols = width // 4
    length = near[-1].shape[0]
    return pl.pallas_call(
        forward_kernel,
        out_shape=(shaped((length // 2, width), BF16), shaped((length // 2, 2 * LANES)))
        + (shaped((length, cols)),) * 5,
        in_specs=[smem()] + [vmem()] * 18,
        out_specs=(vmem(),) * 7,
        compiler_params=params(20),
        cost_estimate=cost(0.05),
        name="forward_scan",
    )(sel, *toks, *near, *early, w_mine, *vectors)


def backward_kernel(sel, *refs, rows, count):
    toks, refs = refs[:count], refs[count:]
    (g0, g1, g23, cand_ref, zf_ref, zr_ref, state, half_prev), refs = refs[:8], refs[8:]
    (half_keep, fw_ref, rw_ref, near_ref, far_ref), refs = refs[:5], refs[5:]
    (dproj_ref, out_ref, dxh_ref, small_ref), refs = refs[:4], refs[4:]
    products, (coef, add, add_e, gz, omf, states) = refs[: len(rows)], refs[len(rows) :]
    length, cols = cand_ref.shape
    block = length // 4
    mine = own_columns(sel, cols)
    half = pl.ds(pl.multiple_of(sel[0] * cols, cols), cols)
    fw, rw = fw_ref[:, mine], rw_ref[:, mine]
    half_fw, half_rw = 0.5 * fw, 0.5 * rw
    step = 16
    zero = jnp.zeros((step, cols), F32)
    sums = (zero, zero)
    everything = slice(0, cols)
    grads = ((g0, 0, mine), (g1, 0, half), (g23, 0, everything), (g23, block, everything))
    row = 0
    for x_ref, (b, first, count) in zip(toks, segments(block)):
        g_ref, g_at, g_cols = grads[b]

        def gate_body(
            i, carry, row=row, x_ref=x_ref, g_ref=g_ref, g_at=g_at + first, g_cols=g_cols
        ):
            at = pl.multiple_of(i * step, step)
            here = pl.ds(pl.multiple_of(row + at, step), step)
            x = x_ref[pl.ds(at, step), mine]
            g = g_ref[pl.ds(pl.multiple_of(g_at + at, step), step), g_cols].astype(F32)
            keep = 2.0 * half_keep[here, :]
            prev = 2.0 * half_prev[here, :]
            c, cd = state[here, :], cand_ref[here, :]
            forget = 0.5 + 0.5 * jnp.tanh(zf_ref[here, :] + half_fw * prev)
            reset = 0.5 + 0.5 * jnp.tanh(zr_ref[here, :] + half_rw * prev)
            not_forget, not_reset = 1.0 - forget, 1.0 - reset
            out_ref[here, :] = reset * c + not_reset * x
            dxh_ref[here, :] = g * not_reset
            dzr = g * (c - x) * reset * not_reset
            slope = (prev - cd) * forget * not_forget
            back, extra = keep * (forget + slope * fw), g * reset
            coef[here, :] = back
            add[here, :] = back * extra + keep * (dzr * rw)
            add_e[here, :] = extra
            gz[here, :] = slope
            omf[here, :] = not_forget
            dproj_ref[here, 2 * cols : 3 * cols] = dzr.astype(BF16)
            return (carry[0] + dzr * prev, carry[1] + dzr)

        sums = lax.fori_loop(0, count // step, gate_body, sums, unroll=True)
        row += count
    rw_sum, rb_sum = sums

    dc = jnp.zeros((1, cols), F32)
    group = 8
    for k in range(3, -1, -1):
        for first, count in reversed(stretches(sel, block, k)):

            def backward_body(i, dc, end=first + count):
                base = pl.multiple_of(end - (i + 1) * group, group)
                for r in range(group - 1, -1, -1):
                    row = pl.ds(base + r, 1)
                    states[row, :] = dc
                    dc = coef[row, :] * dc + add[row, :]
                return dc

            dc = lax.fori_loop(0, count // group, backward_body, dc, unroll=2)

    def grad_body(i, carry):
        here = pl.ds(pl.multiple_of(i * step, step), step)
        total = states[here, :] + add_e[here, :]
        prev = 2.0 * half_prev[here, :]
        dzf = total * gz[here, :]
        dproj_ref[here, 0:cols] = (total * omf[here, :]).astype(BF16)
        dproj_ref[here, cols : 2 * cols] = dzf.astype(BF16)
        return (carry[0] + dzf * prev, carry[1] + dzf)

    fw_sum, fb_sum = lax.fori_loop(0, length // step, grad_body, (zero, zero), unroll=4)
    small_ref[...] = jnp.concatenate(
        [jnp.sum(v, axis=0, keepdims=True) for v in (fw_sum, rw_sum, fb_sum, rb_sum)]
        + [jnp.zeros((4, cols), F32)],
        axis=0,
    )
    outer_products(sel, rows, near_ref, far_ref, dproj_ref, products)


def outer_products(sel, rows, near_ref, far_ref, dproj_ref, outs):
    half, width = near_ref.shape
    part = width // 8
    dims = (((0,), (0,)), ((), ()))
    for out, places in zip(outs, rows):
        for k, place_of in enumerate(places):
            at = pl.ds(pl.multiple_of(row_part(sel, place_of) * part, part), part)
            out[k * part : (k + 1) * part, :] = lax.dot_general(
                near_ref[:, at], dproj_ref[0:half, :], dims, preferred_element_type=F32
            ) + lax.dot_general(
                far_ref[:, at], dproj_ref[half:, :], dims, preferred_element_type=F32
            )


def product_shapes(width, rows):
    return tuple(shaped((len(places) * width // 8, 3 * width // 4)) for places in rows)


def run_backward(sel, toks, cots, scanned, half_keep, gates, normed, rows):
    length, cols = half_keep.shape
    width = 4 * cols
    return pl.pallas_call(
        functools.partial(backward_kernel, rows=rows, count=len(toks)),
        out_shape=(
            shaped((length, 3 * cols), BF16),
            shaped((length, cols)),
            shaped((length, cols)),
            shaped((8, cols)),
        )
        + product_shapes(width, rows),
        in_specs=[smem()] + [vmem()] * (13 + len(toks)),
        out_specs=(vmem(),) * (4 + len(rows)),
        scratch_shapes=[pltpu.VMEM((length, cols), F32)] * 6,
        compiler_params=params(24),
        cost_estimate=cost(0.05),
        name="backward_scan",
    )(sel, *toks, *cots, *scanned, half_keep, *gates[:2], *normed)


def products_kernel(sel, near_ref, far_ref, dproj_ref, *outs, rows):
    outer_products(sel, rows, near_ref, far_ref, dproj_ref, outs[-len(rows) :])


def run_products(sel, normed, dproj, rows, *waits):
    return pl.pallas_call(
        functools.partial(products_kernel, rows=rows),
        out_shape=product_shapes(normed[0].shape[1], rows),
        in_specs=[smem()] + [vmem()] * 3 + [any_spec()] * len(waits),
        out_specs=(vmem(),) * len(rows),
        compiler_params=params(12),
        cost_estimate=cost(0.05),
        name="products",
    )(sel, *normed, dproj, *waits)


def input_kernel(sel, *refs, count):
    toks, (mine_ref, send_ref, dnormed) = refs[:count], refs[-3:]
    (stats_near, stats_far, dproj_ref, dxh_ref, out_ref), refs = refs[count : count + 5], refs[count + 5 :]
    gate_small_ref, w_ref, gain_ref = refs[:3]
    cols = dxh_ref.shape[1]
    block, width = toks[0].shape
    gain = gain_ref[...]
    mine = own_columns(sel, cols)
    step = 16
    sums = (jnp.zeros((step, width), F32), jnp.zeros((step, width), F32))
    row = 0
    for tok, (b, first, count) in zip(toks, segments(block)):
        if row % (2 * block) == 0:
            dnormed[...] = lax.dot_general(
                dproj_ref[row : row + 2 * block, :],
                w_ref[...],
                (((1,), (1,)), ((), ())),
                preferred_element_type=F32,
            )
        rows = slice(row, row + count)
        where = send_ref if b % 2 else mine_ref
        base = (b // 2) * block + first
        stats, at = (stats_near, row) if b < 2 else (stats_far, row - 2 * block)

        def body(i, carry, tok=tok, base=base, where=where, stats=stats, at=at):
            here = pl.ds(pl.multiple_of(i * step, step), step)
            there = pl.ds(pl.multiple_of(base + i * step, step), step)
            kept = pl.ds(pl.multiple_of(at + i * step, step), step)
            mean, rdev = (
                jnp.concatenate([stats[kept, k : k + LANES]] * (width // LANES), axis=1)
                for k in (0, LANES)
            )
            xhat = (tok[here, :] - mean) * rdev
            dn = dnormed[kept, :]
            dxhat = dn * gain
            mean1 = jnp.mean(dxhat, axis=-1, keepdims=True)
            mean2 = jnp.mean(dxhat * xhat, axis=-1, keepdims=True)
            where[there, 0:width] = rdev * (dxhat - mean1 - xhat * mean2)
            return (carry[0] + dn * xhat, carry[1] + dn)

        sums = lax.fori_loop(0, count // step, body, sums, unroll=True if count < block else 11)
        to = pl.ds(base, count)
        where[to, mine] += dxh_ref[rows, :]
        where[to, width : width + cols] = out_ref[rows, :]
        row += count
    tail = slice(2 * block, 2 * block + 8)
    mine_ref[tail, :] = jnp.zeros((8, width + cols), F32)
    mine_ref[2 * block : 2 * block + 4, mine] = gate_small_ref[0:4, :]
    for i, v in enumerate(sums):
        row = 2 * block + 4 + i
        mine_ref[row : row + 1, 0:width] = jnp.sum(v, axis=0, keepdims=True)
    send_ref[tail, :] = mine_ref[tail, :]


def run_input(sel, toks, stats, dproj, dxh, out, gate_small, w_mine, gain, *waits):
    block, width = toks[0].shape
    shape = (2 * block + 8, width + width // 4)
    return pl.pallas_call(
        functools.partial(input_kernel, count=len(toks)),
        out_shape=(shaped(shape), shaped(shape)),
        in_specs=[smem()] + [vmem()] * (8 + len(toks)) + [any_spec()] * len(waits),
        out_specs=(vmem(),) * 2,
        scratch_shapes=[pltpu.VMEM((2 * block, width), F32)],
        compiler_params=params(20),
        cost_estimate=cost(0.05),
        name="input_side",
    )(sel, *toks, *stats, dproj, dxh, out, gate_small, w_mine, gain, *waits)


def combine_kernel(sel, mine_ref, got_ref, *refs):
    keep_grad, keep_out, send_grad, send_out, small_ref = refs[-5:]
    block, width = keep_grad.shape
    cols = width // 4
    low = pl.ds(pl.multiple_of(sel[1] * cols, cols), cols)
    high = pl.ds(pl.multiple_of((1 - sel[1]) * cols, cols), cols)
    for grad, out, first in ((keep_grad, keep_out, 0), (send_grad, send_out, block)):
        here = slice(first, first + block)
        grad[...] = mine_ref[here, 0:width] + got_ref[here, 0:width]
        out[:, low] = mine_ref[here, width:]
        out[:, high] = got_ref[here, width:]
    small_ref[...] = mine_ref[2 * block :, 0:width] + got_ref[2 * block :, 0:width]


def combine(sel, mine, got, *waits):
    block, width = (mine.shape[0] - 8) // 2, mine.shape[1] * 4 // 5
    return pl.pallas_call(
        combine_kernel,
        out_shape=(shaped((block, width)), shaped((block, width // 2))) * 2 + (shaped((8, width)),),
        in_specs=[smem(), vmem(), vmem()] + [any_spec()] * len(waits),
        out_specs=(vmem(),) * 5,
        compiler_params=params(16),
        cost_estimate=cost(0.05),
        name="combine",
    )(sel, mine, got, *waits)


def join_grad_kernel(mine_ref, got_ref, grad_ref, done_ref):
    done_ref[...] = jnp.zeros(done_ref.shape, F32)
    grad_ref[...] = (mine_ref[...] + got_ref[...]).astype(BF16)


def join_grad(mine, got):
    return pl.pallas_call(
        join_grad_kernel,
        out_shape=(shaped(mine.shape, BF16), shaped((8, LANES))),
        in_specs=[vmem()] * 2,
        out_specs=(vmem(),) * 2,
        compiler_params=params(8),
        cost_estimate=cost(0.05),
        name="join_grad",
    )(mine, got)


def join_out_kernel(sel, mine_ref, got_ref, out_ref):
    half = mine_ref.shape[1]
    at = pl.multiple_of(sel[0] * half, half)
    other = pl.multiple_of((1 - sel[0]) * half, half)
    out_ref[:, pl.ds(at, half)] = mine_ref[...].astype(BF16)
    out_ref[:, pl.ds(other, half)] = got_ref[...].astype(BF16)


def join_out(sel, mine, got):
    block, half = mine.shape
    return pl.pallas_call(
        join_out_kernel,
        out_shape=shaped((block, 2 * half), BF16),
        in_specs=[smem()] + [vmem()] * 2,
        out_specs=vmem(),
        compiler_params=params(8),
        cost_estimate=cost(0.05),
        name="join_out",
    )(sel, mine, got)


def fold_small(small):
    rows, cols = 6, small.shape[1] // 4
    tails = [small[i : i + 1, 3 * cols :] for i in range(rows)]
    last = [jnp.concatenate(tails[:3], axis=1), jnp.concatenate(tails[3:], axis=1)]
    return jnp.concatenate([small[0:rows, : 3 * cols]] + last, axis=0)


def finish_kernel(keep_ref, got_ref, a1_ref, a3_ref, small_ref, both_ref):
    part = keep_ref.shape[0]
    both_ref[0:part, :] = keep_ref[...] + got_ref[...] + a1_ref[...] + a3_ref[...]
    both_ref[part:, :] = fold_small(small_ref[...])


def finish(keep, got, a1, a3, small):
    part, cols3 = keep.shape
    return pl.pallas_call(
        finish_kernel,
        out_shape=shaped((part + 8, cols3)),
        in_specs=[vmem()] * 5,
        out_specs=vmem(),
        compiler_params=params(8),
        cost_estimate=cost(0.05),
        name="finish",
    )(keep, got, a1, a3, small)


def second_kernel(both_ref, px0_ref, py0_ref, corner_ref, z1_ref, z3_ref, z13_ref, zs_ref, cs_ref):
    part = z1_ref.shape[0] - 8
    z13_ref[0:part, :] = z1_ref[0:part, :]
    z13_ref[part:, :] = z3_ref[0:part, :]
    small = (both_ref[part:, :] + px0_ref[part:, :]) + (py0_ref[part:, :] + corner_ref[part:, :])
    for ref, out in ((z3_ref, zs_ref), (corner_ref, cs_ref)):
        out[0:part, :] = ref[0:part, :]
        out[part:, :] = small


def second(*pieces):
    part, cols3 = pieces[-1].shape[0] - 8, pieces[-1].shape[1]
    return pl.pallas_call(
        second_kernel,
        out_shape=(shaped((2 * part, cols3)),) + (shaped((part + 8, cols3)),) * 2,
        in_specs=[vmem()] * 6,
        out_specs=(vmem(),) * 3,
        compiler_params=params(10),
        cost_estimate=cost(0.05),
        name="second",
    )(*pieces)


def stack_kernel(*refs, rows):
    at = 0
    for ref, (first, count) in zip(refs, rows):
        refs[-1][at : at + count, :] = ref[first : first + count, :]
        at += count


def stack(*parts):
    rows = tuple((first, count) for _, first, count in parts)
    return pl.pallas_call(
        functools.partial(stack_kernel, rows=rows),
        out_shape=shaped((sum(count for _, count in rows), parts[0][0].shape[1])),
        in_specs=[vmem()] * len(parts),
        out_specs=vmem(),
        compiler_params=params(6),
        cost_estimate=cost(0.05),
        name="stack",
    )(*(array for array, _, _ in parts))


def add_small(places, outs):
    sums = [array[at : at + 8, :] for array, at in places]
    while len(sums) > 1:
        sums = [a + b for a, b in zip(sums[::2], sums[1::2])]
    total = sums[0]
    cols = total.shape[1] // 3
    for i, out in enumerate(outs):
        out[:, 0 : 3 * cols] = total[i : i + 1, :]
        out[:, 3 * cols :] = total[6 + i // 3 : 7 + i // 3, (i % 3) * cols : (i % 3 + 1) * cols]


def place_kernel(sel, *refs, where, give, count, small):
    tails = 6 if small else 0
    outs, scratch = refs[len(refs) - 2 - bool(give) - 2 * tails :], refs[len(refs) - 1 - tails :]
    target, sem, sums = outs[0], scratch[0], scratch[1:]
    cols = refs[0].shape[1] // 3
    width = target.shape[1] // 3
    part = width // 8
    copies = []

    def copy(src, dst):
        copies.append(pltpu.make_async_copy(src, dst, sem.at[len(copies)]))
        copies[-1].start()

    for at, (array, first, rows, row, row_off, x_off, c_off) in enumerate(where):
        piece = refs[array].at[pl.ds(first, rows)]
        to_row = pl.multiple_of(row_part(sel, row) * part + row_off, 8)
        col = (2 * (sel[0] ^ x_off) + (sel[1] ^ c_off)) * cols
        for k in range(3):
            to = pl.multiple_of(col + k * width, cols)
            copy(piece.at[:, pl.ds(k * cols, cols)], target.at[pl.ds(to_row, rows), pl.ds(to, cols)])
        if at < give:
            copy(piece, outs[1].at[pl.ds(at * part, part)])
    if small:
        add_small([(refs[count + i], at) for i, at in small], sums)
        for i in range(tails):
            copy(sums[i], outs[1 + i])
    for c in copies:
        c.wait()


def place(sel, arrays, where, target, width, give, *waits, small=()):
    count = len(arrays)
    extra = [] if target is None else [target]
    outs = [shaped((width, 3 * width))]
    outs += [shaped((give * width // 8, 3 * width // 4))] if give else []
    outs += [shaped((1, width))] * 6 if small else []
    scratch = [pltpu.SemaphoreType.DMA((3 * len(where) + give + (6 if small else 0),))]
    scratch += [pltpu.VMEM((1, width), F32)] * 6 if small else []
    return pl.pallas_call(
        functools.partial(
            place_kernel,
            where=where,
            give=give,
            count=count,
            small=tuple((i, at) for i, (_, at) in enumerate(small)),
        ),
        out_shape=tuple(outs),
        in_specs=[smem()]
        + [vmem()] * (count + len(small))
        + [hbm()] * len(extra)
        + [any_spec()] * len(waits),
        out_specs=(hbm(),) + ((vmem(),) if give else ()) + ((hbm(),) * 6 if small else ()),
        scratch_shapes=scratch,
        input_output_aliases={1 + count + len(small): 0} if extra else {},
        compiler_params=params(8),
        cost_estimate=cost(0.05),
        name="place",
    )(sel, *arrays, *(array for array, _ in small), *extra, *waits)


def given(array, where):
    return [
        (array, i * rows, rows, row, row_off, x_off, 1)
        for i, (_, _, rows, row, row_off, x_off, _) in enumerate(where)
    ]


def on_device(
    tokens,
    offsets,
    w_proj,
    forget_weight,
    reset_weight,
    forget_bias,
    reset_bias,
    layer_norm_gain,
    layer_norm_bias,
    cotangent,
):
    _, block, width = tokens.shape
    z, y, x, c = (lax.axis_index(a) for a in ("z", "y", "x", "c"))
    tuned = lax.axis_size("z") == 4
    sel = jnp.stack([x, c, y, z]).astype(jnp.int32)
    part = width // 8

    cot = cotangent[0]
    own = tokens[0].astype(F32)
    own, *parts = lax.optimization_barrier(
        (own, *(own[first : first + rows] for first, rows in chunks(block)))
    )
    x_a, x_b, x_c = (swap(piece, "x") for piece in parts)
    tok_c = swap(own, "c")
    cot_sibling = swap(widen_cot(sel, cot), "c")
    cot_far = swap(pack_cot(sel, cot, cot_sibling), "x")

    gates = [
        v.reshape(1, width) for v in (forget_weight, reset_weight, forget_bias, reset_bias)
    ]
    gain = layer_norm_gain.reshape(1, width)
    vectors = (*gates, gain, layer_norm_bias.reshape(1, width))
    w_mine = take_weights(sel, w_proj)
    near = run_near(sel, offsets, (own, tok_c), w_mine, vectors)
    (x_a,) = hold((x_a,), near[5])
    xc_a = swap(x_a, "c")
    (x_b,) = hold((x_b,), xc_a)
    xc_b = swap(x_b, "c")
    early = run_early(sel, (x_a, xc_a, x_b, xc_b), w_mine, vectors)
    (x_c,) = hold((x_c,), early[0])
    xc_c = swap(x_c, "c")
    far = run_forward(sel, (x_c, xc_c), near[2:], early, w_mine, vectors)
    normed = (near[0], far[0])
    toks = (own, tok_c, x_a, xc_a, x_b, xc_b, x_c, xc_c)
    if tuned:
        rows = [[[(d, 1)] for d in (2, 3, 1, 0)], [[(d, 0)] for d in (2, 3, 1, 0)]]
    else:
        rows = [[[0], [1], [2], [3]], [[4], [5], [6], [7]]]
    dproj, out, dxh, gate_small, s2, s1 = run_backward(
        sel, toks, (cot, cot_sibling, cot_far), far[2:], near[5], gates, normed, (rows[0][0], rows[0][2])
    )
    s3, k2 = run_products(sel, normed, dproj, (rows[0][1], rows[1][0]))
    grad_mine, grad_send = run_input(
        sel, toks, (near[1], far[1]), dproj, dxh, out, gate_small, w_mine, gain
    )
    late = (rows[0][3], *rows[1][1:])

    if tuned:
        s0, k3, k1, k0 = run_products(sel, normed, dproj, late)
        q2 = add(k2, swap(s2, "y"), s3, s0, grad_send)
        r3 = swap(s3, "y")
        r0 = swap(add(s0, xor_permute(s1, "z", 1), q2), "y")
        a2 = xor_permute(q2, "z", 1)
        h3 = add(add(k3, r3), a2)
        a3 = xor_permute(h3, "z", 3)
        kept, kept_out, sent, sent_out, small = combine(
            sel, grad_mine, swap(grad_send, "c"), q2, tick(grad_send)
        )
        got = swap(sent, "x")
        a1 = xor_permute(k1, "z", 1)
        both = finish(k0, r0, a1, a3, small)
        input_grad, joined = join_grad(kept, got)

        px0, z3, z1, py0 = (
            swap(both, "x"),
            xor_permute(both, "z", 3),
            xor_permute(both, "z", 1),
            swap(both, "y"),
        )
        (px0,) = hold((px0,), joined)
        corner0 = swap(px0, "y")
        (sent_out,) = hold((sent_out,), px0)
        got_out = swap(sent_out, "x")
        py0, corner0, got_out, z1, z3 = hold((py0, corner0, got_out, z1, z3))
        output = join_out(sel, kept_out, got_out)
        full = part + 8
        z13, zs, cs = second(both, px0, py0, corner0, z1, z3)
        z2, px13, py13 = xor_permute(zs, "z", 1), swap(z13, "x"), swap(z13, "y")
        corner3 = xor_permute(cs, "z", 3)
        own = [
            (0, 0, part, (0, 0), 0, 0, 0),
            (1, 0, part, (0, 0), 0, 1, 0),
            (2, 0, part, (0, 1), 0, 0, 0),
            (3, 0, part, (0, 1), 0, 1, 0),
            (4, 0, part, (1, 0), 0, 0, 0),
            (4, part, part, (3, 0), 0, 0, 0),
        ]
        proj_grad, give = place(sel, (both, px0, py0, corner0, z13), own, None, width, 6)
        px13, py13, z2, corner3 = hold((px13, py13, z2, corner3), give)
        by_x, by_y = 3 * part // 8, 3 * part // 8
        rest = part - by_x - by_y
        px2 = swap(stack((z2, 0, part), (py13, 0, by_x)), "x")
        py2 = swap(stack((z2, 0, part), (px13, by_x, by_y)), "y")
        corner12 = xor_permute(
            stack((corner3, 0, part), (corner0, by_x + by_y, rest), (corner3, part, 8)), "z", 1
        )
        other = given(2, own)
        own = [
            (array, part * i, part, (d, y_off), 0, x_off, 0)
            for array, y_off, x_off in ((0, 0, 1), (1, 1, 0))
            for i, d in ((0, 1), (1, 3))
        ]
        proj_grad, give = place(
            sel,
            (px13, py13, swap(give, "c")),
            own + other,
            proj_grad,
            width,
            4,
            tick(give, corner3),
        )
        other = given(3, own)
        first_give, marked = swap(give, "c"), give
        own = [(0, 0, part, (2, 0), 0, 0, 0), (1, 0, part, (3, 1), 0, 1, 0)]
        proj_grad, give = place(sel, (z2, corner3), own, proj_grad, width, 2)
        last = given(3, own)
        px2, py2, corner12 = hold((px2, py2, corner12), give)
        own = [
            (0, 0, part, (2, 0), 0, 1, 0),
            (0, part, by_x, (1, 1), 0, 1, 0),
            (1, 0, part, (2, 1), 0, 0, 0),
            (1, part, by_y, (1, 1), by_x, 1, 0),
            (2, 0, part, (2, 1), 0, 1, 0),
            (2, part, rest, (1, 1), by_x + by_y, 1, 0),
        ]
        small = ((zs, part), (z2, part), (corner12, part + rest), (corner3, part))
        arrays = (px2, py2, corner12, first_give)
        proj_grad, *small = place(
            sel, arrays, own + other, proj_grad, width, 0, tick(marked, give, px2), small=small
        )
        own = [(*place_of[:-1], 1) for place_of in own]
        arrays = [swap(a, "c") for a in (px2, py2, corner12, give)]
        (proj_grad,) = place(sel, arrays, own + last, proj_grad, width, 0)
    else:
        s0, k3, k1, k0 = run_products(sel, normed, dproj, late)
        kept, kept_out, sent, sent_out, small = combine(sel, grad_mine, swap(grad_send, "c"))
        input_grad, _ = join_grad(kept, swap(sent, "x"))
        output = join_out(sel, kept_out, swap(sent_out, "x"))
        small = lax.psum(small + swap(small, "x"), ("z", "y"))
        pieces = jnp.stack([s2, s3, s1, s0, k2, k3, k1, k0])
        pieces = lax.psum(pieces, ("z", "y"))
        proj_grad = None
        for x_off, held in ((0, pieces), (1, swap(pieces, "x"))):
            own = [(r, 0, part, r, 0, x_off, 0) for r in range(8)]
            proj_grad, give = place(sel, list(held), own, proj_grad, width, 8)
            other = given(0, own)
            (proj_grad,) = place(sel, [swap(give, "c")], other, proj_grad, width, 0)
    small = [small[i].reshape(width) for i in range(6)]
    return (output[None], input_grad[None], proj_grad, *small)


def solution(mesh):
    dp, rep = mesh.shape["dp"], mesh.shape["rep"]
    fine = Mesh(mesh.devices.reshape(dp // 2, 2, rep // 2, 2), ("z", "y", "x", "c"))
    row, seq = ("z", "y"), ("x", "c")
    in_specs = (P(row, seq, None), P(row, None)) + (P(),) * 7 + (P(row, seq, None),)
    out_specs = (P(row, seq, None), P(row, seq, None)) + (P(),) * 7
    return jax.shard_map(
        on_device, mesh=fine, in_specs=in_specs, out_specs=out_specs, check_vma=False
    )
```

```python
import functools

import jax
import jax.numpy as jnp
from jax import lax
from jax.experimental import pallas as pl
from jax.experimental.pallas import tpu as pltpu
from jax.sharding import Mesh
from jax.sharding import PartitionSpec as P

EPS = 1e-05
LANES = 128
SWAP = [(0, 1), (1, 0)]
VMEM_BYTES = 56 * 2**20
F32 = jnp.float32
BF16 = jnp.bfloat16


def swap(block, axis):
    return lax.ppermute(block, axis, SWAP)


def xor_permute(block, axis, distance):
    size = lax.axis_size(axis)
    return lax.ppermute(block, axis, [(i, i ^ distance) for i in range(size)])


def any_spec():
    return pl.BlockSpec(memory_space=pl.ANY)


def hbm():
    return pl.BlockSpec(memory_space=pltpu.HBM)


def vmem():
    return pl.BlockSpec(memory_space=pltpu.VMEM)


def smem():
    return pl.BlockSpec(memory_space=pltpu.SMEM)


def shaped(shape, dtype=F32):
    return jax.ShapeDtypeStruct(shape, dtype)


def params(mib):
    return pltpu.CompilerParams(vmem_limit_bytes=mib * 2**20)


def cost(us):
    return pl.CostEstimate(
        flops=int(us * 1.1e9), bytes_accessed=int(us * 3.6e6), transcendentals=0
    )


def own_columns(sel, cols):
    return pl.ds(pl.multiple_of((2 * sel[0] + sel[1]) * cols, cols), cols)


def stored_at(sel, k):
    return 2 * ((k // 2) ^ sel[0]) + ((k % 2) ^ sel[1])


def chunks(block):
    unit = block // 88 * 16
    sizes = (unit, 2 * unit, block - 3 * unit)
    return tuple((sum(sizes[:i]), size) for i, size in enumerate(sizes))


def segments(block):
    far = [(b, first, rows) for first, rows in chunks(block) for b in (2, 3)]
    return ((0, 0, block), (1, 0, block), *far)


def stretches(sel, block, k):
    held = stored_at(sel, k)
    near = held < 2
    return tuple(
        (jnp.where(near, held * block + first, 2 * (block + first) + (held - 2) * rows), rows)
        for first, rows in chunks(block)
    )


def row_part(sel, row):
    return row if isinstance(row, int) else 2 * (sel[3] ^ row[0]) + (sel[2] ^ row[1])


def tick_kernel(*refs):
    refs[-1][...] = jnp.zeros(refs[-1].shape, F32)


def tick(*values):
    return pl.pallas_call(
        tick_kernel,
        out_shape=shaped((8, 128)),
        in_specs=[any_spec()] * len(values),
        out_specs=vmem(),
        compiler_params=params(1),
        cost_estimate=cost(20),
        name="tick",
    )(*values)


def hold_kernel(*refs):
    del refs


def hold(values, *waits):
    count = len(values)
    return pl.pallas_call(
        hold_kernel,
        out_shape=tuple(shaped(v.shape, v.dtype) for v in values),
        in_specs=[any_spec()] * (count + len(waits)),
        out_specs=(any_spec(),) * count,
        input_output_aliases={i: i for i in range(count)},
        compiler_params=params(1),
        cost_estimate=cost(0.05),
        name="hold",
    )(*values, *waits)


def add_kernel(a_ref, b_ref, *refs):
    refs[-1][...] = a_ref[...] + b_ref[...]


def add(a, b, *waits):
    return pl.pallas_call(
        add_kernel,
        out_shape=shaped(a.shape),
        in_specs=[vmem()] * 2 + [any_spec()] * len(waits),
        out_specs=vmem(),
        compiler_params=params(4),
        cost_estimate=cost(0.05),
        name="add",
    )(a, b, *waits)


def take_weights_kernel(sel, w_ref, mine_ref, sem):
    width, cols = mine_ref.shape[0], mine_ref.shape[1] // 3
    copies = []
    for k in range(3):
        at = pl.multiple_of((2 * sel[0] + sel[1]) * cols + k * width, cols)
        copies.append(
            pltpu.make_async_copy(
                w_ref.at[:, pl.ds(at, cols)], mine_ref.at[:, k * cols : (k + 1) * cols], sem.at[k]
            )
        )
    for c in copies:
        c.start()
    for c in copies:
        c.wait()


def take_weights(sel, w_proj):
    width = w_proj.shape[0]
    return pl.pallas_call(
        take_weights_kernel,
        out_shape=shaped((width, 3 * width // 4), BF16),
        in_specs=[smem(), hbm()],
        out_specs=vmem(),
        scratch_shapes=[pltpu.SemaphoreType.DMA((3,))],
        compiler_params=params(4),
        cost_estimate=cost(0.05),
        name="take_weights",
    )(sel, w_proj)


def widen_cot_kernel(sel, cot_ref, cot_out):
    cols = cot_ref.shape[1] // 4
    for k in range(2):
        at = pl.multiple_of((2 * k + 1 - sel[1]) * cols, cols)
        cot_out[:, k * cols : (k + 1) * cols] = cot_ref[:, pl.ds(at, cols)].astype(F32)


def widen_cot(sel, cot):
    return pl.pallas_call(
        widen_cot_kernel,
        out_shape=shaped((cot.shape[0], cot.shape[1] // 2)),
        in_specs=[smem(), vmem()],
        out_specs=vmem(),
        compiler_params=params(4),
        cost_estimate=cost(0.05),
        name="widen_cot",
    )(sel, cot)


def pack_cot_kernel(sel, cot_ref, sibling_ref, cot_out):
    block, cols = cot_ref.shape[0], cot_ref.shape[1] // 4
    mine = pl.multiple_of((2 * (1 - sel[0]) + sel[1]) * cols, cols)
    cot_out[0:block, :] = cot_ref[:, pl.ds(mine, cols)].astype(F32)
    sibling = pl.multiple_of((1 - sel[0]) * cols, cols)
    cot_out[block:, :] = sibling_ref[:, pl.ds(sibling, cols)]


def pack_cot(sel, cot, sibling):
    return pl.pallas_call(
        pack_cot_kernel,
        out_shape=shaped((2 * cot.shape[0], cot.shape[1] // 4)),
        in_specs=[smem(), vmem(), vmem()],
        out_specs=vmem(),
        compiler_params=params(4),
        cost_estimate=cost(0.05),
        name="pack_cot",
    )(sel, cot, sibling)


def standardized(x):
    mean = jnp.mean(x, axis=-1, keepdims=True)
    centred = x - mean
    rdev = lax.rsqrt(jnp.mean(centred * centred, axis=-1, keepdims=True) + EPS)
    return centred * rdev, mean, rdev


def norm_and_project(sel, toks, norm, w_ref, gates, normed, stats, cand, zf, zr, first, base):
    cols = cand.shape[1]
    mine = own_columns(sel, cols)
    gain, bias = norm[0][...], norm[1][...]
    fb, rb = gates[2][:, mine], gates[3][:, mine]
    step = 16
    at = first
    for tok in toks:

        def body(i, carry, tok=tok, at=at):
            here = pl.ds(pl.multiple_of(i * step, step), step)
            there = pl.ds(pl.multiple_of(at + i * step, step), step)
            xhat, mean, rdev = standardized(tok[here, :])
            normed[there, :] = (xhat * gain + bias).astype(BF16)
            stats[there, 0:LANES] = jnp.broadcast_to(mean, (step, LANES))
            stats[there, LANES:] = jnp.broadcast_to(rdev, (step, LANES))
            return carry

        lax.fori_loop(0, tok.shape[0] // step, body, 0, unroll=True)
        at += tok.shape[0]
    rows = normed[first:at, :]
    here = slice(base, base + at - first)
    part = lambda k: jnp.dot(
        rows, w_ref[:, k * cols : (k + 1) * cols], preferred_element_type=F32
    )
    cand[here, :] = part(0)
    zf[here, :] = 0.5 * (part(1) + fb)
    zr[here, :] = 0.5 * (part(2) + rb)


def near_kernel(sel, offsets, tok0, tok1, w_ref, *refs):
    gates, norm, (normed, stats, cand, zf, zr, half_keep) = refs[:4], refs[4:6], refs[6:]
    length, cols = half_keep.shape
    block = length // 4
    step = 16
    row = 0
    for b, first, rows in segments(block):
        base = stored_at(sel, b) * block + first

        def body(i, carry, row=row, base=base):
            at = pl.multiple_of(i * step, step)
            token = base + at + lax.broadcasted_iota(jnp.int32, (step, cols), 0)
            starts = token == offsets[0, 0]
            for k in range(1, offsets.shape[1]):
                starts = starts | (token == offsets[0, k])
            half_keep[pl.ds(pl.multiple_of(row + at, step), step), :] = jnp.where(starts, 0.0, 0.5)
            return carry

        lax.fori_loop(0, rows // step, body, 0)
        row += rows
    norm_and_project(sel, (tok0, tok1), norm, w_ref, gates, normed, stats, cand, zf, zr, 0, 0)


def run_near(sel, offsets, toks, w_mine, vectors):
    block, width = toks[0].shape
    cols = width // 4
    return pl.pallas_call(
        near_kernel,
        out_shape=(shaped((2 * block, width), BF16), shaped((2 * block, 2 * LANES)))
        + (shaped((2 * block, cols)),) * 3
        + (shaped((4 * block, cols)),),
        in_specs=[smem()] * 2 + [vmem()] * 9,
        out_specs=(vmem(),) * 6,
        compiler_params=params(16),
        cost_estimate=cost(0.05),
        name="near_blocks",
    )(sel, offsets, *toks, w_mine, *vectors)


def early_kernel(sel, *refs, count):
    toks, w_ref, refs = refs[:count], refs[count], refs[count + 1 :]
    gates, norm, (normed, stats, cand, zf, zr) = refs[:4], refs[4:6], refs[-5:]
    norm_and_project(sel, toks, norm, w_ref, gates, normed, stats, cand, zf, zr, 0, 0)


def run_early(sel, toks, w_mine, vectors):
    rows, width = sum(tok.shape[0] for tok in toks), toks[0].shape[1]
    cols = width // 4
    return pl.pallas_call(
        functools.partial(early_kernel, count=len(toks)),
        out_shape=(shaped((rows, width), BF16), shaped((rows, 2 * LANES)))
        + (shaped((rows, cols)),) * 3,
        in_specs=[smem()] + [vmem()] * (7 + len(toks)),
        out_specs=(vmem(),) * 5,
        compiler_params=params(12),
        cost_estimate=cost(0.05),
        name="early_blocks",
    )(sel, *toks, w_mine, *vectors)


def forward_kernel(
    sel,
    tok0,
    tok1,
    cand_near,
    zf_near,
    zr_near,
    half_keep,
    normed_early,
    stats_early,
    cand_early,
    zf_early,
    zr_early,
    w_ref,
    *refs,
):
    gates, norm, (normed, stats, cand, zf, zr, state, half_prev) = refs[:4], refs[4:6], refs[6:]
    length, cols = cand.shape
    block = length // 4
    early = normed_early.shape[0]
    normed[0:early, :] = normed_early[...]
    stats[0:early, :] = stats_early[...]
    first = 2 * block
    near, mid = slice(0, first), slice(first, first + early)
    cand[near, :], zf[near, :], zr[near, :] = cand_near[...], zf_near[...], zr_near[...]
    cand[mid, :], zf[mid, :], zr[mid, :] = cand_early[...], zf_early[...], zr_early[...]
    fw = gates[0][:, own_columns(sel, cols)]
    norm_and_project(
        sel, (tok0, tok1), norm, w_ref, gates, normed, stats, cand, zf, zr, early, first + early
    )
    zero = jnp.zeros((1, cols), F32)
    carry = (zero, zero, zero)
    for k in range(4):
        for base, rows in stretches(sel, block, k):

            def body(i, carry, base=base):
                middle, spread, th = carry
                row = pl.ds(base + i, 1)
                half = half_keep[row, :]
                weight = half * fw
                last = middle + spread * th
                th = jnp.tanh((zf[row, :] + weight * middle) + (weight * spread) * th)
                hp = half * last
                hc = 0.5 * cand[row, :]
                middle, spread = hp + hc, hp - hc
                state[row, :] = middle + spread * th
                half_prev[row, :] = hp
                return (middle, spread, th)

            carry = lax.fori_loop(0, rows, body, carry, unroll=16)


def run_forward(sel, toks, near, early, w_mine, vectors):
    late, width = toks[0].shape
    cols = width // 4
    length = near[-1].shape[0]
    return pl.pallas_call(
        forward_kernel,
        out_shape=(shaped((length // 2, width), BF16), shaped((length // 2, 2 * LANES)))
        + (shaped((length, cols)),) * 5,
        in_specs=[smem()] + [vmem()] * 18,
        out_specs=(vmem(),) * 7,
        compiler_params=params(20),
        cost_estimate=cost(0.05),
        name="forward_scan",
    )(sel, *toks, *near, *early, w_mine, *vectors)


def backward_kernel(sel, *refs, rows, count):
    toks, refs = refs[:count], refs[count:]
    (g0, g1, g23, cand_ref, zf_ref, zr_ref, state, half_prev), refs = refs[:8], refs[8:]
    (half_keep, fw_ref, rw_ref, near_ref, far_ref), refs = refs[:5], refs[5:]
    (dproj_ref, out_ref, dxh_ref, small_ref), refs = refs[:4], refs[4:]
    products, (coef, add, add_e, gz, omf, states) = refs[: len(rows)], refs[len(rows) :]
    length, cols = cand_ref.shape
    block = length // 4
    mine = own_columns(sel, cols)
    half = pl.ds(pl.multiple_of(sel[0] * cols, cols), cols)
    fw, rw = fw_ref[:, mine], rw_ref[:, mine]
    half_fw, half_rw = 0.5 * fw, 0.5 * rw
    step = 16
    zero = jnp.zeros((step, cols), F32)
    sums = (zero, zero)
    everything = slice(0, cols)
    grads = ((g0, 0, mine), (g1, 0, half), (g23, 0, everything), (g23, block, everything))
    row = 0
    for x_ref, (b, first, count) in zip(toks, segments(block)):
        g_ref, g_at, g_cols = grads[b]

        def gate_body(
            i, carry, row=row, x_ref=x_ref, g_ref=g_ref, g_at=g_at + first, g_cols=g_cols
        ):
            at = pl.multiple_of(i * step, step)
            here = pl.ds(pl.multiple_of(row + at, step), step)
            x = x_ref[pl.ds(at, step), mine]
            g = g_ref[pl.ds(pl.multiple_of(g_at + at, step), step), g_cols].astype(F32)
            keep = 2.0 * half_keep[here, :]
            prev = 2.0 * half_prev[here, :]
            c, cd = state[here, :], cand_ref[here, :]
            forget = 0.5 + 0.5 * jnp.tanh(zf_ref[here, :] + half_fw * prev)
            reset = 0.5 + 0.5 * jnp.tanh(zr_ref[here, :] + half_rw * prev)
            not_forget, not_reset = 1.0 - forget, 1.0 - reset
            out_ref[here, :] = reset * c + not_reset * x
            dxh_ref[here, :] = g * not_reset
            dzr = g * (c - x) * reset * not_reset
            slope = (prev - cd) * forget * not_forget
            back, extra = keep * (forget + slope * fw), g * reset
            coef[here, :] = back
            add[here, :] = back * extra + keep * (dzr * rw)
            add_e[here, :] = extra
            gz[here, :] = slope
            omf[here, :] = not_forget
            dproj_ref[here, 2 * cols : 3 * cols] = dzr.astype(BF16)
            return (carry[0] + dzr * prev, carry[1] + dzr)

        sums = lax.fori_loop(0, count // step, gate_body, sums, unroll=True)
        row += count
    rw_sum, rb_sum = sums

    dc = jnp.zeros((1, cols), F32)
    group = 8
    for k in range(3, -1, -1):
        for first, count in reversed(stretches(sel, block, k)):

            def backward_body(i, dc, end=first + count):
                base = pl.multiple_of(end - (i + 1) * group, group)
                for r in range(group - 1, -1, -1):
                    row = pl.ds(base + r, 1)
                    states[row, :] = dc
                    dc = coef[row, :] * dc + add[row, :]
                return dc

            dc = lax.fori_loop(0, count // group, backward_body, dc, unroll=2)

    def grad_body(i, carry):
        here = pl.ds(pl.multiple_of(i * step, step), step)
        total = states[here, :] + add_e[here, :]
        prev = 2.0 * half_prev[here, :]
        dzf = total * gz[here, :]
        dproj_ref[here, 0:cols] = (total * omf[here, :]).astype(BF16)
        dproj_ref[here, cols : 2 * cols] = dzf.astype(BF16)
        return (carry[0] + dzf * prev, carry[1] + dzf)

    fw_sum, fb_sum = lax.fori_loop(0, length // step, grad_body, (zero, zero), unroll=4)
    small_ref[...] = jnp.concatenate(
        [jnp.sum(v, axis=0, keepdims=True) for v in (fw_sum, rw_sum, fb_sum, rb_sum)]
        + [jnp.zeros((4, cols), F32)],
        axis=0,
    )
    outer_products(sel, rows, near_ref, far_ref, dproj_ref, products)


def outer_products(sel, rows, near_ref, far_ref, dproj_ref, outs):
    half, width = near_ref.shape
    part = width // 8
    dims = (((0,), (0,)), ((), ()))
    for out, places in zip(outs, rows):
        for k, place_of in enumerate(places):
            at = pl.ds(pl.multiple_of(row_part(sel, place_of) * part, part), part)
            out[k * part : (k + 1) * part, :] = lax.dot_general(
                near_ref[:, at], dproj_ref[0:half, :], dims, preferred_element_type=F32
            ) + lax.dot_general(
                far_ref[:, at], dproj_ref[half:, :], dims, preferred_element_type=F32
            )


def product_shapes(width, rows):
    return tuple(shaped((len(places) * width // 8, 3 * width // 4)) for places in rows)


def run_backward(sel, toks, cots, scanned, half_keep, gates, normed, rows):
    length, cols = half_keep.shape
    width = 4 * cols
    return pl.pallas_call(
        functools.partial(backward_kernel, rows=rows, count=len(toks)),
        out_shape=(
            shaped((length, 3 * cols), BF16),
            shaped((length, cols)),
            shaped((length, cols)),
            shaped((8, cols)),
        )
        + product_shapes(width, rows),
        in_specs=[smem()] + [vmem()] * (13 + len(toks)),
        out_specs=(vmem(),) * (4 + len(rows)),
        scratch_shapes=[pltpu.VMEM((length, cols), F32)] * 6,
        compiler_params=params(24),
        cost_estimate=cost(0.05),
        name="backward_scan",
    )(sel, *toks, *cots, *scanned, half_keep, *gates[:2], *normed)


def products_kernel(sel, near_ref, far_ref, dproj_ref, *outs, rows):
    outer_products(sel, rows, near_ref, far_ref, dproj_ref, outs[-len(rows) :])


def run_products(sel, normed, dproj, rows, *waits):
    return pl.pallas_call(
        functools.partial(products_kernel, rows=rows),
        out_shape=product_shapes(normed[0].shape[1], rows),
        in_specs=[smem()] + [vmem()] * 3 + [any_spec()] * len(waits),
        out_specs=(vmem(),) * len(rows),
        compiler_params=params(12),
        cost_estimate=cost(0.05),
        name="products",
    )(sel, *normed, dproj, *waits)


def input_kernel(sel, *refs, count):
    toks, (mine_ref, send_ref, dnormed) = refs[:count], refs[-3:]
    (stats_near, stats_far, dproj_ref, dxh_ref, out_ref), refs = refs[count : count + 5], refs[count + 5 :]
    gate_small_ref, w_ref, gain_ref = refs[:3]
    cols = dxh_ref.shape[1]
    block, width = toks[0].shape
    gain = gain_ref[...]
    mine = own_columns(sel, cols)
    step = 16
    sums = (jnp.zeros((step, width), F32), jnp.zeros((step, width), F32))
    row = 0
    for tok, (b, first, count) in zip(toks, segments(block)):
        if row % (2 * block) == 0:
            dnormed[...] = lax.dot_general(
                dproj_ref[row : row + 2 * block, :],
                w_ref[...],
                (((1,), (1,)), ((), ())),
                preferred_element_type=F32,
            )
        rows = slice(row, row + count)
        where = send_ref if b % 2 else mine_ref
        base = (b // 2) * block + first
        stats, at = (stats_near, row) if b < 2 else (stats_far, row - 2 * block)

        def body(i, carry, tok=tok, base=base, where=where, stats=stats, at=at):
            here = pl.ds(pl.multiple_of(i * step, step), step)
            there = pl.ds(pl.multiple_of(base + i * step, step), step)
            kept = pl.ds(pl.multiple_of(at + i * step, step), step)
            mean, rdev = (
                jnp.concatenate([stats[kept, k : k + LANES]] * (width // LANES), axis=1)
                for k in (0, LANES)
            )
            xhat = (tok[here, :] - mean) * rdev
            dn = dnormed[kept, :]
            dxhat = dn * gain
            mean1 = jnp.mean(dxhat, axis=-1, keepdims=True)
            mean2 = jnp.mean(dxhat * xhat, axis=-1, keepdims=True)
            where[there, 0:width] = rdev * (dxhat - mean1 - xhat * mean2)
            return (carry[0] + dn * xhat, carry[1] + dn)

        sums = lax.fori_loop(0, count // step, body, sums, unroll=True if count < block else 11)
        to = pl.ds(base, count)
        where[to, mine] += dxh_ref[rows, :]
        where[to, width : width + cols] = out_ref[rows, :]
        row += count
    tail = slice(2 * block, 2 * block + 8)
    mine_ref[tail, :] = jnp.zeros((8, width + cols), F32)
    mine_ref[2 * block : 2 * block + 4, mine] = gate_small_ref[0:4, :]
    for i, v in enumerate(sums):
        row = 2 * block + 4 + i
        mine_ref[row : row + 1, 0:width] = jnp.sum(v, axis=0, keepdims=True)
    send_ref[tail, :] = mine_ref[tail, :]


def run_input(sel, toks, stats, dproj, dxh, out, gate_small, w_mine, gain, *waits):
    block, width = toks[0].shape
    shape = (2 * block + 8, width + width // 4)
    return pl.pallas_call(
        functools.partial(input_kernel, count=len(toks)),
        out_shape=(shaped(shape), shaped(shape)),
        in_specs=[smem()] + [vmem()] * (8 + len(toks)) + [any_spec()] * len(waits),
        out_specs=(vmem(),) * 2,
        scratch_shapes=[pltpu.VMEM((2 * block, width), F32)],
        compiler_params=params(20),
        cost_estimate=cost(0.05),
        name="input_side",
    )(sel, *toks, *stats, dproj, dxh, out, gate_small, w_mine, gain, *waits)


def combine_kernel(sel, mine_ref, got_ref, *refs):
    keep_grad, keep_out, send_grad, send_out, small_ref = refs[-5:]
    block, width = keep_grad.shape
    cols = width // 4
    low = pl.ds(pl.multiple_of(sel[1] * cols, cols), cols)
    high = pl.ds(pl.multiple_of((1 - sel[1]) * cols, cols), cols)
    for grad, out, first in ((keep_grad, keep_out, 0), (send_grad, send_out, block)):
        here = slice(first, first + block)
        grad[...] = mine_ref[here, 0:width] + got_ref[here, 0:width]
        out[:, low] = mine_ref[here, width:]
        out[:, high] = got_ref[here, width:]
    small_ref[...] = mine_ref[2 * block :, 0:width] + got_ref[2 * block :, 0:width]


def combine(sel, mine, got, *waits):
    block, width = (mine.shape[0] - 8) // 2, mine.shape[1] * 4 // 5
    return pl.pallas_call(
        combine_kernel,
        out_shape=(shaped((block, width)), shaped((block, width // 2))) * 2 + (shaped((8, width)),),
        in_specs=[smem(), vmem(), vmem()] + [any_spec()] * len(waits),
        out_specs=(vmem(),) * 5,
        compiler_params=params(16),
        cost_estimate=cost(0.05),
        name="combine",
    )(sel, mine, got, *waits)


def join_grad_kernel(mine_ref, got_ref, grad_ref, done_ref):
    done_ref[...] = jnp.zeros(done_ref.shape, F32)
    grad_ref[...] = (mine_ref[...] + got_ref[...]).astype(BF16)


def join_grad(mine, got):
    return pl.pallas_call(
        join_grad_kernel,
        out_shape=(shaped(mine.shape, BF16), shaped((8, LANES))),
        in_specs=[vmem()] * 2,
        out_specs=(vmem(),) * 2,
        compiler_params=params(8),
        cost_estimate=cost(0.05),
        name="join_grad",
    )(mine, got)


def join_out_kernel(sel, mine_ref, got_ref, out_ref):
    half = mine_ref.shape[1]
    at = pl.multiple_of(sel[0] * half, half)
    other = pl.multiple_of((1 - sel[0]) * half, half)
    out_ref[:, pl.ds(at, half)] = mine_ref[...].astype(BF16)
    out_ref[:, pl.ds(other, half)] = got_ref[...].astype(BF16)


def join_out(sel, mine, got):
    block, half = mine.shape
    return pl.pallas_call(
        join_out_kernel,
        out_shape=shaped((block, 2 * half), BF16),
        in_specs=[smem()] + [vmem()] * 2,
        out_specs=vmem(),
        compiler_params=params(8),
        cost_estimate=cost(0.05),
        name="join_out",
    )(sel, mine, got)


def fold_small(small):
    rows, cols = 6, small.shape[1] // 4
    tails = [small[i : i + 1, 3 * cols :] for i in range(rows)]
    last = [jnp.concatenate(tails[:3], axis=1), jnp.concatenate(tails[3:], axis=1)]
    return jnp.concatenate([small[0:rows, : 3 * cols]] + last, axis=0)


def finish_kernel(keep_ref, got_ref, a1_ref, a3_ref, small_ref, both_ref):
    part = keep_ref.shape[0]
    both_ref[0:part, :] = keep_ref[...] + got_ref[...] + a1_ref[...] + a3_ref[...]
    both_ref[part:, :] = fold_small(small_ref[...])


def finish(keep, got, a1, a3, small):
    part, cols3 = keep.shape
    return pl.pallas_call(
        finish_kernel,
        out_shape=shaped((part + 8, cols3)),
        in_specs=[vmem()] * 5,
        out_specs=vmem(),
        compiler_params=params(8),
        cost_estimate=cost(0.05),
        name="finish",
    )(keep, got, a1, a3, small)


def second_kernel(both_ref, px0_ref, py0_ref, corner_ref, z1_ref, z3_ref, z13_ref, zs_ref, cs_ref):
    part = z1_ref.shape[0] - 8
    z13_ref[0:part, :] = z1_ref[0:part, :]
    z13_ref[part:, :] = z3_ref[0:part, :]
    small = (both_ref[part:, :] + px0_ref[part:, :]) + (py0_ref[part:, :] + corner_ref[part:, :])
    for ref, out in ((z3_ref, zs_ref), (corner_ref, cs_ref)):
        out[0:part, :] = ref[0:part, :]
        out[part:, :] = small


def second(*pieces):
    part, cols3 = pieces[-1].shape[0] - 8, pieces[-1].shape[1]
    return pl.pallas_call(
        second_kernel,
        out_shape=(shaped((2 * part, cols3)),) + (shaped((part + 8, cols3)),) * 2,
        in_specs=[vmem()] * 6,
        out_specs=(vmem(),) * 3,
        compiler_params=params(10),
        cost_estimate=cost(0.05),
        name="second",
    )(*pieces)


def stack_kernel(*refs, rows):
    at = 0
    for ref, (first, count) in zip(refs, rows):
        refs[-1][at : at + count, :] = ref[first : first + count, :]
        at += count


def stack(*parts):
    rows = tuple((first, count) for _, first, count in parts)
    return pl.pallas_call(
        functools.partial(stack_kernel, rows=rows),
        out_shape=shaped((sum(count for _, count in rows), parts[0][0].shape[1])),
        in_specs=[vmem()] * len(parts),
        out_specs=vmem(),
        compiler_params=params(6),
        cost_estimate=cost(0.05),
        name="stack",
    )(*(array for array, _, _ in parts))


def add_small(places, outs):
    sums = [array[at : at + 8, :] for array, at in places]
    while len(sums) > 1:
        sums = [a + b for a, b in zip(sums[::2], sums[1::2])]
    total = sums[0]
    cols = total.shape[1] // 3
    for i, out in enumerate(outs):
        out[:, 0 : 3 * cols] = total[i : i + 1, :]
        out[:, 3 * cols :] = total[6 + i // 3 : 7 + i // 3, (i % 3) * cols : (i % 3 + 1) * cols]


def place_kernel(sel, *refs, where, give, count, small):
    tails = 6 if small else 0
    outs, scratch = refs[len(refs) - 2 - bool(give) - 2 * tails :], refs[len(refs) - 1 - tails :]
    target, sem, sums = outs[0], scratch[0], scratch[1:]
    cols = refs[0].shape[1] // 3
    width = target.shape[1] // 3
    part = width // 8
    copies = []

    def copy(src, dst):
        copies.append(pltpu.make_async_copy(src, dst, sem.at[len(copies)]))
        copies[-1].start()

    for at, (array, first, rows, row, row_off, x_off, c_off) in enumerate(where):
        piece = refs[array].at[pl.ds(first, rows)]
        to_row = pl.multiple_of(row_part(sel, row) * part + row_off, 8)
        col = (2 * (sel[0] ^ x_off) + (sel[1] ^ c_off)) * cols
        for k in range(3):
            to = pl.multiple_of(col + k * width, cols)
            copy(piece.at[:, pl.ds(k * cols, cols)], target.at[pl.ds(to_row, rows), pl.ds(to, cols)])
        if at < give:
            copy(piece, outs[1].at[pl.ds(at * part, part)])
    if small:
        add_small([(refs[count + i], at) for i, at in small], sums)
        for i in range(tails):
            copy(sums[i], outs[1 + i])
    for c in copies:
        c.wait()


def place(sel, arrays, where, target, width, give, *waits, small=()):
    count = len(arrays)
    extra = [] if target is None else [target]
    outs = [shaped((width, 3 * width))]
    outs += [shaped((give * width // 8, 3 * width // 4))] if give else []
    outs += [shaped((1, width))] * 6 if small else []
    scratch = [pltpu.SemaphoreType.DMA((3 * len(where) + give + (6 if small else 0),))]
    scratch += [pltpu.VMEM((1, width), F32)] * 6 if small else []
    return pl.pallas_call(
        functools.partial(
            place_kernel,
            where=where,
            give=give,
            count=count,
            small=tuple((i, at) for i, (_, at) in enumerate(small)),
        ),
        out_shape=tuple(outs),
        in_specs=[smem()]
        + [vmem()] * (count + len(small))
        + [hbm()] * len(extra)
        + [any_spec()] * len(waits),
        out_specs=(hbm(),) + ((vmem(),) if give else ()) + ((hbm(),) * 6 if small else ()),
        scratch_shapes=scratch,
        input_output_aliases={1 + count + len(small): 0} if extra else {},
        compiler_params=params(8),
        cost_estimate=cost(0.05),
        name="place",
    )(sel, *arrays, *(array for array, _ in small), *extra, *waits)


def given(array, where):
    return [
        (array, i * rows, rows, row, row_off, x_off, 1)
        for i, (_, _, rows, row, row_off, x_off, _) in enumerate(where)
    ]


def on_device(
    tokens,
    offsets,
    w_proj,
    forget_weight,
    reset_weight,
    forget_bias,
    reset_bias,
    layer_norm_gain,
    layer_norm_bias,
    cotangent,
):
    _, block, width = tokens.shape
    z, y, x, c = (lax.axis_index(a) for a in ("z", "y", "x", "c"))
    tuned = lax.axis_size("z") == 4
    sel = jnp.stack([x, c, y, z]).astype(jnp.int32)
    part = width // 8

    cot = cotangent[0]
    own = tokens[0].astype(F32)
    own, *parts = lax.optimization_barrier(
        (own, *(own[first : first + rows] for first, rows in chunks(block)))
    )
    x_a, x_b, x_c = (swap(piece, "x") for piece in parts)
    tok_c = swap(own, "c")
    cot_sibling = swap(widen_cot(sel, cot), "c")
    cot_far = swap(pack_cot(sel, cot, cot_sibling), "x")

    gates = [
        v.reshape(1, width) for v in (forget_weight, reset_weight, forget_bias, reset_bias)
    ]
    gain = layer_norm_gain.reshape(1, width)
    vectors = (*gates, gain, layer_norm_bias.reshape(1, width))
    w_mine = take_weights(sel, w_proj)
    near = run_near(sel, offsets, (own, tok_c), w_mine, vectors)
    (x_a,) = hold((x_a,), near[5])
    xc_a = swap(x_a, "c")
    (x_b,) = hold((x_b,), xc_a)
    xc_b = swap(x_b, "c")
    early = run_early(sel, (x_a, xc_a, x_b, xc_b), w_mine, vectors)
    (x_c,) = hold((x_c,), early[0])
    xc_c = swap(x_c, "c")
    far = run_forward(sel, (x_c, xc_c), near[2:], early, w_mine, vectors)
    normed = (near[0], far[0])
    toks = (own, tok_c, x_a, xc_a, x_b, xc_b, x_c, xc_c)
    if tuned:
        rows = [[[(d, 1)] for d in (2, 3, 1, 0)], [[(d, 0)] for d in (2, 3, 1, 0)]]
    else:
        rows = [[[0], [1], [2], [3]], [[4], [5], [6], [7]]]
    dproj, out, dxh, gate_small, s2, s1 = run_backward(
        sel, toks, (cot, cot_sibling, cot_far), far[2:], near[5], gates, normed, (rows[0][0], rows[0][2])
    )
    s3, k2 = run_products(sel, normed, dproj, (rows[0][1], rows[1][0]))
    grad_mine, grad_send = run_input(
        sel, toks, (near[1], far[1]), dproj, dxh, out, gate_small, w_mine, gain
    )
    late = (rows[0][3], *rows[1][1:])

    if tuned:
        s0, k3, k1, k0 = run_products(sel, normed, dproj, late)
        q2 = add(k2, swap(s2, "y"), s3, s0, grad_send)
        r3 = swap(s3, "y")
        r0 = swap(add(s0, xor_permute(s1, "z", 1), q2), "y")
        a2 = xor_permute(q2, "z", 1)
        h3 = add(add(k3, r3), a2)
        a3 = xor_permute(h3, "z", 3)
        kept, kept_out, sent, sent_out, small = combine(
            sel, grad_mine, swap(grad_send, "c"), q2, tick(grad_send)
        )
        got = swap(sent, "x")
        a1 = xor_permute(k1, "z", 1)
        both = finish(k0, r0, a1, a3, small)
        input_grad, joined = join_grad(kept, got)

        px0, z3, z1, py0 = (
            swap(both, "x"),
            xor_permute(both, "z", 3),
            xor_permute(both, "z", 1),
            swap(both, "y"),
        )
        (px0,) = hold((px0,), joined)
        corner0 = swap(px0, "y")
        (sent_out,) = hold((sent_out,), px0)
        got_out = swap(sent_out, "x")
        py0, corner0, got_out, z1, z3 = hold((py0, corner0, got_out, z1, z3))
        output = join_out(sel, kept_out, got_out)
        full = part + 8
        z13, zs, cs = second(both, px0, py0, corner0, z1, z3)
        z2, px13, py13 = xor_permute(zs, "z", 1), swap(z13, "x"), swap(z13, "y")
        corner3 = xor_permute(cs, "z", 3)
        own = [
            (0, 0, part, (0, 0), 0, 0, 0),
            (1, 0, part, (0, 0), 0, 1, 0),
            (2, 0, part, (0, 1), 0, 0, 0),
            (3, 0, part, (0, 1), 0, 1, 0),
            (4, 0, part, (1, 0), 0, 0, 0),
            (4, part, part, (3, 0), 0, 0, 0),
        ]
        proj_grad, give = place(sel, (both, px0, py0, corner0, z13), own, None, width, 6)
        px13, py13, z2, corner3 = hold((px13, py13, z2, corner3), give)
        by_x, by_y = 5 * part // 16, 5 * part // 16
        rest = part - by_x - by_y
        px2 = swap(stack((z2, 0, part), (py13, 0, by_x)), "x")
        py2 = swap(stack((z2, 0, part), (px13, by_x, by_y)), "y")
        corner12 = xor_permute(
            stack((corner3, 0, part), (corner0, by_x + by_y, rest), (corner3, part, 8)), "z", 1
        )
        other = given(2, own)
        own = [
            (array, part * i, part, (d, y_off), 0, x_off, 0)
            for array, y_off, x_off in ((0, 0, 1), (1, 1, 0))
            for i, d in ((0, 1), (1, 3))
        ]
        proj_grad, give = place(
            sel,
            (px13, py13, swap(give, "c")),
            own + other,
            proj_grad,
            width,
            4,
            tick(give, corner3),
        )
        other = given(3, own)
        first_give, marked = swap(give, "c"), give
        own = [(0, 0, part, (2, 0), 0, 0, 0), (1, 0, part, (3, 1), 0, 1, 0)]
        proj_grad, give = place(sel, (z2, corner3), own, proj_grad, width, 2)
        last = given(3, own)
        px2, py2, corner12 = hold((px2, py2, corner12), give)
        own = [
            (0, 0, part, (2, 0), 0, 1, 0),
            (0, part, by_x, (1, 1), 0, 1, 0),
            (1, 0, part, (2, 1), 0, 0, 0),
            (1, part, by_y, (1, 1), by_x, 1, 0),
            (2, 0, part, (2, 1), 0, 1, 0),
            (2, part, rest, (1, 1), by_x + by_y, 1, 0),
        ]
        small = ((zs, part), (z2, part), (corner12, part + rest), (corner3, part))
        arrays = (px2, py2, corner12, first_give)
        proj_grad, *small = place(
            sel, arrays, own + other, proj_grad, width, 0, tick(marked, give, px2), small=small
        )
        own = [(*place_of[:-1], 1) for place_of in own]
        arrays = [swap(a, "c") for a in (px2, py2, corner12, give)]
        (proj_grad,) = place(sel, arrays, own + last, proj_grad, width, 0)
    else:
        s0, k3, k1, k0 = run_products(sel, normed, dproj, late)
        kept, kept_out, sent, sent_out, small = combine(sel, grad_mine, swap(grad_send, "c"))
        input_grad, _ = join_grad(kept, swap(sent, "x"))
        output = join_out(sel, kept_out, swap(sent_out, "x"))
        small = lax.psum(small + swap(small, "x"), ("z", "y"))
        pieces = jnp.stack([s2, s3, s1, s0, k2, k3, k1, k0])
        pieces = lax.psum(pieces, ("z", "y"))
        proj_grad = None
        for x_off, held in ((0, pieces), (1, swap(pieces, "x"))):
            own = [(r, 0, part, r, 0, x_off, 0) for r in range(8)]
            proj_grad, give = place(sel, list(held), own, proj_grad, width, 8)
            other = given(0, own)
            (proj_grad,) = place(sel, [swap(give, "c")], other, proj_grad, width, 0)
    small = [small[i].reshape(width) for i in range(6)]
    return (output[None], input_grad[None], proj_grad, *small)


def solution(mesh):
    dp, rep = mesh.shape["dp"], mesh.shape["rep"]
    fine = Mesh(mesh.devices.reshape(dp // 2, 2, rep // 2, 2), ("z", "y", "x", "c"))
    row, seq = ("z", "y"), ("x", "c")
    in_specs = (P(row, seq, None), P(row, None)) + (P(),) * 7 + (P(row, seq, None),)
    out_specs = (P(row, seq, None), P(row, seq, None)) + (P(),) * 7
    return jax.shard_map(
        on_device, mesh=fine, in_specs=in_specs, out_specs=out_specs, check_vma=False
    )
```

```python
import functools

import jax
import jax.numpy as jnp
from jax import lax
from jax.experimental import pallas as pl
from jax.experimental.pallas import tpu as pltpu
from jax.sharding import Mesh
from jax.sharding import PartitionSpec as P

EPS = 1e-05
LANES = 128
SWAP = [(0, 1), (1, 0)]
VMEM_BYTES = 56 * 2**20
F32 = jnp.float32
BF16 = jnp.bfloat16


def swap(block, axis):
    return lax.ppermute(block, axis, SWAP)


def xor_permute(block, axis, distance):
    size = lax.axis_size(axis)
    return lax.ppermute(block, axis, [(i, i ^ distance) for i in range(size)])


def any_spec():
    return pl.BlockSpec(memory_space=pl.ANY)


def hbm():
    return pl.BlockSpec(memory_space=pltpu.HBM)


def vmem():
    return pl.BlockSpec(memory_space=pltpu.VMEM)


def smem():
    return pl.BlockSpec(memory_space=pltpu.SMEM)


def shaped(shape, dtype=F32):
    return jax.ShapeDtypeStruct(shape, dtype)


def params(mib):
    return pltpu.CompilerParams(vmem_limit_bytes=mib * 2**20)


def cost(us):
    return pl.CostEstimate(
        flops=int(us * 1.1e9), bytes_accessed=int(us * 3.6e6), transcendentals=0
    )


def own_columns(sel, cols):
    return pl.ds(pl.multiple_of((2 * sel[0] + sel[1]) * cols, cols), cols)


def stored_at(sel, k):
    return 2 * ((k // 2) ^ sel[0]) + ((k % 2) ^ sel[1])


def chunks(block):
    unit = block // 88 * 16
    sizes = (unit, 2 * unit, block - 3 * unit)
    return tuple((sum(sizes[:i]), size) for i, size in enumerate(sizes))


def segments(block):
    far = [(b, first, rows) for first, rows in chunks(block) for b in (2, 3)]
    return ((0, 0, block), (1, 0, block), *far)


def stretches(sel, block, k):
    held = stored_at(sel, k)
    near = held < 2
    return tuple(
        (jnp.where(near, held * block + first, 2 * (block + first) + (held - 2) * rows), rows)
        for first, rows in chunks(block)
    )


def row_part(sel, row):
    return row if isinstance(row, int) else 2 * (sel[3] ^ row[0]) + (sel[2] ^ row[1])


def tick_kernel(*refs):
    refs[-1][...] = jnp.zeros(refs[-1].shape, F32)


def tick(*values):
    return pl.pallas_call(
        tick_kernel,
        out_shape=shaped((8, 128)),
        in_specs=[any_spec()] * len(values),
        out_specs=vmem(),
        compiler_params=params(1),
        cost_estimate=cost(20),
        name="tick",
    )(*values)


def hold_kernel(*refs):
    del refs


def hold(values, *waits):
    count = len(values)
    return pl.pallas_call(
        hold_kernel,
        out_shape=tuple(shaped(v.shape, v.dtype) for v in values),
        in_specs=[any_spec()] * (count + len(waits)),
        out_specs=(any_spec(),) * count,
        input_output_aliases={i: i for i in range(count)},
        compiler_params=params(1),
        cost_estimate=cost(0.05),
        name="hold",
    )(*values, *waits)


def add_kernel(a_ref, b_ref, *refs):
    refs[-1][...] = a_ref[...] + b_ref[...]


def add(a, b, *waits):
    return pl.pallas_call(
        add_kernel,
        out_shape=shaped(a.shape),
        in_specs=[vmem()] * 2 + [any_spec()] * len(waits),
        out_specs=vmem(),
        compiler_params=params(4),
        cost_estimate=cost(0.05),
        name="add",
    )(a, b, *waits)


def take_weights_kernel(sel, w_ref, mine_ref, sem):
    width, cols = mine_ref.shape[0], mine_ref.shape[1] // 3
    copies = []
    for k in range(3):
        at = pl.multiple_of((2 * sel[0] + sel[1]) * cols + k * width, cols)
        copies.append(
            pltpu.make_async_copy(
                w_ref.at[:, pl.ds(at, cols)], mine_ref.at[:, k * cols : (k + 1) * cols], sem.at[k]
            )
        )
    for c in copies:
        c.start()
    for c in copies:
        c.wait()


def take_weights(sel, w_proj):
    width = w_proj.shape[0]
    return pl.pallas_call(
        take_weights_kernel,
        out_shape=shaped((width, 3 * width // 4), BF16),
        in_specs=[smem(), hbm()],
        out_specs=vmem(),
        scratch_shapes=[pltpu.SemaphoreType.DMA((3,))],
        compiler_params=params(4),
        cost_estimate=cost(0.05),
        name="take_weights",
    )(sel, w_proj)


def widen_cot_kernel(sel, cot_ref, cot_out):
    cols = cot_ref.shape[1] // 4
    for k in range(2):
        at = pl.multiple_of((2 * k + 1 - sel[1]) * cols, cols)
        cot_out[:, k * cols : (k + 1) * cols] = cot_ref[:, pl.ds(at, cols)].astype(F32)


def widen_cot(sel, cot):
    return pl.pallas_call(
        widen_cot_kernel,
        out_shape=shaped((cot.shape[0], cot.shape[1] // 2)),
        in_specs=[smem(), vmem()],
        out_specs=vmem(),
        compiler_params=params(4),
        cost_estimate=cost(0.05),
        name="widen_cot",
    )(sel, cot)


def pack_cot_kernel(sel, cot_ref, sibling_ref, cot_out):
    block, cols = cot_ref.shape[0], cot_ref.shape[1] // 4
    mine = pl.multiple_of((2 * (1 - sel[0]) + sel[1]) * cols, cols)
    cot_out[0:block, :] = cot_ref[:, pl.ds(mine, cols)].astype(F32)
    sibling = pl.multiple_of((1 - sel[0]) * cols, cols)
    cot_out[block:, :] = sibling_ref[:, pl.ds(sibling, cols)]


def pack_cot(sel, cot, sibling):
    return pl.pallas_call(
        pack_cot_kernel,
        out_shape=shaped((2 * cot.shape[0], cot.shape[1] // 4)),
        in_specs=[smem(), vmem(), vmem()],
        out_specs=vmem(),
        compiler_params=params(4),
        cost_estimate=cost(0.05),
        name="pack_cot",
    )(sel, cot, sibling)


def standardized(x):
    mean = jnp.mean(x, axis=-1, keepdims=True)
    centred = x - mean
    rdev = lax.rsqrt(jnp.mean(centred * centred, axis=-1, keepdims=True) + EPS)
    return centred * rdev, mean, rdev


def norm_and_project(sel, toks, norm, w_ref, gates, normed, stats, cand, zf, zr, first, base):
    cols = cand.shape[1]
    mine = own_columns(sel, cols)
    gain, bias = norm[0][...], norm[1][...]
    fb, rb = gates[2][:, mine], gates[3][:, mine]
    step = 16
    at = first
    for tok in toks:

        def body(i, carry, tok=tok, at=at):
            here = pl.ds(pl.multiple_of(i * step, step), step)
            there = pl.ds(pl.multiple_of(at + i * step, step), step)
            xhat, mean, rdev = standardized(tok[here, :])
            normed[there, :] = (xhat * gain + bias).astype(BF16)
            stats[there, 0:LANES] = jnp.broadcast_to(mean, (step, LANES))
            stats[there, LANES:] = jnp.broadcast_to(rdev, (step, LANES))
            return carry

        lax.fori_loop(0, tok.shape[0] // step, body, 0, unroll=True)
        at += tok.shape[0]
    rows = normed[first:at, :]
    here = slice(base, base + at - first)
    part = lambda k: jnp.dot(
        rows, w_ref[:, k * cols : (k + 1) * cols], preferred_element_type=F32
    )
    cand[here, :] = part(0)
    zf[here, :] = 0.5 * (part(1) + fb)
    zr[here, :] = 0.5 * (part(2) + rb)


def near_kernel(sel, offsets, tok0, tok1, w_ref, *refs):
    gates, norm, (normed, stats, cand, zf, zr, half_keep) = refs[:4], refs[4:6], refs[6:]
    length, cols = half_keep.shape
    block = length // 4
    step = 16
    row = 0
    for b, first, rows in segments(block):
        base = stored_at(sel, b) * block + first

        def body(i, carry, row=row, base=base):
            at = pl.multiple_of(i * step, step)
            token = base + at + lax.broadcasted_iota(jnp.int32, (step, cols), 0)
            starts = token == offsets[0, 0]
            for k in range(1, offsets.shape[1]):
                starts = starts | (token == offsets[0, k])
            half_keep[pl.ds(pl.multiple_of(row + at, step), step), :] = jnp.where(starts, 0.0, 0.5)
            return carry

        lax.fori_loop(0, rows // step, body, 0)
        row += rows
    norm_and_project(sel, (tok0, tok1), norm, w_ref, gates, normed, stats, cand, zf, zr, 0, 0)


def run_near(sel, offsets, toks, w_mine, vectors):
    block, width = toks[0].shape
    cols = width // 4
    return pl.pallas_call(
        near_kernel,
        out_shape=(shaped((2 * block, width), BF16), shaped((2 * block, 2 * LANES)))
        + (shaped((2 * block, cols)),) * 3
        + (shaped((4 * block, cols)),),
        in_specs=[smem()] * 2 + [vmem()] * 9,
        out_specs=(vmem(),) * 6,
        compiler_params=params(16),
        cost_estimate=cost(0.05),
        name="near_blocks",
    )(sel, offsets, *toks, w_mine, *vectors)


def early_kernel(sel, *refs, count):
    toks, w_ref, refs = refs[:count], refs[count], refs[count + 1 :]
    gates, norm, (normed, stats, cand, zf, zr) = refs[:4], refs[4:6], refs[-5:]
    norm_and_project(sel, toks, norm, w_ref, gates, normed, stats, cand, zf, zr, 0, 0)


def run_early(sel, toks, w_mine, vectors):
    rows, width = sum(tok.shape[0] for tok in toks), toks[0].shape[1]
    cols = width // 4
    return pl.pallas_call(
        functools.partial(early_kernel, count=len(toks)),
        out_shape=(shaped((rows, width), BF16), shaped((rows, 2 * LANES)))
        + (shaped((rows, cols)),) * 3,
        in_specs=[smem()] + [vmem()] * (7 + len(toks)),
        out_specs=(vmem(),) * 5,
        compiler_params=params(12),
        cost_estimate=cost(0.05),
        name="early_blocks",
    )(sel, *toks, w_mine, *vectors)


def forward_kernel(
    sel,
    tok0,
    tok1,
    cand_near,
    zf_near,
    zr_near,
    half_keep,
    normed_early,
    stats_early,
    cand_early,
    zf_early,
    zr_early,
    w_ref,
    *refs,
):
    gates, norm, (normed, stats, cand, zf, zr, state, half_prev) = refs[:4], refs[4:6], refs[6:]
    length, cols = cand.shape
    block = length // 4
    early = normed_early.shape[0]
    normed[0:early, :] = normed_early[...]
    stats[0:early, :] = stats_early[...]
    first = 2 * block
    near, mid = slice(0, first), slice(first, first + early)
    cand[near, :], zf[near, :], zr[near, :] = cand_near[...], zf_near[...], zr_near[...]
    cand[mid, :], zf[mid, :], zr[mid, :] = cand_early[...], zf_early[...], zr_early[...]
    fw = gates[0][:, own_columns(sel, cols)]
    norm_and_project(
        sel, (tok0, tok1), norm, w_ref, gates, normed, stats, cand, zf, zr, early, first + early
    )
    zero = jnp.zeros((1, cols), F32)
    carry = (zero, zero, zero)
    for k in range(4):
        for base, rows in stretches(sel, block, k):

            def body(i, carry, base=base):
                middle, spread, th = carry
                row = pl.ds(base + i, 1)
                half = half_keep[row, :]
                weight = half * fw
                last = middle + spread * th
                th = jnp.tanh((zf[row, :] + weight * middle) + (weight * spread) * th)
                hp = half * last
                hc = 0.5 * cand[row, :]
                middle, spread = hp + hc, hp - hc
                state[row, :] = middle + spread * th
                half_prev[row, :] = hp
                return (middle, spread, th)

            carry = lax.fori_loop(0, rows, body, carry, unroll=16)


def run_forward(sel, toks, near, early, w_mine, vectors):
    late, width = toks[0].shape
    cols = width // 4
    length = near[-1].shape[0]
    return pl.pallas_call(
        forward_kernel,
        out_shape=(shaped((length // 2, width), BF16), shaped((length // 2, 2 * LANES)))
        + (shaped((length, cols)),) * 5,
        in_specs=[smem()] + [vmem()] * 18,
        out_specs=(vmem(),) * 7,
        compiler_params=params(20),
        cost_estimate=cost(0.05),
        name="forward_scan",
    )(sel, *toks, *near, *early, w_mine, *vectors)


def backward_kernel(sel, *refs, rows, count):
    toks, refs = refs[:count], refs[count:]
    (g0, g1, g23, cand_ref, zf_ref, zr_ref, state, half_prev), refs = refs[:8], refs[8:]
    (half_keep, fw_ref, rw_ref, near_ref, far_ref), refs = refs[:5], refs[5:]
    (dproj_ref, out_ref, dxh_ref, small_ref), refs = refs[:4], refs[4:]
    products, (coef, add, add_e, gz, omf, states) = refs[: len(rows)], refs[len(rows) :]
    length, cols = cand_ref.shape
    block = length // 4
    mine = own_columns(sel, cols)
    half = pl.ds(pl.multiple_of(sel[0] * cols, cols), cols)
    fw, rw = fw_ref[:, mine], rw_ref[:, mine]
    half_fw, half_rw = 0.5 * fw, 0.5 * rw
    step = 16
    zero = jnp.zeros((step, cols), F32)
    sums = (zero, zero)
    everything = slice(0, cols)
    grads = ((g0, 0, mine), (g1, 0, half), (g23, 0, everything), (g23, block, everything))
    row = 0
    for x_ref, (b, first, count) in zip(toks, segments(block)):
        g_ref, g_at, g_cols = grads[b]

        def gate_body(
            i, carry, row=row, x_ref=x_ref, g_ref=g_ref, g_at=g_at + first, g_cols=g_cols
        ):
            at = pl.multiple_of(i * step, step)
            here = pl.ds(pl.multiple_of(row + at, step), step)
            x = x_ref[pl.ds(at, step), mine]
            g = g_ref[pl.ds(pl.multiple_of(g_at + at, step), step), g_cols].astype(F32)
            keep = 2.0 * half_keep[here, :]
            prev = 2.0 * half_prev[here, :]
            c, cd = state[here, :], cand_ref[here, :]
            forget = 0.5 + 0.5 * jnp.tanh(zf_ref[here, :] + half_fw * prev)
            reset = 0.5 + 0.5 * jnp.tanh(zr_ref[here, :] + half_rw * prev)
            not_forget, not_reset = 1.0 - forget, 1.0 - reset
            out_ref[here, :] = reset * c + not_reset * x
            dxh_ref[here, :] = g * not_reset
            dzr = g * (c - x) * reset * not_reset
            slope = (prev - cd) * forget * not_forget
            back, extra = keep * (forget + slope * fw), g * reset
            coef[here, :] = back
            add[here, :] = back * extra + keep * (dzr * rw)
            add_e[here, :] = extra
            gz[here, :] = slope
            omf[here, :] = not_forget
            dproj_ref[here, 2 * cols : 3 * cols] = dzr.astype(BF16)
            return (carry[0] + dzr * prev, carry[1] + dzr)

        sums = lax.fori_loop(0, count // step, gate_body, sums, unroll=True)
        row += count
    rw_sum, rb_sum = sums

    dc = jnp.zeros((1, cols), F32)
    group = 8
    for k in range(3, -1, -1):
        for first, count in reversed(stretches(sel, block, k)):

            def backward_body(i, dc, end=first + count):
                base = pl.multiple_of(end - (i + 1) * group, group)
                for r in range(group - 1, -1, -1):
                    row = pl.ds(base + r, 1)
                    states[row, :] = dc
                    dc = coef[row, :] * dc + add[row, :]
                return dc

            dc = lax.fori_loop(0, count // group, backward_body, dc, unroll=2)

    def grad_body(i, carry):
        here = pl.ds(pl.multiple_of(i * step, step), step)
        total = states[here, :] + add_e[here, :]
        prev = 2.0 * half_prev[here, :]
        dzf = total * gz[here, :]
        dproj_ref[here, 0:cols] = (total * omf[here, :]).astype(BF16)
        dproj_ref[here, cols : 2 * cols] = dzf.astype(BF16)
        return (carry[0] + dzf * prev, carry[1] + dzf)

    fw_sum, fb_sum = lax.fori_loop(0, length // step, grad_body, (zero, zero), unroll=4)
    small_ref[...] = jnp.concatenate(
        [jnp.sum(v, axis=0, keepdims=True) for v in (fw_sum, rw_sum, fb_sum, rb_sum)]
        + [jnp.zeros((4, cols), F32)],
        axis=0,
    )
    outer_products(sel, rows, near_ref, far_ref, dproj_ref, products)


def outer_products(sel, rows, near_ref, far_ref, dproj_ref, outs):
    half, width = near_ref.shape
    part = width // 8
    dims = (((0,), (0,)), ((), ()))
    for out, places in zip(outs, rows):
        for k, place_of in enumerate(places):
            at = pl.ds(pl.multiple_of(row_part(sel, place_of) * part, part), part)
            out[k * part : (k + 1) * part, :] = lax.dot_general(
                near_ref[:, at], dproj_ref[0:half, :], dims, preferred_element_type=F32
            ) + lax.dot_general(
                far_ref[:, at], dproj_ref[half:, :], dims, preferred_element_type=F32
            )


def product_shapes(width, rows):
    return tuple(shaped((len(places) * width // 8, 3 * width // 4)) for places in rows)


def run_backward(sel, toks, cots, scanned, half_keep, gates, normed, rows):
    length, cols = half_keep.shape
    width = 4 * cols
    return pl.pallas_call(
        functools.partial(backward_kernel, rows=rows, count=len(toks)),
        out_shape=(
            shaped((length, 3 * cols), BF16),
            shaped((length, cols)),
            shaped((length, cols)),
            shaped((8, cols)),
        )
        + product_shapes(width, rows),
        in_specs=[smem()] + [vmem()] * (13 + len(toks)),
        out_specs=(vmem(),) * (4 + len(rows)),
        scratch_shapes=[pltpu.VMEM((length, cols), F32)] * 6,
        compiler_params=params(24),
        cost_estimate=cost(0.05),
        name="backward_scan",
    )(sel, *toks, *cots, *scanned, half_keep, *gates[:2], *normed)


def products_kernel(sel, near_ref, far_ref, dproj_ref, *outs, rows):
    outer_products(sel, rows, near_ref, far_ref, dproj_ref, outs[-len(rows) :])


def run_products(sel, normed, dproj, rows, *waits):
    return pl.pallas_call(
        functools.partial(products_kernel, rows=rows),
        out_shape=product_shapes(normed[0].shape[1], rows),
        in_specs=[smem()] + [vmem()] * 3 + [any_spec()] * len(waits),
        out_specs=(vmem(),) * len(rows),
        compiler_params=params(12),
        cost_estimate=cost(0.05),
        name="products",
    )(sel, *normed, dproj, *waits)


def input_kernel(sel, *refs, count):
    toks, (mine_ref, send_ref, dnormed) = refs[:count], refs[-3:]
    (stats_near, stats_far, dproj_ref, dxh_ref, out_ref), refs = refs[count : count + 5], refs[count + 5 :]
    gate_small_ref, w_ref, gain_ref = refs[:3]
    cols = dxh_ref.shape[1]
    block, width = toks[0].shape
    gain = gain_ref[...]
    mine = own_columns(sel, cols)
    step = 16
    sums = (jnp.zeros((step, width), F32), jnp.zeros((step, width), F32))
    row = 0
    for tok, (b, first, count) in zip(toks, segments(block)):
        if row % (2 * block) == 0:
            dnormed[...] = lax.dot_general(
                dproj_ref[row : row + 2 * block, :],
                w_ref[...],
                (((1,), (1,)), ((), ())),
                preferred_element_type=F32,
            )
        rows = slice(row, row + count)
        where = send_ref if b % 2 else mine_ref
        base = (b // 2) * block + first
        stats, at = (stats_near, row) if b < 2 else (stats_far, row - 2 * block)

        def body(i, carry, tok=tok, base=base, where=where, stats=stats, at=at):
            here = pl.ds(pl.multiple_of(i * step, step), step)
            there = pl.ds(pl.multiple_of(base + i * step, step), step)
            kept = pl.ds(pl.multiple_of(at + i * step, step), step)
            mean, rdev = (
                jnp.concatenate([stats[kept, k : k + LANES]] * (width // LANES), axis=1)
                for k in (0, LANES)
            )
            xhat = (tok[here, :] - mean) * rdev
            dn = dnormed[kept, :]
            dxhat = dn * gain
            mean1 = jnp.mean(dxhat, axis=-1, keepdims=True)
            mean2 = jnp.mean(dxhat * xhat, axis=-1, keepdims=True)
            where[there, 0:width] = rdev * (dxhat - mean1 - xhat * mean2)
            return (carry[0] + dn * xhat, carry[1] + dn)

        sums = lax.fori_loop(0, count // step, body, sums, unroll=True if count < block else 11)
        to = pl.ds(base, count)
        where[to, mine] += dxh_ref[rows, :]
        where[to, width : width + cols] = out_ref[rows, :]
        row += count
    tail = slice(2 * block, 2 * block + 8)
    mine_ref[tail, :] = jnp.zeros((8, width + cols), F32)
    mine_ref[2 * block : 2 * block + 4, mine] = gate_small_ref[0:4, :]
    for i, v in enumerate(sums):
        row = 2 * block + 4 + i
        mine_ref[row : row + 1, 0:width] = jnp.sum(v, axis=0, keepdims=True)
    send_ref[tail, :] = mine_ref[tail, :]


def run_input(sel, toks, stats, dproj, dxh, out, gate_small, w_mine, gain, *waits):
    block, width = toks[0].shape
    shape = (2 * block + 8, width + width // 4)
    return pl.pallas_call(
        functools.partial(input_kernel, count=len(toks)),
        out_shape=(shaped(shape), shaped(shape)),
        in_specs=[smem()] + [vmem()] * (8 + len(toks)) + [any_spec()] * len(waits),
        out_specs=(vmem(),) * 2,
        scratch_shapes=[pltpu.VMEM((2 * block, width), F32)],
        compiler_params=params(20),
        cost_estimate=cost(0.05),
        name="input_side",
    )(sel, *toks, *stats, dproj, dxh, out, gate_small, w_mine, gain, *waits)


def combine_kernel(sel, mine_ref, got_ref, *refs):
    keep_grad, keep_out, send_grad, send_out, small_ref = refs[-5:]
    block, width = keep_grad.shape
    cols = width // 4
    low = pl.ds(pl.multiple_of(sel[1] * cols, cols), cols)
    high = pl.ds(pl.multiple_of((1 - sel[1]) * cols, cols), cols)
    for grad, out, first in ((keep_grad, keep_out, 0), (send_grad, send_out, block)):
        here = slice(first, first + block)
        grad[...] = mine_ref[here, 0:width] + got_ref[here, 0:width]
        out[:, low] = mine_ref[here, width:]
        out[:, high] = got_ref[here, width:]
    small_ref[...] = mine_ref[2 * block :, 0:width] + got_ref[2 * block :, 0:width]


def combine(sel, mine, got, *waits):
    block, width = (mine.shape[0] - 8) // 2, mine.shape[1] * 4 // 5
    return pl.pallas_call(
        combine_kernel,
        out_shape=(shaped((block, width)), shaped((block, width // 2))) * 2 + (shaped((8, width)),),
        in_specs=[smem(), vmem(), vmem()] + [any_spec()] * len(waits),
        out_specs=(vmem(),) * 5,
        compiler_params=params(16),
        cost_estimate=cost(0.05),
        name="combine",
    )(sel, mine, got, *waits)


def join_grad_kernel(mine_ref, got_ref, grad_ref, done_ref):
    done_ref[...] = jnp.zeros(done_ref.shape, F32)
    grad_ref[...] = (mine_ref[...] + got_ref[...]).astype(BF16)


def join_grad(mine, got):
    return pl.pallas_call(
        join_grad_kernel,
        out_shape=(shaped(mine.shape, BF16), shaped((8, LANES))),
        in_specs=[vmem()] * 2,
        out_specs=(vmem(),) * 2,
        compiler_params=params(8),
        cost_estimate=cost(0.05),
        name="join_grad",
    )(mine, got)


def join_out_kernel(sel, mine_ref, got_ref, out_ref):
    half = mine_ref.shape[1]
    at = pl.multiple_of(sel[0] * half, half)
    other = pl.multiple_of((1 - sel[0]) * half, half)
    out_ref[:, pl.ds(at, half)] = mine_ref[...].astype(BF16)
    out_ref[:, pl.ds(other, half)] = got_ref[...].astype(BF16)


def join_out(sel, mine, got):
    block, half = mine.shape
    return pl.pallas_call(
        join_out_kernel,
        out_shape=shaped((block, 2 * half), BF16),
        in_specs=[smem()] + [vmem()] * 2,
        out_specs=vmem(),
        compiler_params=params(8),
        cost_estimate=cost(0.05),
        name="join_out",
    )(sel, mine, got)


def fold_small(small):
    rows, cols = 6, small.shape[1] // 4
    tails = [small[i : i + 1, 3 * cols :] for i in range(rows)]
    last = [jnp.concatenate(tails[:3], axis=1), jnp.concatenate(tails[3:], axis=1)]
    return jnp.concatenate([small[0:rows, : 3 * cols]] + last, axis=0)


def finish_kernel(keep_ref, got_ref, a1_ref, a3_ref, small_ref, both_ref):
    part = keep_ref.shape[0]
    both_ref[0:part, :] = keep_ref[...] + got_ref[...] + a1_ref[...] + a3_ref[...]
    both_ref[part:, :] = fold_small(small_ref[...])


def finish(keep, got, a1, a3, small):
    part, cols3 = keep.shape
    return pl.pallas_call(
        finish_kernel,
        out_shape=shaped((part + 8, cols3)),
        in_specs=[vmem()] * 5,
        out_specs=vmem(),
        compiler_params=params(8),
        cost_estimate=cost(0.05),
        name="finish",
    )(keep, got, a1, a3, small)


def second_kernel(both_ref, px0_ref, py0_ref, corner_ref, z1_ref, z3_ref, z13_ref, zs_ref, cs_ref):
    part = z1_ref.shape[0] - 8
    z13_ref[0:part, :] = z1_ref[0:part, :]
    z13_ref[part:, :] = z3_ref[0:part, :]
    small = (both_ref[part:, :] + px0_ref[part:, :]) + (py0_ref[part:, :] + corner_ref[part:, :])
    for ref, out in ((z3_ref, zs_ref), (corner_ref, cs_ref)):
        out[0:part, :] = ref[0:part, :]
        out[part:, :] = small


def second(*pieces):
    part, cols3 = pieces[-1].shape[0] - 8, pieces[-1].shape[1]
    return pl.pallas_call(
        second_kernel,
        out_shape=(shaped((2 * part, cols3)),) + (shaped((part + 8, cols3)),) * 2,
        in_specs=[vmem()] * 6,
        out_specs=(vmem(),) * 3,
        compiler_params=params(10),
        cost_estimate=cost(0.05),
        name="second",
    )(*pieces)


def stack_kernel(*refs, rows):
    at = 0
    for ref, (first, count) in zip(refs, rows):
        refs[-1][at : at + count, :] = ref[first : first + count, :]
        at += count


def stack(*parts):
    rows = tuple((first, count) for _, first, count in parts)
    return pl.pallas_call(
        functools.partial(stack_kernel, rows=rows),
        out_shape=shaped((sum(count for _, count in rows), parts[0][0].shape[1])),
        in_specs=[vmem()] * len(parts),
        out_specs=vmem(),
        compiler_params=params(6),
        cost_estimate=cost(0.05),
        name="stack",
    )(*(array for array, _, _ in parts))


def add_small(places, outs):
    sums = [array[at : at + 8, :] for array, at in places]
    while len(sums) > 1:
        sums = [a + b for a, b in zip(sums[::2], sums[1::2])]
    total = sums[0]
    cols = total.shape[1] // 3
    for i, out in enumerate(outs):
        out[:, 0 : 3 * cols] = total[i : i + 1, :]
        out[:, 3 * cols :] = total[6 + i // 3 : 7 + i // 3, (i % 3) * cols : (i % 3 + 1) * cols]


def place_kernel(sel, *refs, where, give, count, small):
    tails = 6 if small else 0
    outs, scratch = refs[len(refs) - 2 - bool(give) - 2 * tails :], refs[len(refs) - 1 - tails :]
    target, sem, sums = outs[0], scratch[0], scratch[1:]
    cols = refs[0].shape[1] // 3
    width = target.shape[1] // 3
    part = width // 8
    copies = []

    def copy(src, dst):
        copies.append(pltpu.make_async_copy(src, dst, sem.at[len(copies)]))
        copies[-1].start()

    for at, (array, first, rows, row, row_off, x_off, c_off) in enumerate(where):
        piece = refs[array].at[pl.ds(first, rows)]
        to_row = pl.multiple_of(row_part(sel, row) * part + row_off, 8)
        col = (2 * (sel[0] ^ x_off) + (sel[1] ^ c_off)) * cols
        for k in range(3):
            to = pl.multiple_of(col + k * width, cols)
            copy(piece.at[:, pl.ds(k * cols, cols)], target.at[pl.ds(to_row, rows), pl.ds(to, cols)])
        if at < give:
            copy(piece, outs[1].at[pl.ds(at * part, part)])
    if small:
        add_small([(refs[count + i], at) for i, at in small], sums)
        for i in range(tails):
            copy(sums[i], outs[1 + i])
    for c in copies:
        c.wait()


def place(sel, arrays, where, target, width, give, *waits, small=()):
    count = len(arrays)
    extra = [] if target is None else [target]
    outs = [shaped((width, 3 * width))]
    outs += [shaped((give * width // 8, 3 * width // 4))] if give else []
    outs += [shaped((1, width))] * 6 if small else []
    scratch = [pltpu.SemaphoreType.DMA((3 * len(where) + give + (6 if small else 0),))]
    scratch += [pltpu.VMEM((1, width), F32)] * 6 if small else []
    return pl.pallas_call(
        functools.partial(
            place_kernel,
            where=where,
            give=give,
            count=count,
            small=tuple((i, at) for i, (_, at) in enumerate(small)),
        ),
        out_shape=tuple(outs),
        in_specs=[smem()]
        + [vmem()] * (count + len(small))
        + [hbm()] * len(extra)
        + [any_spec()] * len(waits),
        out_specs=(hbm(),) + ((vmem(),) if give else ()) + ((hbm(),) * 6 if small else ()),
        scratch_shapes=scratch,
        input_output_aliases={1 + count + len(small): 0} if extra else {},
        compiler_params=params(8),
        cost_estimate=cost(0.05),
        name="place",
    )(sel, *arrays, *(array for array, _ in small), *extra, *waits)


def given(array, where):
    return [
        (array, i * rows, rows, row, row_off, x_off, 1)
        for i, (_, _, rows, row, row_off, x_off, _) in enumerate(where)
    ]


def on_device(
    tokens,
    offsets,
    w_proj,
    forget_weight,
    reset_weight,
    forget_bias,
    reset_bias,
    layer_norm_gain,
    layer_norm_bias,
    cotangent,
):
    _, block, width = tokens.shape
    z, y, x, c = (lax.axis_index(a) for a in ("z", "y", "x", "c"))
    tuned = lax.axis_size("z") == 4
    sel = jnp.stack([x, c, y, z]).astype(jnp.int32)
    part = width // 8

    cot = cotangent[0]
    own = tokens[0].astype(F32)
    own, *parts = lax.optimization_barrier(
        (own, *(own[first : first + rows] for first, rows in chunks(block)))
    )
    x_a, x_b, x_c = (swap(piece, "x") for piece in parts)
    tok_c = swap(own, "c")
    cot_sibling = swap(widen_cot(sel, cot), "c")
    cot_far = swap(pack_cot(sel, cot, cot_sibling), "x")

    gates = [
        v.reshape(1, width) for v in (forget_weight, reset_weight, forget_bias, reset_bias)
    ]
    gain = layer_norm_gain.reshape(1, width)
    vectors = (*gates, gain, layer_norm_bias.reshape(1, width))
    w_mine = take_weights(sel, w_proj)
    near = run_near(sel, offsets, (own, tok_c), w_mine, vectors)
    (x_a,) = hold((x_a,), near[5])
    xc_a = swap(x_a, "c")
    (x_b,) = hold((x_b,), xc_a)
    xc_b = swap(x_b, "c")
    early = run_early(sel, (x_a, xc_a, x_b, xc_b), w_mine, vectors)
    (x_c,) = hold((x_c,), early[0])
    xc_c = swap(x_c, "c")
    far = run_forward(sel, (x_c, xc_c), near[2:], early, w_mine, vectors)
    normed = (near[0], far[0])
    toks = (own, tok_c, x_a, xc_a, x_b, xc_b, x_c, xc_c)
    if tuned:
        rows = [[[(d, 1)] for d in (2, 3, 1, 0)], [[(d, 0)] for d in (2, 3, 1, 0)]]
    else:
        rows = [[[0], [1], [2], [3]], [[4], [5], [6], [7]]]
    dproj, out, dxh, gate_small, s2, s1 = run_backward(
        sel, toks, (cot, cot_sibling, cot_far), far[2:], near[5], gates, normed, (rows[0][0], rows[0][2])
    )
    s3, k2 = run_products(sel, normed, dproj, (rows[0][1], rows[1][0]))
    grad_mine, grad_send = run_input(
        sel, toks, (near[1], far[1]), dproj, dxh, out, gate_small, w_mine, gain
    )
    late = (rows[0][3], *rows[1][1:])

    if tuned:
        s0, k3, k1, k0 = run_products(sel, normed, dproj, late)
        q2 = add(k2, swap(s2, "y"), s3, s0, grad_send)
        r3 = swap(s3, "y")
        r0 = swap(add(s0, xor_permute(s1, "z", 1), q2), "y")
        a2 = xor_permute(q2, "z", 1)
        h3 = add(add(k3, r3), a2)
        a3 = xor_permute(h3, "z", 3)
        kept, kept_out, sent, sent_out, small = combine(
            sel, grad_mine, swap(grad_send, "c"), q2, tick(grad_send)
        )
        got = swap(sent, "x")
        a1 = xor_permute(k1, "z", 1)
        both = finish(k0, r0, a1, a3, small)
        input_grad, joined = join_grad(kept, got)

        px0, z3, z1, py0 = (
            swap(both, "x"),
            xor_permute(both, "z", 3),
            xor_permute(both, "z", 1),
            swap(both, "y"),
        )
        (px0,) = hold((px0,), joined)
        corner0 = swap(px0, "y")
        (sent_out,) = hold((sent_out,), joined)
        got_out = swap(sent_out, "x")
        py0, corner0, got_out, z1, z3 = hold((py0, corner0, got_out, z1, z3))
        output = join_out(sel, kept_out, got_out)
        full = part + 8
        z13, zs, cs = second(both, px0, py0, corner0, z1, z3)
        z2, px13, py13 = xor_permute(zs, "z", 1), swap(z13, "x"), swap(z13, "y")
        corner3 = xor_permute(cs, "z", 3)
        own = [
            (0, 0, part, (0, 0), 0, 0, 0),
            (1, 0, part, (0, 0), 0, 1, 0),
            (2, 0, part, (0, 1), 0, 0, 0),
            (3, 0, part, (0, 1), 0, 1, 0),
            (4, 0, part, (1, 0), 0, 0, 0),
            (4, part, part, (3, 0), 0, 0, 0),
        ]
        proj_grad, give = place(sel, (both, px0, py0, corner0, z13), own, None, width, 6)
        px13, py13, z2, corner3 = hold((px13, py13, z2, corner3), give)
        by_x, by_y = 5 * part // 16, 5 * part // 16
        rest = part - by_x - by_y
        px2 = swap(stack((z2, 0, part), (py13, 0, by_x)), "x")
        py2 = swap(stack((z2, 0, part), (px13, by_x, by_y)), "y")
        corner12 = xor_permute(
            stack((corner3, 0, part), (corner0, by_x + by_y, rest), (corner3, part, 8)), "z", 1
        )
        other = given(2, own)
        own = [
            (array, part * i, part, (d, y_off), 0, x_off, 0)
            for array, y_off, x_off in ((0, 0, 1), (1, 1, 0))
            for i, d in ((0, 1), (1, 3))
        ]
        proj_grad, give = place(
            sel,
            (px13, py13, swap(give, "c")),
            own + other,
            proj_grad,
            width,
            4,
            tick(give, corner3),
        )
        other = given(3, own)
        first_give, marked = swap(give, "c"), give
        own = [(0, 0, part, (2, 0), 0, 0, 0), (1, 0, part, (3, 1), 0, 1, 0)]
        proj_grad, give = place(sel, (z2, corner3), own, proj_grad, width, 2)
        last = given(3, own)
        px2, py2, corner12 = hold((px2, py2, corner12), give)
        own = [
            (0, 0, part, (2, 0), 0, 1, 0),
            (0, part, by_x, (1, 1), 0, 1, 0),
            (1, 0, part, (2, 1), 0, 0, 0),
            (1, part, by_y, (1, 1), by_x, 1, 0),
            (2, 0, part, (2, 1), 0, 1, 0),
            (2, part, rest, (1, 1), by_x + by_y, 1, 0),
        ]
        small = ((zs, part), (z2, part), (corner12, part + rest), (corner3, part))
        arrays = (px2, py2, corner12, first_give)
        proj_grad, *small = place(
            sel, arrays, own + other, proj_grad, width, 0, tick(marked, give, px2), small=small
        )
        own = [(*place_of[:-1], 1) for place_of in own]
        arrays = [swap(a, "c") for a in (px2, py2, corner12, give)]
        (proj_grad,) = place(sel, arrays, own + last, proj_grad, width, 0)
    else:
        s0, k3, k1, k0 = run_products(sel, normed, dproj, late)
        kept, kept_out, sent, sent_out, small = combine(sel, grad_mine, swap(grad_send, "c"))
        input_grad, _ = join_grad(kept, swap(sent, "x"))
        output = join_out(sel, kept_out, swap(sent_out, "x"))
        small = lax.psum(small + swap(small, "x"), ("z", "y"))
        pieces = jnp.stack([s2, s3, s1, s0, k2, k3, k1, k0])
        pieces = lax.psum(pieces, ("z", "y"))
        proj_grad = None
        for x_off, held in ((0, pieces), (1, swap(pieces, "x"))):
            own = [(r, 0, part, r, 0, x_off, 0) for r in range(8)]
            proj_grad, give = place(sel, list(held), own, proj_grad, width, 8)
            other = given(0, own)
            (proj_grad,) = place(sel, [swap(give, "c")], other, proj_grad, width, 0)
    small = [small[i].reshape(width) for i in range(6)]
    return (output[None], input_grad[None], proj_grad, *small)


def solution(mesh):
    dp, rep = mesh.shape["dp"], mesh.shape["rep"]
    fine = Mesh(mesh.devices.reshape(dp // 2, 2, rep // 2, 2), ("z", "y", "x", "c"))
    row, seq = ("z", "y"), ("x", "c")
    in_specs = (P(row, seq, None), P(row, None)) + (P(),) * 7 + (P(row, seq, None),)
    out_specs = (P(row, seq, None), P(row, seq, None)) + (P(),) * 7
    return jax.shard_map(
        on_device, mesh=fine, in_specs=in_specs, out_specs=out_specs, check_vma=False
    )
```
